32 devices in a mesh: parts: 2 (over y), dp: 4 (over z), tp: 4 (over x, core).
Axes of the slice: x: 2, y: 2, z: 4, core: 2. Of those that a mesh axis runs over, the one named last changes fastest.
Arguments:
- memory_hidden: bfloat16 [512, 5120], P(('parts', 'dp'), 'tp'), parts along dimension 0, may hold values from -6 to 6
- kv_weight: bfloat16 [2, 5120, 1024], P(None, None, 'tp'), may hold values from -0.078125 to 0.078125
- kv_bias: bfloat16 [2, 1024], P(None, 'tp'), may hold values from -3 to 3
- memory_sections: int32 [512], P('parts'), parts along dimension 0, may hold values from 0 to 3, never falling along the last dimension, each value on 1 to 128 neighbouring positions
- group_sections: int32 [8], P(('parts', 'dp')), parts along dimension 0, may hold values from 0 to 3
- queries: bfloat16 [64, 5120], P(('parts', 'dp'), 'tp'), parts along dimension 0, may hold values from -130 to 130
- new_keys: bfloat16 [64, 1024], P(('parts', 'dp'), 'tp'), parts along dimension 0, may hold values from -5 to 5
- new_values: bfloat16 [64, 1024], P(('parts', 'dp'), 'tp'), parts along dimension 0, may hold values from -5 to 5
- cache_keys: bfloat16 [32, 512, 1024], P(('parts', 'dp'), None, 'tp'), parts along dimension 0, may hold values from -5 to 5
- cache_values: bfloat16 [32, 512, 1024], P(('parts', 'dp'), None, 'tp'), parts along dimension 0, may hold values from -5 to 5
- cache_lengths: int32 [32], P(('parts', 'dp')), parts along dimension 0, may hold values from 2 to 512, as said below
- out_weight: bfloat16 [5120, 5120], P('tp', 'dp'), may hold values from -1.25 to 1.25
Outputs:
- output: bfloat16 [64, 5120], P(('parts', 'tp'), 'dp'), parts along dimension 0
The draws below stay inside these ranges and needn't reach their ends.
There are 2 independent parts, one for each index of `parts`. The reference program is written for one: setup_inputs(seed, part) draws one part's arguments, and reference() takes and returns one part's arrays. A program takes and returns all parts, laid end to end along the dimension named above; an argument that names none is the same for every part. Nothing has to cross between parts.
Inputs may be any that keep to these rules, and one draw needn't show every extreme that they name: `memory_sections`: memory rows are grouped by section in order; every section holds at least one row. `cache_lengths`: some request has all 512 slots live.
All inputs are finite; a program needn't handle non-finite values.
Results may differ from the reference program's by a relative error of at most 0.0054.
Values may be sent and summed in bfloat16 or wider, within the bound.
No kernel may reach another device: no remote copies, remote signals or barrier semaphores. Data moves between devices by JAX's collectives and lax.ppermute only.
A program may use at most 64 MiB of HBM per device.

```python
import math
import jax
import jax.numpy as jnp
import numpy as np
from jax import lax

D = 5120
HQ = 40
KVH = 8
HD = 128
MROWS = 256
SECTIONS = 4
NEW = 2
REQ_DEV = 4
LMAX = 512
GROUPS = 4
REQUESTS = 16
ROWS = 32


def common_keys(key):
    return jax.random.truncated_normal(jax.random.fold_in(key, 101), -5.0, 5.0, (REQUESTS, LMAX, KVH * HD), jnp.float32)


def draw_cache_keys(key, part):
    keys = common_keys(key)
    return keys.astype(jnp.bfloat16)


def draw_queries(key, part):
    drawn = jax.random.truncated_normal(jax.random.fold_in(key, 103), -6.0, 6.0, (ROWS, HQ * HD), jnp.float32)
    return drawn.astype(jnp.bfloat16)


def draw_cache_lengths(key, part):
    shift = jax.random.randint(jax.random.fold_in(key, 105), (GROUPS,), 0, 4)
    caps = jnp.maximum(LMAX // jnp.power(2, shift), 2)
    per_request = jnp.repeat(caps, REQ_DEV, total_repeat_length=REQUESTS)
    lengths = jax.random.randint(jax.random.fold_in(key, 106), (REQUESTS,), 2, per_request + 1)
    longest = jax.random.randint(jax.random.fold_in(key, 107), (), 0, REQUESTS)
    return jnp.where(jnp.arange(REQUESTS) == longest, LMAX, lengths).astype(jnp.int32)


def plant(drawn, key, least, largest):
    longest = drawn.shape.index(max(drawn.shape))
    spots = []
    for shift in (0, 1):
        where = [jax.random.randint(jax.random.fold_in(key, axis), (), 0, length) for axis, length in enumerate(drawn.shape)]
        where[longest] = (where[longest] + shift) % drawn.shape[longest]
        spots.append(tuple(where))
    return drawn.at[spots[0]].set(least).at[spots[1]].set(largest)


def block_scale(key, extent, cuts, smallest, largest):
    gain = 1.0
    for dim, blocks in cuts:
        steps = jax.random.uniform(jax.random.fold_in(jax.random.fold_in(key, 6), dim), (blocks,), jnp.float32, smallest / len(cuts), largest / len(cuts))
        gain = gain * jnp.repeat(jnp.exp(steps), extent[dim] // blocks).reshape((-1,) + (1,) * (len(extent) - 1 - dim))
    return gain


def split_up(number_of, total, bound, skew):
    loads = [(1 << 20) // math.isqrt(rank ** skew) + 1 for rank in range(2, number_of + 1)]
    rest, counts = total - bound - (number_of - 1), [1] * (number_of - 1)
    while rest > 0:
        movable = [i for i in range(number_of - 1) if counts[i] < bound]
        whole, left = sum([loads[i] for i in movable]), rest
        for i in movable:
            more = min(bound - counts[i], max(1, left * loads[i] // whole), rest)
            counts[i] = counts[i] + more
            rest = rest - more
    return np.array([bound] + counts)


def ragged_sizes(rng, number_of, total, reach, skew):
    if number_of == 2:
        one = jax.random.randint(rng, (), max(1, total - reach), min(reach, total - 1) + 1)
        return jnp.stack([one, total - one])
    tallies = jnp.asarray(split_up(number_of, total, reach, skew), jnp.int32)
    couples = (number_of - 1) // 2
    source_of, taker = tallies[1:1 + 2 * couples:2], tallies[2:2 + 2 * couples:2]
    slack = jnp.minimum(source_of - 1, reach - taker)
    moved = jax.random.randint(jax.random.fold_in(rng, 1), (couples,), 0, 1 << 20) % (slack + 1)
    tallies = tallies.at[1:1 + 2 * couples:2].set(source_of - moved).at[2:2 + 2 * couples:2].set(taker + moved)
    return tallies[jax.random.permutation(jax.random.fold_in(rng, 2), number_of)]


def normal_values(own_key, extent, deviation, reach, pieces=(), kind=jnp.bfloat16):
    entries = deviation * jax.random.normal(own_key, extent, jnp.float32)
    if pieces:
        entries = entries * block_scale(own_key, extent, pieces, -0.22, 0.18)
    return jnp.clip(entries, -reach, reach).astype(kind)


def setup_inputs(seed: int = 0, part: int = 0) -> dict:
    seeds = jax.random.split(jax.random.key(seed), 13)
    part_keys = jax.random.split(jax.random.fold_in(seeds[12], part), 13)
    memory_hidden = normal_values(part_keys[0], (MROWS, D), 1.0, 6.0, ((0, 4), (1, 4)))
    kv_weight = normal_values(seeds[1], (2, D, KVH * HD), D ** -0.5, 0.078125, ((2, 4),))
    kv_bias = normal_values(seeds[2], (2, KVH * HD), 0.5, 3.0, ((1, 4),))
    memory_sections = jnp.searchsorted(jnp.cumsum(ragged_sizes(part_keys[3], SECTIONS, MROWS, MROWS // 2, 0)), jnp.arange(MROWS), side="right").astype(jnp.int32)
    group_sections = plant(jax.random.randint(part_keys[4], (GROUPS,), 0, SECTIONS), jax.random.fold_in(part_keys[4], 1), 0, SECTIONS - 1).astype(jnp.int32)
    queries = draw_queries(jax.random.fold_in(jax.random.fold_in(seeds[12], part), 71), part)
    new_keys = normal_values(part_keys[6], (ROWS, KVH * HD), 1.0, 5.0, ((0, 4), (1, 4)))
    new_values = normal_values(part_keys[7], (ROWS, KVH * HD), 1.0, 5.0, ((0, 4), (1, 4)))
    cache_keys = draw_cache_keys(jax.random.fold_in(jax.random.fold_in(seeds[12], part), 71), part)
    cache_values = normal_values(part_keys[9], (REQUESTS, LMAX, KVH * HD), 1.0, 5.0, ((0, 4), (2, 4)))
    cache_lengths = draw_cache_lengths(jax.random.fold_in(jax.random.fold_in(seeds[12], part), 71), part)
    out_weight = normal_values(seeds[11], (HQ * HD, D), (HQ * HD // 256) ** -0.5, 1.25, ((0, 4), (1, 4)))
    return dict(memory_hidden=memory_hidden, kv_weight=kv_weight, kv_bias=kv_bias, memory_sections=memory_sections, group_sections=group_sections, queries=queries, new_keys=new_keys, new_values=new_values, cache_keys=cache_keys, cache_values=cache_values, cache_lengths=cache_lengths, out_weight=out_weight)


masked_score = -1e+30

def reference(memory_hidden, kv_weight, kv_bias, memory_sections, group_sections, queries, new_keys, new_values, cache_keys, cache_values, cache_lengths, out_weight):
    wide = memory_hidden.astype(jnp.float32)
    scale = lax.rsqrt(lax.optimization_barrier(jnp.mean(wide * wide, axis=1, keepdims=True)) + 1e-06)
    bias = kv_bias.astype(jnp.float32)
    mem_keys = (jnp.dot(memory_hidden, kv_weight[0], preferred_element_type=jnp.float32) * scale + bias[0]).astype(jnp.bfloat16)
    mem_values = (jnp.dot(memory_hidden, kv_weight[1], preferred_element_type=jnp.float32) * scale + bias[1]).astype(jnp.bfloat16)
    requests = cache_lengths.shape[0]
    per_head = HQ // KVH
    inv = 1.0 / HD ** 0.5
    query = queries.astype(jnp.float32).reshape(requests, NEW, KVH, per_head, HD)
    mk = mem_keys.astype(jnp.float32).reshape(MROWS, KVH, HD)
    mv = mem_values.astype(jnp.float32).reshape(MROWS, KVH, HD)
    ck = cache_keys.astype(jnp.float32).reshape(requests, LMAX, KVH, HD)
    cv = cache_values.astype(jnp.float32).reshape(requests, LMAX, KVH, HD)
    nk = new_keys.astype(jnp.float32).reshape(requests, NEW, KVH, HD)
    nv = new_values.astype(jnp.float32).reshape(requests, NEW, KVH, HD)
    sec_req = jnp.repeat(group_sections, REQ_DEV)
    mem_ok = (memory_sections[None, :] == sec_req[:, None])[:, None, None, None, :]
    cache_ok = (jnp.arange(LMAX)[None, :] < cache_lengths[:, None])[:, None, None, None, :]
    new_ok = (jnp.arange(NEW)[None, :] <= jnp.arange(NEW)[:, None])[None, :, None, None, :]
    s_mem = jnp.where(mem_ok, jnp.einsum('rnkgd,mkd->rnkgm', query, mk) * inv, masked_score)
    s_cache = jnp.where(cache_ok, jnp.einsum('rnkgd,rlkd->rnkgl', query, ck) * inv, masked_score)
    s_new = jnp.where(new_ok, jnp.einsum('rnkgd,rjkd->rnkgj', query, nk) * inv, masked_score)
    top = jnp.maximum(jnp.maximum(lax.optimization_barrier(jnp.max(s_mem, axis=-1)), lax.optimization_barrier(jnp.max(s_cache, axis=-1))), lax.optimization_barrier(jnp.max(s_new, axis=-1)))
    p_mem = jnp.where(mem_ok, jnp.exp(s_mem - top[..., None]), 0.0)
    p_cache = jnp.where(cache_ok, jnp.exp(s_cache - top[..., None]), 0.0)
    p_new = jnp.where(new_ok, jnp.exp(s_new - top[..., None]), 0.0)
    total = lax.optimization_barrier(jnp.sum(p_mem, axis=-1)) + lax.optimization_barrier(jnp.sum(p_cache, axis=-1)) + lax.optimization_barrier(jnp.sum(p_new, axis=-1))
    r_mem = lax.optimization_barrier(p_mem.astype(jnp.bfloat16)).astype(jnp.float32)
    r_cache = lax.optimization_barrier(p_cache.astype(jnp.bfloat16)).astype(jnp.float32)
    r_new = lax.optimization_barrier(p_new.astype(jnp.bfloat16)).astype(jnp.float32)
    acc = jnp.einsum('rnkgm,mkd->rnkgd', r_mem, mv)
    acc = acc + jnp.einsum('rnkgl,rlkd->rnkgd', r_cache, cv)
    acc = acc + jnp.einsum('rnkgj,rjkd->rnkgd', r_new, nv)
    attended = (acc / total[..., None]).astype(jnp.bfloat16).reshape(requests * NEW, HQ * HD)
    return jnp.dot(attended, out_weight, preferred_element_type=jnp.float32).astype(jnp.bfloat16)
```

```python
import functools

import jax
import jax.numpy as jnp
from jax import lax
from jax.experimental import pallas as pl
from jax.experimental.pallas import tpu as pltpu
from jax.sharding import PartitionSpec as P

D = 5120
HQ = 40
KVH = 8
HD = 128
NEW = 2
PER_HEAD = HQ // KVH
INV = 1.0 / HD**0.5

masked_score = -1e30
bf16 = jnp.bfloat16
f32 = jnp.float32

TOP, TOTAL_HIGH, TOTAL_LOW, SECTION = range(4)


def nt(a, b):
    return lax.dot_general(a, b, (((1,), (1,)), ((), ())), preferred_element_type=f32)


def nn(a, b):
    return jnp.dot(a, b, preferred_element_type=f32)


def spread(blocks):
    zeros = jnp.zeros_like(blocks[0])
    rows = [
        jnp.concatenate([b if i == j else zeros for i in range(len(blocks))], axis=1)
        if len(blocks) > 1
        else b
        for j, b in enumerate(blocks)
    ]
    return jnp.concatenate(rows, axis=0)


def cache_kernel(lens_ref, group_ref, q_ref, nk_ref, nv_ref, ck_ref, cv_ref, out_ref):
    requests, slots, cols = ck_ref.shape
    heads = cols // HD
    tokens = requests * NEW
    per = PER_HEAD * tokens
    rows = heads * per
    q = q_ref[...].astype(f32)
    blocks = []
    for j in range(heads):
        parts = [q[:, (j * PER_HEAD + g) * HD : (j * PER_HEAD + g + 1) * HD] for g in range(PER_HEAD)]
        blocks.append(jnp.concatenate(parts, axis=0))
    out_ref[0:rows, :] = jnp.concatenate(blocks, axis=0).astype(bf16)
    qs = spread(blocks).astype(bf16)

    row = lax.broadcasted_iota(jnp.int32, (rows, 1), 0)
    request = lax.rem(lax.div(row, NEW), requests)
    token = lax.rem(row, NEW)
    s = nt(qs, ck_ref[0])
    limit = jnp.full((rows, 1), lens_ref[0], jnp.int32)
    for r in range(1, requests):
        s = jnp.where(request == r, nt(qs, ck_ref[r]), s)
        limit = jnp.where(request == r, lens_ref[r], limit)
    live = lax.broadcasted_iota(jnp.int32, (rows, slots), 1) < limit
    s = jnp.where(live, s * INV, masked_score)
    fresh = lax.broadcasted_iota(jnp.int32, (rows, tokens), 1)
    seen = (lax.div(fresh, NEW) == request) & (lax.rem(fresh, NEW) <= token)
    s_new = jnp.where(seen, nt(qs, nk_ref[...]) * INV, masked_score)

    top = jnp.maximum(jnp.max(s, axis=1, keepdims=True), jnp.max(s_new, axis=1, keepdims=True))
    top = top.astype(bf16).astype(f32)
    p = jnp.where(live, jnp.exp(s - top), 0.0)
    p_new = jnp.where(seen, jnp.exp(s_new - top), 0.0)
    total = jnp.sum(p, axis=1, keepdims=True) + jnp.sum(p_new, axis=1, keepdims=True)
    p = p.astype(bf16)
    acc = nn(p, cv_ref[0])
    for r in range(1, requests):
        acc = jnp.where(request == r, nn(p, cv_ref[r]), acc)
    acc = acc + nn(p_new.astype(bf16).astype(f32), nv_ref[...].astype(f32))
    mine = jnp.concatenate([acc[j * per : (j + 1) * per, j * HD : (j + 1) * HD] for j in range(heads)], axis=0)
    out_ref[rows : 2 * rows, :] = (mine / total).astype(bf16)

    high = total.astype(bf16).astype(f32)
    lane = lax.broadcasted_iota(jnp.int32, (rows, HD), 1)
    stats = jnp.where(lane == TOP, top, 0.0)
    stats = jnp.where(lane == TOTAL_HIGH, high, stats)
    stats = jnp.where(lane == TOTAL_LOW, total - high, stats)
    stats = jnp.where(lane == SECTION, group_ref[0].astype(f32), stats)
    out_ref[2 * rows : 3 * rows, :] = stats.astype(bf16)


def project_kernel(count, *refs):
    pieces, (w_ref, b_ref, out_ref) = refs[:count], refs[count:]
    rows, depth = pieces[0].shape
    me = lax.axis_index("tp")
    acc = [None, None]
    squares = None
    for k, piece in enumerate(pieces):
        h = piece[...]
        wide = h.astype(f32)
        square = jnp.sum(wide * wide, axis=1, keepdims=True)
        squares = square if squares is None else squares + square
        first = pl.multiple_of((me ^ k) * depth, depth)
        for s in range(2):
            term = nn(h, w_ref[s, pl.ds(first, depth), :])
            acc[s] = term if acc[s] is None else acc[s] + term
    scale = lax.rsqrt(squares / D + 1e-06)
    for s in range(2):
        bias = b_ref[s : s + 1, :].astype(f32)
        out_ref[s * rows : (s + 1) * rows, :] = (acc[s] * scale + bias).astype(bf16)


def attend_kernel(groups, shares, *refs):
    parts, kvs = refs[:groups], refs[groups : 2 * groups]
    section_ref, w_ref = refs[2 * groups : 2 * groups + 2]
    outs = refs[2 * groups + 2 : 2 * groups + 2 + shares]
    k_ref, v_ref, attended_ref, sums_ref = refs[2 * groups + 2 + shares :]
    me_dp, me_tp = lax.axis_index("dp"), lax.axis_index("tp")
    rows = parts[0].shape[0] // 3
    memory = kvs[0].shape[0] // 2
    heads = kvs[0].shape[1] // HD
    per = rows // heads
    tokens = per // PER_HEAD
    for k, kv in enumerate(kvs):
        first = pl.multiple_of((me_dp ^ k) * memory, memory)
        k_ref[pl.ds(first, memory), :] = kv[0:memory, :].astype(k_ref.dtype)
        v_ref[pl.ds(first, memory), :] = kv[memory : 2 * memory, :].astype(v_ref.dtype)
    qs = jnp.concatenate(
        [spread([part[j * per : (j + 1) * per, :] for j in range(heads)]) for part in parts], axis=0
    )
    old = jnp.concatenate([part[rows : 2 * rows, :] for part in parts], axis=0).astype(f32)
    stats = jnp.concatenate([part[2 * rows : 3 * rows, :] for part in parts], axis=0).astype(f32)
    old_top = stats[:, TOP : TOP + 1]
    old_total = stats[:, TOTAL_HIGH : TOTAL_HIGH + 1] + stats[:, TOTAL_LOW : TOTAL_LOW + 1]
    ok = stats[:, SECTION : SECTION + 1] == section_ref[...].astype(f32)
    s = jnp.where(ok, nt(qs, k_ref[...].astype(bf16)) * INV, masked_score)
    top = jnp.maximum(jnp.max(s, axis=1, keepdims=True), old_top)
    p = jnp.where(ok, jnp.exp(s - top), 0.0)
    old_weight = jnp.exp(old_top - top) * old_total
    total = jnp.sum(p, axis=1, keepdims=True) + old_weight
    acc = nn(p.astype(bf16), v_ref[...].astype(bf16))
    for k in range(groups):
        at = pl.multiple_of((me_dp ^ k) * tokens, tokens)
        for j in range(heads):
            a = k * rows + j * per
            block = acc[a : a + per, j * HD : (j + 1) * HD] + old[a : a + per] * old_weight[a : a + per]
            block = block / total[a : a + per]
            for g in range(PER_HEAD):
                c = (j * PER_HEAD + g) * HD
                attended_ref[pl.ds(at, tokens), c : c + HD] = block[g * tokens : (g + 1) * tokens, :]
    sums_ref[...] = nn(attended_ref[...].astype(bf16), w_ref[...])
    share = sums_ref.shape[0] // shares
    for k, out in enumerate(outs):
        at = pl.multiple_of((me_tp ^ k) * share, share)
        out[...] = sums_ref[pl.ds(at, share), :].astype(out.dtype)


VMEM = pl.BlockSpec(memory_space=pltpu.VMEM)
SMEM = pl.BlockSpec(memory_space=pltpu.SMEM)
PARAMS = pltpu.CompilerParams(vmem_limit_bytes=40 * 1024 * 1024)


def call(kernel, in_specs, out_shape, scratch, flops, bytes_accessed):
    return pl.pallas_call(
        kernel,
        in_specs=in_specs,
        out_shape=out_shape,
        out_specs=jax.tree.map(lambda _: VMEM, out_shape),
        scratch_shapes=scratch,
        compiler_params=PARAMS,
        cost_estimate=pl.CostEstimate(flops=flops, bytes_accessed=bytes_accessed, transcendentals=0),
    )


def others(x, axis):
    n = lax.axis_size(axis)
    return [x] + [lax.ppermute(x, axis, [(i, i ^ k) for i in range(n)]) for k in range(1, n)]


def body(
    memory_hidden,
    kv_weight,
    kv_bias,
    memory_sections,
    group_sections,
    queries,
    new_keys,
    new_values,
    cache_keys,
    cache_values,
    cache_lengths,
    out_weight,
):
    groups, shares = lax.axis_size("dp"), lax.axis_size("tp")
    memory, depth = memory_hidden.shape
    requests, slots, cols = cache_keys.shape
    tokens = requests * NEW
    rows = (cols // HD) * PER_HEAD * tokens
    every = memory_sections.shape[0]

    hidden = others(memory_hidden, "tp")
    part = call(
        cache_kernel,
        [SMEM, SMEM] + [VMEM] * 5,
        jax.ShapeDtypeStruct((3 * rows, HD), bf16),
        [],
        4 * rows * slots * cols * requests,
        2 * 2 * requests * slots * cols,
    )(cache_lengths, group_sections, queries, new_keys, new_values, cache_keys, cache_values)
    parts = others(part, "dp")
    kv = call(
        functools.partial(project_kernel, shares),
        [VMEM] * (shares + 2),
        jax.ShapeDtypeStruct((2 * memory, cols), bf16),
        [],
        4 * memory * D * cols,
        4 * D * cols,
    )(*hidden, kv_weight, kv_bias)
    kvs = others(kv, "dp")

    out_rows, out_cols = groups * tokens, out_weight.shape[1]
    share = out_rows // shares
    held = bf16 if memory % 16 == 0 else f32
    pieces = call(
        functools.partial(attend_kernel, groups, shares),
        [VMEM] * (2 * groups + 2),
        [jax.ShapeDtypeStruct((share, out_cols), f32 if k == 0 else bf16) for k in range(shares)],
        [
            pltpu.VMEM((every, cols), held),
            pltpu.VMEM((every, cols), held),
            pltpu.VMEM((out_rows, out_weight.shape[0]), f32),
            pltpu.VMEM((out_rows, out_cols), f32),
        ],
        2 * out_rows * out_weight.size,
        2 * out_weight.size,
    )(*parts, *kvs, memory_sections.reshape(1, every), out_weight)
    summed = pieces[0]
    for k in range(1, shares):
        summed = summed + lax.ppermute(pieces[k], "tp", [(i, i ^ k) for i in range(shares)]).astype(f32)
    return summed.astype(bf16)


def solution(mesh):
    return jax.shard_map(
        body,
        mesh=mesh,
        in_specs=(
            P(("parts", "dp"), "tp"),
            P(None, None, "tp"),
            P(None, "tp"),
            P("parts"),
            P(("parts", "dp")),
            P(("parts", "dp"), "tp"),
            P(("parts", "dp"), "tp"),
            P(("parts", "dp"), "tp"),
            P(("parts", "dp"), None, "tp"),
            P(("parts", "dp"), None, "tp"),
            P(("parts", "dp")),
            P("tp", "dp"),
        ),
        out_specs=P(("parts", "tp"), "dp"),
        check_vma=False,
    )
```

```python
import functools

import jax
import jax.numpy as jnp
from jax import lax
from jax.experimental import pallas as pl
from jax.experimental.pallas import tpu as pltpu
from jax.sharding import PartitionSpec as P

D = 5120
HQ = 40
KVH = 8
HD = 128
NEW = 2
PER_HEAD = HQ // KVH
INV = 1.0 / HD**0.5

masked_score = -1e30
bf16 = jnp.bfloat16
f32 = jnp.float32

TOP, TOTAL, SECTION = 0, 3, 5
STATS = 16


def nt(a, b):
    return lax.dot_general(a, b, (((1,), (1,)), ((), ())), preferred_element_type=f32)


def nn(a, b):
    return jnp.dot(a, b, preferred_element_type=f32)


def spread(blocks):
    zeros = jnp.zeros_like(blocks[0])
    rows = [
        jnp.concatenate([b if i == j else zeros for i in range(len(blocks))], axis=1)
        if len(blocks) > 1
        else b
        for j, b in enumerate(blocks)
    ]
    return jnp.concatenate(rows, axis=0)


def split(x, pieces):
    out = []
    for _ in range(pieces):
        piece = x.astype(bf16).astype(f32)
        out.append(piece)
        x = x - piece
    return out


def eye(rows, cols):
    row = lax.broadcasted_iota(jnp.int32, (rows, cols), 0)
    return (row == lax.broadcasted_iota(jnp.int32, (rows, cols), 1)).astype(f32).astype(bf16)


def up(n, to):
    return -(-n // to) * to


def cache_kernel(
    lens_ref, group_ref, q_hbm, nk_hbm, nv_hbm, ck_hbm, cv_hbm, w_hbm, b_hbm, h_hbm,
    out_ref, w_ref, b_ref, h_ref,
    q_ref, nk_ref, nv_ref, ck_ref, cv_ref, sems,
):
    requests, slots, cols = ck_ref.shape
    small = [
        pltpu.make_async_copy(src, dst, sems.at[i])
        for i, (src, dst) in enumerate(
            [(q_hbm, q_ref), (nk_hbm, nk_ref), (nv_hbm, nv_ref)]
        )
    ]
    first = len(small)
    keys = [pltpu.make_async_copy(ck_hbm.at[r], ck_ref.at[r], sems.at[first + r]) for r in range(requests)]
    first += requests
    values = [pltpu.make_async_copy(cv_hbm.at[r], cv_ref.at[r], sems.at[first + r]) for r in range(requests)]
    first += requests
    kept = [
        pltpu.make_async_copy(src, dst, sems.at[first + i])
        for i, (src, dst) in enumerate([(h_hbm, h_ref), (w_hbm, w_ref), (b_hbm, b_ref)])
    ]
    for copy in small + keys + values + kept:
        copy.start()

    heads = cols // HD
    tokens = requests * NEW
    per = PER_HEAD * tokens
    rows = heads * per
    row = lax.broadcasted_iota(jnp.int32, (rows, 1), 0)
    request = lax.rem(lax.div(row, NEW), requests)
    token = lax.rem(row, NEW)
    for copy in small:
        copy.wait()
    q = q_ref[...].astype(f32)
    blocks = []
    for j in range(heads):
        parts = [q[:, (j * PER_HEAD + g) * HD : (j * PER_HEAD + g + 1) * HD] for g in range(PER_HEAD)]
        blocks.append(jnp.concatenate(parts, axis=0))
    out_ref[0:rows, :] = jnp.concatenate(blocks, axis=0).astype(bf16)
    qs = spread(blocks).astype(bf16)
    fresh = lax.broadcasted_iota(jnp.int32, (rows, tokens), 1)
    seen = (lax.div(fresh, NEW) == request) & (lax.rem(fresh, NEW) <= token)
    s_new = jnp.where(seen, nt(qs, nk_ref[...]) * INV, masked_score)
    limit = jnp.full((rows, 1), lens_ref[0], jnp.int32)
    for r in range(1, requests):
        limit = jnp.where(request == r, lens_ref[r], limit)
    live = lax.broadcasted_iota(jnp.int32, (rows, slots), 1) < limit
    keys[0].wait()
    s = nt(qs, ck_ref[0])
    for r in range(1, requests):
        keys[r].wait()
        s = jnp.where(request == r, nt(qs, ck_ref[r]), s)
    s = jnp.where(live, s * INV, masked_score)

    top = jnp.maximum(jnp.max(s, axis=1, keepdims=True), jnp.max(s_new, axis=1, keepdims=True))
    p = jnp.where(live, jnp.exp(s - top), 0.0)
    p_new = jnp.where(seen, jnp.exp(s_new - top), 0.0)
    total = jnp.sum(p, axis=1, keepdims=True) + jnp.sum(p_new, axis=1, keepdims=True)
    p = p.astype(bf16)
    values[0].wait()
    acc = nn(p, cv_ref[0])
    for r in range(1, requests):
        values[r].wait()
        acc = jnp.where(request == r, nn(p, cv_ref[r]), acc)
    acc = acc + nn(p_new.astype(bf16).astype(f32), nv_ref[...].astype(f32))
    mine = jnp.concatenate([acc[j * per : (j + 1) * per, j * HD : (j + 1) * HD] for j in range(heads)], axis=0)
    seg = up(rows, 16)
    out_ref[seg : seg + rows, :] = (mine / total).astype(bf16)

    lane = lax.broadcasted_iota(jnp.int32, (rows, HD), 1)
    stats = jnp.where(lane == SECTION, group_ref[0].astype(f32), 0.0)
    for i, piece in enumerate(split(top, 3)):
        stats = jnp.where(lane == TOP + i, piece, stats)
    for i, piece in enumerate(split(total, 2)):
        stats = jnp.where(lane == TOTAL + i, piece, stats)
    if rows < HD:
        stats = jnp.concatenate([stats, jnp.zeros((HD - rows, HD), f32)], axis=0)
    out_ref[2 * seg : 2 * seg + STATS, :] = nt(eye(STATS, HD), stats.astype(bf16)).astype(bf16)
    for copy in kept:
        copy.wait()


def project_kernel(count, *refs):
    pieces, (w_ref, b_ref), out_ref = refs[:count], refs[count : count + 2], refs[-1]
    rows, depth = pieces[0].shape
    me = lax.axis_index("tp")
    acc = [None, None]
    squares = None
    for k, piece in enumerate(pieces):
        h = piece[...]
        wide = h.astype(f32)
        square = jnp.sum(wide * wide, axis=1, keepdims=True)
        squares = square if squares is None else squares + square
        first = pl.multiple_of((me ^ k) * depth, depth)
        for s in range(2):
            term = nn(h, w_ref[s, pl.ds(first, depth), :])
            acc[s] = term if acc[s] is None else acc[s] + term
    scale = lax.rsqrt(squares / D + 1e-06)
    for s in range(2):
        bias = b_ref[s : s + 1, :].astype(f32)
        out_ref[s * rows : (s + 1) * rows, :] = (acc[s] * scale + bias).astype(bf16)


def attend_kernel(groups, shares, *refs):
    parts, kvs = refs[:groups], refs[groups : 2 * groups]
    section_ref, w_ref = refs[2 * groups : 2 * groups + 2]
    outs = refs[2 * groups + 2 : 2 * groups + 2 + shares]
    k_ref, v_ref, attended_ref, sums_ref = refs[2 * groups + 2 + shares :]
    me_dp, me_tp = lax.axis_index("dp"), lax.axis_index("tp")
    seg = (parts[0].shape[0] - STATS) // 2
    memory = kvs[0].shape[0] // 2
    heads = kvs[0].shape[1] // HD
    tokens = attended_ref.shape[0] // groups
    per = PER_HEAD * tokens
    rows = heads * per
    for k, kv in enumerate(kvs):
        first = pl.multiple_of((me_dp ^ k) * memory, memory)
        k_ref[pl.ds(first, memory), :] = kv[0:memory, :].astype(k_ref.dtype)
        v_ref[pl.ds(first, memory), :] = kv[memory : 2 * memory, :].astype(v_ref.dtype)
    blocks = [part[0:rows, :].astype(f32) for part in parts]
    qs = jnp.concatenate(
        [spread([b[j * per : (j + 1) * per, :] for j in range(heads)]) for b in blocks], axis=0
    ).astype(bf16)
    old = jnp.concatenate([part[seg : seg + rows, :] for part in parts], axis=0).astype(f32)
    stats = nt(
        eye(rows, HD), jnp.concatenate([part[2 * seg : 2 * seg + STATS, :] for part in parts], axis=0)
    )

    def column(at, pieces):
        columns = []
        for k in range(groups):
            c = k * STATS + at
            columns.append(sum([stats[:, c + i : c + i + 1] for i in range(pieces)]))
        return jnp.concatenate(columns, axis=0)

    old_top, old_total = column(TOP, 3), column(TOTAL, 2)
    ok = column(SECTION, 1) == section_ref[...].astype(f32)
    s = jnp.where(ok, nt(qs, k_ref[...].astype(bf16)) * INV, masked_score)
    top = jnp.maximum(jnp.max(s, axis=1, keepdims=True), old_top)
    p = jnp.where(ok, jnp.exp(s - top), 0.0)
    old_weight = jnp.exp(old_top - top) * old_total
    total = jnp.sum(p, axis=1, keepdims=True) + old_weight
    acc = nn(p.astype(bf16), v_ref[...].astype(bf16))
    for k in range(groups):
        at = pl.multiple_of((me_dp ^ k) * tokens, tokens)
        for j in range(heads):
            a = k * rows + j * per
            block = acc[a : a + per, j * HD : (j + 1) * HD] + old[a : a + per] * old_weight[a : a + per]
            block = block / total[a : a + per]
            for g in range(PER_HEAD):
                c = (j * PER_HEAD + g) * HD
                attended_ref[pl.ds(at, tokens), c : c + HD] = block[g * tokens : (g + 1) * tokens, :]
    sums_ref[...] = nn(attended_ref[...].astype(bf16), w_ref[...])
    share = sums_ref.shape[0] // shares
    for k, out in enumerate(outs):
        at = pl.multiple_of((me_tp ^ k) * share, share)
        out[...] = sums_ref[pl.ds(at, share), :].astype(out.dtype)


SMEM = pl.BlockSpec(memory_space=pltpu.SMEM)
VMEM = pl.BlockSpec(memory_space=pltpu.VMEM)
HBM = pl.BlockSpec(memory_space=pltpu.HBM)
ANY = pl.BlockSpec(memory_space=pl.ANY)
PARAMS = pltpu.CompilerParams(vmem_limit_bytes=24 * 1024 * 1024)


def call(kernel, in_specs, out_shape, scratch, flops, bytes_accessed):
    return pl.pallas_call(
        kernel,
        in_specs=in_specs,
        out_shape=out_shape,
        out_specs=jax.tree.map(lambda _: VMEM, out_shape),
        scratch_shapes=scratch,
        compiler_params=PARAMS,
        cost_estimate=pl.CostEstimate(flops=flops, bytes_accessed=bytes_accessed, transcendentals=0),
    )


def in_hbm(*arrays):
    return [pltpu.with_memory_space_constraint(x, pltpu.HBM) for x in arrays]


def others(x, axis):
    n = lax.axis_size(axis)
    return [x] + [lax.ppermute(x, axis, [(i, i ^ k) for i in range(n)]) for k in range(1, n)]


def body(
    memory_hidden,
    kv_weight,
    kv_bias,
    memory_sections,
    group_sections,
    queries,
    new_keys,
    new_values,
    cache_keys,
    cache_values,
    cache_lengths,
    out_weight,
):
    groups, shares = lax.axis_size("dp"), lax.axis_size("tp")
    memory, depth = memory_hidden.shape
    requests, slots, cols = cache_keys.shape
    tokens = requests * NEW
    rows = (cols // HD) * PER_HEAD * tokens
    every = memory_sections.shape[0]

    hidden = others(memory_hidden, "tp")
    part, weight, bias, own = call(
        cache_kernel,
        [SMEM] * 2 + [HBM] * 8,
        [
            pltpu.VMEM((2 * up(rows, 16) + STATS, HD), bf16),
            pltpu.VMEM(kv_weight.shape, bf16),
            pltpu.VMEM(kv_bias.shape, bf16),
            pltpu.VMEM(memory_hidden.shape, bf16),
        ],
        [
            pltpu.VMEM(queries.shape, bf16),
            pltpu.VMEM(new_keys.shape, bf16),
            pltpu.VMEM(new_values.shape, bf16),
            pltpu.VMEM(cache_keys.shape, bf16),
            pltpu.VMEM(cache_values.shape, bf16),
            pltpu.SemaphoreType.DMA((8 + 2 * requests,)),
        ],
        4 * rows * slots * cols * requests,
        2 * 2 * requests * slots * cols + 4 * D * cols,
    )(
        cache_lengths,
        group_sections,
        *in_hbm(
            queries, new_keys, new_values, cache_keys, cache_values, kv_weight, kv_bias, memory_hidden
        ),
    )
    parts = others(part, "dp")
    kv = call(
        functools.partial(project_kernel, shares),
        [VMEM] * (shares + 2) + [ANY] * groups,
        jax.ShapeDtypeStruct((2 * memory, cols), bf16),
        [],
        4 * memory * D * cols,
        4 * D * cols,
    )(own, *hidden[1:], weight, bias, *parts)
    kvs = others(kv, "dp")

    out_rows, out_cols = groups * tokens, out_weight.shape[1]
    share = out_rows // shares
    held = bf16 if memory % 16 == 0 else f32
    pieces = call(
        functools.partial(attend_kernel, groups, shares),
        [VMEM] * (2 * groups + 2),
        [jax.ShapeDtypeStruct((share, out_cols), f32 if k == 0 else bf16) for k in range(shares)],
        [
            pltpu.VMEM((every, cols), held),
            pltpu.VMEM((every, cols), held),
            pltpu.VMEM((out_rows, out_weight.shape[0]), f32),
            pltpu.VMEM((out_rows, out_cols), f32),
        ],
        2 * out_rows * out_weight.size,
        2 * out_weight.size,
    )(*parts, *kvs, memory_sections.reshape(1, every), out_weight)
    summed = pieces[0]
    for k in range(1, shares):
        summed = summed + lax.ppermute(pieces[k], "tp", [(i, i ^ k) for i in range(shares)]).astype(f32)
    return summed.astype(bf16)


def solution(mesh):
    return jax.shard_map(
        body,
        mesh=mesh,
        in_specs=(
            P(("parts", "dp"), "tp"),
            P(None, None, "tp"),
            P(None, "tp"),
            P("parts"),
            P(("parts", "dp")),
            P(("parts", "dp"), "tp"),
            P(("parts", "dp"), "tp"),
            P(("parts", "dp"), "tp"),
            P(("parts", "dp"), None, "tp"),
            P(("parts", "dp"), None, "tp"),
            P(("parts", "dp")),
            P("tp", "dp"),
        ),
        out_specs=P(("parts", "tp"), "dp"),
        check_vma=False,
    )
```

```python
import functools

import jax
import jax.numpy as jnp
from jax import lax
from jax.experimental import pallas as pl
from jax.experimental.pallas import tpu as pltpu
from jax.sharding import PartitionSpec as P

D = 5120
HQ = 40
KVH = 8
HD = 128
NEW = 2
PER_HEAD = HQ // KVH
INV = 1.0 / HD**0.5

masked_score = -1e30
bf16 = jnp.bfloat16
f32 = jnp.float32

TOP, TOTAL, SECTION = 0, 3, 5
STATS = 16


def nt(a, b):
    return lax.dot_general(a, b, (((1,), (1,)), ((), ())), preferred_element_type=f32)


def nn(a, b):
    return jnp.dot(a, b, preferred_element_type=f32)


def spread(blocks):
    zeros = jnp.zeros_like(blocks[0])
    rows = [
        jnp.concatenate([b if i == j else zeros for i in range(len(blocks))], axis=1)
        if len(blocks) > 1
        else b
        for j, b in enumerate(blocks)
    ]
    return jnp.concatenate(rows, axis=0)


def split(x, pieces):
    out = []
    for _ in range(pieces):
        piece = x.astype(bf16).astype(f32)
        out.append(piece)
        x = x - piece
    return out


def eye(rows, cols):
    row = lax.broadcasted_iota(jnp.int32, (rows, cols), 0)
    return (row == lax.broadcasted_iota(jnp.int32, (rows, cols), 1)).astype(f32).astype(bf16)


def up(n, to):
    return -(-n // to) * to


def cache_kernel(
    group_ref, lens_hbm, q_hbm, nk_hbm, nv_hbm, ck_hbm, cv_hbm, b_hbm, h_hbm, early,
    out_ref, b_ref, h_ref,
    lens_ref, q_ref, nk_ref, nv_ref, ck_ref, cv_ref, sems,
):
    requests, slots, cols = ck_ref.shape
    small = [
        pltpu.make_async_copy(src, dst, sems.at[i])
        for i, (src, dst) in enumerate(
            [(lens_hbm, lens_ref), (q_hbm, q_ref), (nk_hbm, nk_ref), (nv_hbm, nv_ref)]
        )
    ]
    first = len(small)
    keys = [pltpu.make_async_copy(ck_hbm.at[r], ck_ref.at[r], sems.at[first + r]) for r in range(requests)]
    first += requests
    values = [pltpu.make_async_copy(cv_hbm.at[r], cv_ref.at[r], sems.at[first + r]) for r in range(requests)]
    first += requests
    kept = [
        pltpu.make_async_copy(src, dst, sems.at[first + i])
        for i, (src, dst) in enumerate([(h_hbm, h_ref), (b_hbm, b_ref)])
    ]
    for copy in small + keys + values + kept:
        copy.start()

    heads = cols // HD
    tokens = requests * NEW
    per = PER_HEAD * tokens
    rows = heads * per
    row = lax.broadcasted_iota(jnp.int32, (rows, 1), 0)
    request = lax.rem(lax.div(row, NEW), requests)
    token = lax.rem(row, NEW)
    for copy in small:
        copy.wait()
    q = q_ref[...].astype(f32)
    blocks = []
    for j in range(heads):
        parts = [q[:, (j * PER_HEAD + g) * HD : (j * PER_HEAD + g + 1) * HD] for g in range(PER_HEAD)]
        blocks.append(jnp.concatenate(parts, axis=0))
    out_ref[0:rows, :] = jnp.concatenate(blocks, axis=0).astype(bf16)
    qs = spread(blocks).astype(bf16)
    fresh = lax.broadcasted_iota(jnp.int32, (rows, tokens), 1)
    seen = (lax.div(fresh, NEW) == request) & (lax.rem(fresh, NEW) <= token)
    s_new = jnp.where(seen, nt(qs, nk_ref[...]) * INV, masked_score)
    limit = jnp.full((rows, 1), lens_ref[0], jnp.int32)
    for r in range(1, requests):
        limit = jnp.where(request == r, lens_ref[r], limit)
    live = lax.broadcasted_iota(jnp.int32, (rows, slots), 1) < limit
    keys[0].wait()
    s = nt(qs, ck_ref[0])
    for r in range(1, requests):
        keys[r].wait()
        s = jnp.where(request == r, nt(qs, ck_ref[r]), s)
    s = jnp.where(live, s * INV, masked_score)

    top = jnp.maximum(jnp.max(s, axis=1, keepdims=True), jnp.max(s_new, axis=1, keepdims=True))
    p = jnp.where(live, jnp.exp(s - top), 0.0)
    p_new = jnp.where(seen, jnp.exp(s_new - top), 0.0)
    total = jnp.sum(p, axis=1, keepdims=True) + jnp.sum(p_new, axis=1, keepdims=True)
    p = p.astype(bf16)
    values[0].wait()
    acc = nn(p, cv_ref[0])
    for r in range(1, requests):
        values[r].wait()
        acc = jnp.where(request == r, nn(p, cv_ref[r]), acc)
    acc = acc + nn(p_new.astype(bf16).astype(f32), nv_ref[...].astype(f32))
    mine = jnp.concatenate([acc[j * per : (j + 1) * per, j * HD : (j + 1) * HD] for j in range(heads)], axis=0)
    seg = up(rows, 16)
    out_ref[seg : seg + rows, :] = (mine / total).astype(bf16)

    lane = lax.broadcasted_iota(jnp.int32, (rows, HD), 1)
    stats = jnp.where(lane == SECTION, group_ref[0].astype(f32), 0.0)
    for i, piece in enumerate(split(top, 3)):
        stats = jnp.where(lane == TOP + i, piece, stats)
    for i, piece in enumerate(split(total, 2)):
        stats = jnp.where(lane == TOTAL + i, piece, stats)
    if rows < HD:
        stats = jnp.concatenate([stats, jnp.zeros((HD - rows, HD), f32)], axis=0)
    out_ref[2 * seg : 2 * seg + STATS, :] = nt(eye(STATS, HD), stats.astype(bf16)).astype(bf16)
    for copy in kept:
        copy.wait()


def project_kernel(count, *refs):
    pieces, (b_ref, w_hbm, out_ref, w_ref, sems) = refs[:count], refs[count:]
    rows, depth = pieces[0].shape
    me = lax.axis_index("tp")
    firsts = [pl.multiple_of((me ^ k) * depth, depth) for k in range(count)]
    copies = [
        [
            pltpu.make_async_copy(
                w_hbm.at[s, pl.ds(first, depth)], w_ref.at[s, pl.ds(first, depth)], sems.at[2 * k + s]
            )
            for s in range(2)
        ]
        for k, first in enumerate(firsts)
    ]
    for pair in copies:
        for copy in pair:
            copy.start()
    squares = None
    for piece in pieces:
        wide = piece[...].astype(f32)
        square = jnp.sum(wide * wide, axis=1, keepdims=True)
        squares = square if squares is None else squares + square
    acc = [None, None]
    for k, piece in enumerate(pieces):
        for s in range(2):
            copies[k][s].wait()
            term = nn(piece[...], w_ref[s, pl.ds(firsts[k], depth), :])
            acc[s] = term if acc[s] is None else acc[s] + term
    scale = lax.rsqrt(squares / D + 1e-06)
    for s in range(2):
        bias = b_ref[s : s + 1, :].astype(f32)
        out_ref[s * rows : (s + 1) * rows, :] = (acc[s] * scale + bias).astype(bf16)


def prepare_kernel(heads, *refs):
    parts, (section_ref, q_ref, bias_ref, old_ref, stats_ref) = refs[:-5], refs[-5:]
    groups = len(parts)
    seg = (parts[0].shape[0] - STATS) // 2
    rows = q_ref.shape[0] // groups
    per = rows // heads
    blocks = [part[0:rows, :].astype(f32) for part in parts]
    q_ref[...] = jnp.concatenate(
        [spread([b[j * per : (j + 1) * per, :] for j in range(heads)]) for b in blocks], axis=0
    ).astype(bf16)
    stats = nt(
        eye(rows, HD), jnp.concatenate([part[2 * seg : 2 * seg + STATS, :] for part in parts], axis=0)
    )

    def column(at, pieces):
        columns = []
        for k in range(groups):
            c = k * STATS + at
            columns.append(sum([stats[:, c + i : c + i + 1] for i in range(pieces)]))
        return jnp.concatenate(columns, axis=0)

    top, total = column(TOP, 3), column(TOTAL, 2)
    bias_ref[...] = jnp.where(column(SECTION, 1) == section_ref[...].astype(f32), 0.0, masked_score)
    old = jnp.concatenate([part[seg : seg + rows, :] for part in parts], axis=0).astype(f32)
    old_ref[...] = old * total
    lane = lax.broadcasted_iota(jnp.int32, stats_ref.shape, 1)
    stats_ref[...] = jnp.where(lane == 0, top, total)


def attend_kernel(groups, shares, *refs):
    kvs, (q_ref, bias_ref, old_ref, stats_ref, w_ref) = refs[:groups], refs[groups : groups + 5]
    outs = refs[groups + 5 : groups + 5 + shares]
    k_ref, v_ref, attended_ref, sums_ref = refs[groups + 5 + shares :]
    me_dp, me_tp = lax.axis_index("dp"), lax.axis_index("tp")
    memory = kvs[0].shape[0] // 2
    heads = kvs[0].shape[1] // HD
    tokens = attended_ref.shape[0] // groups
    per = PER_HEAD * tokens
    rows = heads * per
    for k, kv in enumerate(kvs):
        first = pl.multiple_of((me_dp ^ k) * memory, memory)
        k_ref[pl.ds(first, memory), :] = kv[0:memory, :].astype(k_ref.dtype)
        v_ref[pl.ds(first, memory), :] = kv[memory : 2 * memory, :].astype(v_ref.dtype)
    s = nt(q_ref[...], k_ref[...].astype(bf16)) * INV + bias_ref[...]
    old_top, old_total = stats_ref[:, 0:1], stats_ref[:, 1:2]
    top = jnp.maximum(jnp.max(s, axis=1, keepdims=True), old_top)
    p = jnp.exp(s - top)
    shrink = jnp.exp(old_top - top)
    total = jnp.sum(p, axis=1, keepdims=True) + shrink * old_total
    acc = nn(p.astype(bf16), v_ref[...].astype(bf16))
    for k in range(groups):
        at = pl.multiple_of((me_dp ^ k) * tokens, tokens)
        for j in range(heads):
            a = k * rows + j * per
            block = acc[a : a + per, j * HD : (j + 1) * HD] + old_ref[a : a + per, :] * shrink[a : a + per]
            block = block / total[a : a + per]
            for g in range(PER_HEAD):
                c = (j * PER_HEAD + g) * HD
                attended_ref[pl.ds(at, tokens), c : c + HD] = block[g * tokens : (g + 1) * tokens, :]
    sums_ref[...] = nn(attended_ref[...].astype(bf16), w_ref[...])
    share = sums_ref.shape[0] // shares
    for k, out in enumerate(outs):
        at = pl.multiple_of((me_tp ^ k) * share, share)
        out[...] = sums_ref[pl.ds(at, share), :].astype(out.dtype)


SMEM = pl.BlockSpec(memory_space=pltpu.SMEM)
VMEM = pl.BlockSpec(memory_space=pltpu.VMEM)
ANY = pl.BlockSpec(memory_space=pl.ANY)
HBM = pl.BlockSpec(memory_space=pltpu.HBM)
PARAMS = pltpu.CompilerParams(vmem_limit_bytes=24 * 1024 * 1024)


def call(kernel, in_specs, out_shape, scratch, flops, bytes_accessed):
    return pl.pallas_call(
        kernel,
        in_specs=in_specs,
        out_shape=out_shape,
        out_specs=jax.tree.map(lambda _: VMEM, out_shape),
        scratch_shapes=scratch,
        compiler_params=PARAMS,
        cost_estimate=pl.CostEstimate(flops=flops, bytes_accessed=bytes_accessed, transcendentals=0),
    )


def in_hbm(*arrays):
    return [pltpu.with_memory_space_constraint(x, pltpu.HBM) for x in arrays]


def others(x, axis):
    n = lax.axis_size(axis)
    return [x] + [lax.ppermute(x, axis, [(i, i ^ k) for i in range(n)]) for k in range(1, n)]


def body(
    memory_hidden,
    kv_weight,
    kv_bias,
    memory_sections,
    group_sections,
    queries,
    new_keys,
    new_values,
    cache_keys,
    cache_values,
    cache_lengths,
    out_weight,
):
    groups, shares = lax.axis_size("dp"), lax.axis_size("tp")
    memory, depth = memory_hidden.shape
    requests, slots, cols = cache_keys.shape
    tokens = requests * NEW
    rows = (cols // HD) * PER_HEAD * tokens
    every = memory_sections.shape[0]

    hidden = others(memory_hidden, "tp")
    part, bias, own = call(
        cache_kernel,
        [SMEM] + [HBM] * 8 + [ANY],
        [
            pltpu.VMEM((2 * up(rows, 16) + STATS, HD), bf16),
            pltpu.VMEM(kv_bias.shape, bf16),
            pltpu.VMEM(memory_hidden.shape, bf16),
        ],
        [
            pltpu.SMEM(cache_lengths.shape, jnp.int32),
            pltpu.VMEM(queries.shape, bf16),
            pltpu.VMEM(new_keys.shape, bf16),
            pltpu.VMEM(new_values.shape, bf16),
            pltpu.VMEM(cache_keys.shape, bf16),
            pltpu.VMEM(cache_values.shape, bf16),
            pltpu.SemaphoreType.DMA((6 + 2 * requests,)),
        ],
        4 * rows * slots * cols * requests,
        4 * D * cols + 4 * requests * slots * cols,
    )(
        group_sections,
        *in_hbm(
            cache_lengths, queries, new_keys, new_values, cache_keys, cache_values, kv_bias, memory_hidden
        ),
        hidden[1],
    )
    parts = others(part, "dp")
    kv = call(
        functools.partial(project_kernel, shares),
        [VMEM] * (shares + 1) + [HBM],
        pltpu.VMEM((2 * memory, cols), bf16),
        [pltpu.VMEM(kv_weight.shape, bf16), pltpu.SemaphoreType.DMA((2 * shares,))],
        4 * memory * D * cols,
        4 * D * cols,
    )(own, *hidden[1:], bias, *in_hbm(kv_weight))
    kv = pl.pallas_call(
        lambda *refs: None,
        in_specs=[VMEM] + [ANY] * groups,
        out_shape=pltpu.VMEM(kv.shape, bf16),
        out_specs=VMEM,
        input_output_aliases={0: 0},
        compiler_params=PARAMS,
    )(kv, *parts)
    kvs = others(kv, "dp")
    prepared = call(
        functools.partial(prepare_kernel, cols // HD),
        [VMEM] * (groups + 1),
        [
            pltpu.VMEM((groups * rows, cols), bf16),
            pltpu.VMEM((groups * rows, every), f32),
            pltpu.VMEM((groups * rows, HD), f32),
            pltpu.VMEM((groups * rows, HD), f32),
        ],
        [],
        2 * groups * rows * HD * STATS * groups,
        16 * D * cols,
    )(*parts, memory_sections.reshape(1, every))

    out_rows, out_cols = groups * tokens, out_weight.shape[1]
    share = out_rows // shares
    held = bf16 if memory % 16 == 0 else f32
    pieces = call(
        functools.partial(attend_kernel, groups, shares),
        [VMEM] * (groups + 5),
        [pltpu.VMEM((share, out_cols), f32 if k == 0 else bf16) for k in range(shares)],
        [
            pltpu.VMEM((every, cols), held),
            pltpu.VMEM((every, cols), held),
            pltpu.VMEM((out_rows, out_weight.shape[0]), f32),
            pltpu.VMEM((out_rows, out_cols), f32),
        ],
        2 * out_rows * out_weight.size,
        2 * out_weight.size,
    )(*kvs, *prepared, out_weight)
    summed = pieces[0]
    for k in range(1, shares):
        summed = summed + lax.ppermute(pieces[k], "tp", [(i, i ^ k) for i in range(shares)]).astype(f32)
    return summed.astype(bf16)


def solution(mesh):
    return jax.shard_map(
        body,
        mesh=mesh,
        in_specs=(
            P(("parts", "dp"), "tp"),
            P(None, None, "tp"),
            P(None, "tp"),
            P("parts"),
            P(("parts", "dp")),
            P(("parts", "dp"), "tp"),
            P(("parts", "dp"), "tp"),
            P(("parts", "dp"), "tp"),
            P(("parts", "dp"), None, "tp"),
            P(("parts", "dp"), None, "tp"),
            P(("parts", "dp")),
            P("tp", "dp"),
        ),
        out_specs=P(("parts", "tp"), "dp"),
        check_vma=False,
    )
```

```python
import functools

import jax
import jax.numpy as jnp
from jax import lax
from jax.experimental import pallas as pl
from jax.experimental.pallas import tpu as pltpu
from jax.sharding import PartitionSpec as P

D = 5120
HQ = 40
KVH = 8
HD = 128
NEW = 2
PER_HEAD = HQ // KVH
INV = 1.0 / HD**0.5

masked_score = -1e30
bf16 = jnp.bfloat16
f32 = jnp.float32

TOP, TOTAL, SECTION = 0, 3, 5
STATS = 16


def nt(a, b):
    return lax.dot_general(a, b, (((1,), (1,)), ((), ())), preferred_element_type=f32)


def nn(a, b):
    return jnp.dot(a, b, preferred_element_type=f32)


def spread(blocks):
    zeros = jnp.zeros_like(blocks[0])
    rows = [
        jnp.concatenate([b if i == j else zeros for i in range(len(blocks))], axis=1)
        if len(blocks) > 1
        else b
        for j, b in enumerate(blocks)
    ]
    return jnp.concatenate(rows, axis=0)


def split(x, pieces):
    out = []
    for _ in range(pieces):
        piece = x.astype(bf16).astype(f32)
        out.append(piece)
        x = x - piece
    return out


def eye(rows, cols):
    row = lax.broadcasted_iota(jnp.int32, (rows, cols), 0)
    return (row == lax.broadcasted_iota(jnp.int32, (rows, cols), 1)).astype(f32).astype(bf16)


def up(n, to):
    return -(-n // to) * to


def cache_kernel(lens_ref, group_ref, q_ref, nk_ref, nv_ref, ck_ref, cv_ref, after, out_ref):
    requests, slots, cols = ck_ref.shape
    heads = cols // HD
    tokens = requests * NEW
    per = PER_HEAD * tokens
    rows = heads * per
    row = lax.broadcasted_iota(jnp.int32, (rows, 1), 0)
    request = lax.rem(lax.div(row, NEW), requests)
    token = lax.rem(row, NEW)
    q = q_ref[...].astype(f32)
    blocks = []
    for j in range(heads):
        parts = [q[:, (j * PER_HEAD + g) * HD : (j * PER_HEAD + g + 1) * HD] for g in range(PER_HEAD)]
        blocks.append(jnp.concatenate(parts, axis=0))
    out_ref[0:rows, :] = jnp.concatenate(blocks, axis=0).astype(bf16)
    qs = spread(blocks).astype(bf16)
    fresh = lax.broadcasted_iota(jnp.int32, (rows, tokens), 1)
    seen = (lax.div(fresh, NEW) == request) & (lax.rem(fresh, NEW) <= token)
    s_new = jnp.where(seen, nt(qs, nk_ref[...]) * INV, masked_score)
    limit = jnp.full((rows, 1), lens_ref[0], jnp.int32)
    for r in range(1, requests):
        limit = jnp.where(request == r, lens_ref[r], limit)
    live = lax.broadcasted_iota(jnp.int32, (rows, slots), 1) < limit
    s = nt(qs, ck_ref[0])
    for r in range(1, requests):
        s = jnp.where(request == r, nt(qs, ck_ref[r]), s)
    s = jnp.where(live, s * INV, masked_score)

    top = jnp.maximum(jnp.max(s, axis=1, keepdims=True), jnp.max(s_new, axis=1, keepdims=True))
    p = jnp.where(live, jnp.exp(s - top), 0.0)
    p_new = jnp.where(seen, jnp.exp(s_new - top), 0.0)
    total = jnp.sum(p, axis=1, keepdims=True) + jnp.sum(p_new, axis=1, keepdims=True)
    p = p.astype(bf16)
    acc = nn(p, cv_ref[0])
    for r in range(1, requests):
        acc = jnp.where(request == r, nn(p, cv_ref[r]), acc)
    acc = acc + nn(p_new.astype(bf16).astype(f32), nv_ref[...].astype(f32))
    mine = jnp.concatenate([acc[j * per : (j + 1) * per, j * HD : (j + 1) * HD] for j in range(heads)], axis=0)
    seg = up(rows, 16)
    out_ref[seg : seg + rows, :] = (mine / total).astype(bf16)

    lane = lax.broadcasted_iota(jnp.int32, (rows, HD), 1)
    stats = jnp.where(lane == SECTION, group_ref[0].astype(f32), 0.0)
    for i, piece in enumerate(split(top, 3)):
        stats = jnp.where(lane == TOP + i, piece, stats)
    for i, piece in enumerate(split(total, 2)):
        stats = jnp.where(lane == TOTAL + i, piece, stats)
    if rows < HD:
        stats = jnp.concatenate([stats, jnp.zeros((HD - rows, HD), f32)], axis=0)
    out_ref[2 * seg : 2 * seg + STATS, :] = nt(eye(STATS, HD), stats.astype(bf16)).astype(bf16)


def project_kernel(count, *refs):
    pieces, (w_ref, b_ref, out_ref) = refs[:count], refs[count:]
    rows, depth = pieces[0].shape
    me = lax.axis_index("tp")
    acc = [None, None]
    squares = None
    for k, piece in enumerate(pieces):
        h = piece[...]
        wide = h.astype(f32)
        square = jnp.sum(wide * wide, axis=1, keepdims=True)
        squares = square if squares is None else squares + square
        first = pl.multiple_of((me ^ k) * depth, depth)
        for s in range(2):
            term = nn(h, w_ref[s, pl.ds(first, depth), :])
            acc[s] = term if acc[s] is None else acc[s] + term
    scale = lax.rsqrt(squares / D + 1e-06)
    for s in range(2):
        bias = b_ref[s : s + 1, :].astype(f32)
        out_ref[s * rows : (s + 1) * rows, :] = (acc[s] * scale + bias).astype(bf16)


def prepare_kernel(heads, *refs):
    parts, (section_ref, q_ref, bias_ref, old_ref, stats_ref) = refs[:-5], refs[-5:]
    groups = len(parts)
    seg = (parts[0].shape[0] - STATS) // 2
    rows = q_ref.shape[0] // groups
    per = rows // heads
    blocks = [part[0:rows, :].astype(f32) for part in parts]
    q_ref[...] = jnp.concatenate(
        [spread([b[j * per : (j + 1) * per, :] for j in range(heads)]) for b in blocks], axis=0
    ).astype(bf16)
    stats = nt(
        eye(rows, HD), jnp.concatenate([part[2 * seg : 2 * seg + STATS, :] for part in parts], axis=0)
    )

    def column(at, pieces):
        columns = []
        for k in range(groups):
            c = k * STATS + at
            columns.append(sum([stats[:, c + i : c + i + 1] for i in range(pieces)]))
        return jnp.concatenate(columns, axis=0)

    top, total = column(TOP, 3), column(TOTAL, 2)
    bias_ref[...] = jnp.where(column(SECTION, 1) == section_ref[...].astype(f32), 0.0, masked_score)
    old = jnp.concatenate([part[seg : seg + rows, :] for part in parts], axis=0).astype(f32)
    old_ref[...] = old * total
    lane = lax.broadcasted_iota(jnp.int32, stats_ref.shape, 1)
    stats_ref[...] = jnp.where(lane == 0, top, total)


def attend_kernel(groups, shares, *refs):
    kvs, (q_ref, bias_ref, old_ref, stats_ref, w_ref) = refs[:groups], refs[groups : groups + 5]
    out_ref, k_ref, v_ref, attended_ref, sums_ref = refs[groups + 5 :]
    me_dp, me_tp = lax.axis_index("dp"), lax.axis_index("tp")
    memory = kvs[0].shape[0] // 2
    heads = kvs[0].shape[1] // HD
    tokens = attended_ref.shape[0] // groups
    per = PER_HEAD * tokens
    rows = heads * per
    for k, kv in enumerate(kvs):
        first = pl.multiple_of((me_dp ^ k) * memory, memory)
        k_ref[pl.ds(first, memory), :] = kv[0:memory, :].astype(k_ref.dtype)
        v_ref[pl.ds(first, memory), :] = kv[memory : 2 * memory, :].astype(v_ref.dtype)
    s = nt(q_ref[...], k_ref[...].astype(bf16)) * INV + bias_ref[...]
    old_top, old_total = stats_ref[:, 0:1], stats_ref[:, 1:2]
    top = jnp.maximum(jnp.max(s, axis=1, keepdims=True), old_top)
    p = jnp.exp(s - top)
    shrink = jnp.exp(old_top - top)
    total = jnp.sum(p, axis=1, keepdims=True) + shrink * old_total
    acc = nn(p.astype(bf16), v_ref[...].astype(bf16))
    for k in range(groups):
        at = pl.multiple_of((me_dp ^ k) * tokens, tokens)
        for j in range(heads):
            a = k * rows + j * per
            block = acc[a : a + per, j * HD : (j + 1) * HD] + old_ref[a : a + per, :] * shrink[a : a + per]
            block = block / total[a : a + per]
            for g in range(PER_HEAD):
                c = (j * PER_HEAD + g) * HD
                attended_ref[pl.ds(at, tokens), c : c + HD] = block[g * tokens : (g + 1) * tokens, :]
    sums_ref[...] = nn(attended_ref[...].astype(bf16), w_ref[...])
    share = sums_ref.shape[0] // shares
    for k in range(shares):
        out_ref[k] = sums_ref[k * share : (k + 1) * share, :].astype(bf16)


SMEM = pl.BlockSpec(memory_space=pltpu.SMEM)
VMEM = pl.BlockSpec(memory_space=pltpu.VMEM)
ANY = pl.BlockSpec(memory_space=pl.ANY)
HBM = pl.BlockSpec(memory_space=pltpu.HBM)
PARAMS = pltpu.CompilerParams(vmem_limit_bytes=24 * 1024 * 1024)


def call(kernel, in_specs, out_shape, scratch, flops, bytes_accessed):
    return pl.pallas_call(
        kernel,
        in_specs=in_specs,
        out_shape=out_shape,
        out_specs=jax.tree.map(lambda _: VMEM, out_shape),
        scratch_shapes=scratch,
        compiler_params=PARAMS,
        cost_estimate=pl.CostEstimate(flops=flops, bytes_accessed=bytes_accessed, transcendentals=0),
    )


def in_hbm(*arrays):
    return [pltpu.with_memory_space_constraint(x, pltpu.HBM) for x in arrays]


def others(x, axis):
    n = lax.axis_size(axis)
    return [x] + [lax.ppermute(x, axis, [(i, i ^ k) for i in range(n)]) for k in range(1, n)]


def body(
    memory_hidden,
    kv_weight,
    kv_bias,
    memory_sections,
    group_sections,
    queries,
    new_keys,
    new_values,
    cache_keys,
    cache_values,
    cache_lengths,
    out_weight,
):
    groups, shares = lax.axis_size("dp"), lax.axis_size("tp")
    memory, depth = memory_hidden.shape
    requests, slots, cols = cache_keys.shape
    tokens = requests * NEW
    rows = (cols // HD) * PER_HEAD * tokens
    every = memory_sections.shape[0]

    hidden = others(memory_hidden, "tp")
    opened = call(
        lambda *refs: None,
        [ANY],
        jax.ShapeDtypeStruct((8, HD), f32),
        [],
        1 << 36,
        64 * D * cols,
    )(hidden[1])
    part = call(
        cache_kernel,
        [SMEM] * 2 + [VMEM] * 5 + [ANY],
        pltpu.VMEM((2 * up(rows, 16) + STATS, HD), bf16),
        [],
        4 * rows * slots * cols * requests,
        4 * requests * slots * cols,
    )(cache_lengths, group_sections, queries, new_keys, new_values, cache_keys, cache_values, opened)
    parts = others(part, "dp")
    kv = call(
        functools.partial(project_kernel, shares),
        [VMEM] * (shares + 2),
        pltpu.VMEM((2 * memory, cols), bf16),
        [],
        4 * memory * D * cols,
        4 * D * cols,
    )(*hidden, kv_weight, kv_bias)
    kv = pl.pallas_call(
        lambda *refs: None,
        in_specs=[VMEM] + [ANY] * groups,
        out_shape=pltpu.VMEM(kv.shape, bf16),
        out_specs=VMEM,
        input_output_aliases={0: 0},
        compiler_params=PARAMS,
    )(kv, *parts)
    kvs = others(kv, "dp")
    prepared = call(
        functools.partial(prepare_kernel, cols // HD),
        [VMEM] * (groups + 1),
        [
            pltpu.VMEM((groups * rows, cols), bf16),
            pltpu.VMEM((groups * rows, every), f32),
            pltpu.VMEM((groups * rows, HD), f32),
            pltpu.VMEM((groups * rows, HD), f32),
        ],
        [],
        2 * groups * rows * HD * STATS * groups,
        16 * D * cols,
    )(*parts, memory_sections.reshape(1, every))

    out_rows, out_cols = groups * tokens, out_weight.shape[1]
    share = out_rows // shares
    held = bf16 if memory % 16 == 0 else f32
    sent = call(
        functools.partial(attend_kernel, groups, shares),
        [VMEM] * (groups + 5),
        pltpu.VMEM((shares, share, out_cols), bf16),
        [
            pltpu.VMEM((every, cols), held),
            pltpu.VMEM((every, cols), held),
            pltpu.VMEM((out_rows, out_weight.shape[0]), f32),
            pltpu.VMEM((out_rows, out_cols), f32),
        ],
        2 * out_rows * out_weight.size,
        2 * out_weight.size,
    )(*kvs, *prepared, out_weight)
    return jnp.sum(lax.all_to_all(sent, "tp", 0, 0, tiled=True).astype(f32), axis=0).astype(bf16)


def solution(mesh):
    return jax.shard_map(
        body,
        mesh=mesh,
        in_specs=(
            P(("parts", "dp"), "tp"),
            P(None, None, "tp"),
            P(None, "tp"),
            P("parts"),
            P(("parts", "dp")),
            P(("parts", "dp"), "tp"),
            P(("parts", "dp"), "tp"),
            P(("parts", "dp"), "tp"),
            P(("parts", "dp"), None, "tp"),
            P(("parts", "dp"), None, "tp"),
            P(("parts", "dp")),
            P("tp", "dp"),
        ),
        out_specs=P(("parts", "tp"), "dp"),
        check_vma=False,
    )
```

```python
import functools

import jax
import jax.numpy as jnp
from jax import lax
from jax.experimental import pallas as pl
from jax.experimental.pallas import tpu as pltpu
from jax.sharding import PartitionSpec as P

D = 5120
HQ = 40
KVH = 8
HD = 128
NEW = 2
PER_HEAD = HQ // KVH
INV = 1.0 / HD**0.5

masked_score = -1e30
bf16 = jnp.bfloat16
f32 = jnp.float32

TOP, TOTAL, SECTION = 0, 3, 5
STATS = 16


def nt(a, b):
    return lax.dot_general(a, b, (((1,), (1,)), ((), ())), preferred_element_type=f32)


def nn(a, b):
    return jnp.dot(a, b, preferred_element_type=f32)


def spread(blocks):
    zeros = jnp.zeros_like(blocks[0])
    rows = [
        jnp.concatenate([b if i == j else zeros for i in range(len(blocks))], axis=1)
        if len(blocks) > 1
        else b
        for j, b in enumerate(blocks)
    ]
    return jnp.concatenate(rows, axis=0)


def split(x, pieces):
    out = []
    for _ in range(pieces):
        piece = x.astype(bf16).astype(f32)
        out.append(piece)
        x = x - piece
    return out


def eye(rows, cols):
    row = lax.broadcasted_iota(jnp.int32, (rows, cols), 0)
    return (row == lax.broadcasted_iota(jnp.int32, (rows, cols), 1)).astype(f32).astype(bf16)


def up(n, to):
    return -(-n // to) * to


def cache_kernel(lens_ref, group_ref, q_ref, nk_ref, nv_ref, ck_ref, cv_ref, after, out_ref):
    requests, slots, cols = ck_ref.shape
    heads = cols // HD
    tokens = requests * NEW
    per = PER_HEAD * tokens
    rows = heads * per
    row = lax.broadcasted_iota(jnp.int32, (rows, 1), 0)
    request = lax.rem(lax.div(row, NEW), requests)
    token = lax.rem(row, NEW)
    q = q_ref[...].astype(f32)
    blocks = []
    for j in range(heads):
        parts = [q[:, (j * PER_HEAD + g) * HD : (j * PER_HEAD + g + 1) * HD] for g in range(PER_HEAD)]
        blocks.append(jnp.concatenate(parts, axis=0))
    qs = spread(blocks).astype(bf16)
    fresh = lax.broadcasted_iota(jnp.int32, (rows, tokens), 1)
    seen = (lax.div(fresh, NEW) == request) & (lax.rem(fresh, NEW) <= token)
    s_new = jnp.where(seen, nt(qs, nk_ref[...]) * INV, masked_score)
    limit = jnp.full((rows, 1), lens_ref[0], jnp.int32)
    for r in range(1, requests):
        limit = jnp.where(request == r, lens_ref[r], limit)
    live = lax.broadcasted_iota(jnp.int32, (rows, slots), 1) < limit
    s = nt(qs, ck_ref[0])
    for r in range(1, requests):
        s = jnp.where(request == r, nt(qs, ck_ref[r]), s)
    s = jnp.where(live, s * INV, masked_score)

    top = jnp.maximum(jnp.max(s, axis=1, keepdims=True), jnp.max(s_new, axis=1, keepdims=True))
    p = jnp.where(live, jnp.exp(s - top), 0.0)
    p_new = jnp.where(seen, jnp.exp(s_new - top), 0.0)
    total = jnp.sum(p, axis=1, keepdims=True) + jnp.sum(p_new, axis=1, keepdims=True)
    p = p.astype(bf16)
    acc = nn(p, cv_ref[0])
    for r in range(1, requests):
        acc = jnp.where(request == r, nn(p, cv_ref[r]), acc)
    acc = acc + nn(p_new.astype(bf16).astype(f32), nv_ref[...].astype(f32))
    mine = jnp.concatenate([acc[j * per : (j + 1) * per, j * HD : (j + 1) * HD] for j in range(heads)], axis=0)
    lane = lax.broadcasted_iota(jnp.int32, (rows, HD), 1)
    stats = jnp.where(lane == SECTION, group_ref[0].astype(f32), 0.0)
    for i, piece in enumerate(split(top, 3)):
        stats = jnp.where(lane == TOP + i, piece, stats)
    for i, piece in enumerate(split(total, 2)):
        stats = jnp.where(lane == TOTAL + i, piece, stats)
    if rows < HD:
        stats = jnp.concatenate([stats, jnp.zeros((HD - rows, HD), f32)], axis=0)
    stats = nt(eye(STATS, HD), stats.astype(bf16))
    folded = out_ref.shape[0]
    answer = jnp.concatenate([mine / total, stats], axis=0)
    if answer.shape[0] < heads * folded:
        answer = jnp.concatenate([answer, jnp.zeros((heads * folded - answer.shape[0], HD), f32)], axis=0)
    for j in range(heads):
        out_ref[:, j * HD : (j + 1) * HD] = answer[j * folded : (j + 1) * folded, :].astype(bf16)


def project_kernel(count, *refs):
    pieces, (w_ref, b_ref, answer_ref), out_ref = refs[:count], refs[count : count + 3], refs[-1]
    rows, depth = pieces[0].shape
    me = lax.axis_index("tp")
    acc = [None, None]
    squares = None
    for k, piece in enumerate(pieces):
        h = piece[...]
        wide = h.astype(f32)
        square = jnp.sum(wide * wide, axis=1, keepdims=True)
        squares = square if squares is None else squares + square
        first = pl.multiple_of((me ^ k) * depth, depth)
        for s in range(2):
            term = nn(h, w_ref[s, pl.ds(first, depth), :])
            acc[s] = term if acc[s] is None else acc[s] + term
    scale = lax.rsqrt(squares / D + 1e-06)
    for s in range(2):
        bias = b_ref[s : s + 1, :].astype(f32)
        out_ref[s * rows : (s + 1) * rows, :] = (acc[s] * scale + bias).astype(bf16)
    out_ref[2 * rows :, :] = answer_ref[...]


def prepare_kernel(heads, *refs):
    blocks = []
    for q_ref in refs[:-1]:
        q = q_ref[...].astype(f32)
        rows = []
        for j in range(heads):
            parts = [q[:, (j * PER_HEAD + g) * HD : (j * PER_HEAD + g + 1) * HD] for g in range(PER_HEAD)]
            rows.append(jnp.concatenate(parts, axis=0))
        blocks.append(spread(rows))
    refs[-1][...] = jnp.concatenate(blocks, axis=0).astype(bf16)


def attend_kernel(groups, shares, *refs):
    kvs, (q_ref, section_ref, w_ref) = refs[:groups], refs[groups : groups + 3]
    keep_ref, give_ref, k_ref, v_ref, attended_ref, sums_ref = refs[groups + 3 :]
    me_dp, me_tp = lax.axis_index("dp"), lax.axis_index("tp")
    memory = k_ref.shape[0] // groups
    heads = kvs[0].shape[1] // HD
    tokens = attended_ref.shape[0] // groups
    per = PER_HEAD * tokens
    rows = heads * per
    answers, stats = [], []
    for k, kv in enumerate(kvs):
        first = pl.multiple_of((me_dp ^ k) * memory, memory)
        k_ref[pl.ds(first, memory), :] = kv[0:memory, :].astype(k_ref.dtype)
        v_ref[pl.ds(first, memory), :] = kv[memory : 2 * memory, :].astype(v_ref.dtype)
        answer = kv[2 * memory :, :].astype(f32)
        answer = jnp.concatenate([answer[:, j * HD : (j + 1) * HD] for j in range(heads)], axis=0)
        answers.append(answer[0:rows])
        stats.append(answer[rows : rows + STATS])
    old = jnp.concatenate(answers, axis=0)
    stats = nt(eye(rows, HD), jnp.concatenate(stats, axis=0).astype(bf16))

    def column(at, pieces):
        columns = []
        for k in range(groups):
            c = k * STATS + at
            columns.append(sum([stats[:, c + i : c + i + 1] for i in range(pieces)]))
        return jnp.concatenate(columns, axis=0)

    old_top, old_total = column(TOP, 3), column(TOTAL, 2)
    ok = column(SECTION, 1) == section_ref[...].astype(f32)
    s = jnp.where(ok, nt(q_ref[...], k_ref[...].astype(bf16)) * INV, masked_score)
    top = jnp.maximum(jnp.max(s, axis=1, keepdims=True), old_top)
    p = jnp.where(ok, jnp.exp(s - top), 0.0)
    old_weight = jnp.exp(old_top - top) * old_total
    total = jnp.sum(p, axis=1, keepdims=True) + old_weight
    acc = nn(p.astype(bf16), v_ref[...].astype(bf16))
    for k in range(groups):
        at = pl.multiple_of((me_dp ^ k) * tokens, tokens)
        for j in range(heads):
            a = k * rows + j * per
            block = acc[a : a + per, j * HD : (j + 1) * HD] + old[a : a + per, :] * old_weight[a : a + per]
            block = block / total[a : a + per]
            for g in range(PER_HEAD):
                c = (j * PER_HEAD + g) * HD
                attended_ref[pl.ds(at, tokens), c : c + HD] = block[g * tokens : (g + 1) * tokens, :]
    sums_ref[...] = nn(attended_ref[...].astype(bf16), w_ref[...])
    share = sums_ref.shape[0] // shares
    for k in range(shares):
        at = pl.multiple_of((me_tp ^ k) * share, share)
        out = give_ref if k % 2 else keep_ref
        out[k // 2] = sums_ref[pl.ds(at, share), :]


SMEM = pl.BlockSpec(memory_space=pltpu.SMEM)
VMEM = pl.BlockSpec(memory_space=pltpu.VMEM)
ANY = pl.BlockSpec(memory_space=pl.ANY)
PARAMS = pltpu.CompilerParams(vmem_limit_bytes=24 * 1024 * 1024)


def call(kernel, in_specs, out_shape, scratch, flops, bytes_accessed):
    return pl.pallas_call(
        kernel,
        in_specs=in_specs,
        out_shape=out_shape,
        out_specs=jax.tree.map(lambda _: VMEM, out_shape),
        scratch_shapes=scratch,
        compiler_params=PARAMS,
        cost_estimate=pl.CostEstimate(flops=flops, bytes_accessed=bytes_accessed, transcendentals=0),
    )


def permute(x, axis, bits):
    return lax.ppermute(x, axis, [(i, i ^ bits) for i in range(lax.axis_size(axis))])


def others(x, axis):
    return [x] + [permute(x, axis, bits) for bits in range(1, lax.axis_size(axis))]


def passed_on(x, axis):
    n = lax.axis_size(axis)
    held = {0: x}
    bit = n // 2
    while bit:
        for bits in sorted(held):
            held[bits | bit] = permute(held[bits], axis, bit)
        bit //= 2
    return [held[bits] for bits in range(n)]


def body(
    memory_hidden,
    kv_weight,
    kv_bias,
    memory_sections,
    group_sections,
    queries,
    new_keys,
    new_values,
    cache_keys,
    cache_values,
    cache_lengths,
    out_weight,
):
    groups, shares = lax.axis_size("dp"), lax.axis_size("tp")
    memory, depth = memory_hidden.shape
    requests, slots, cols = cache_keys.shape
    tokens = requests * NEW
    rows = (cols // HD) * PER_HEAD * tokens
    every = memory_sections.shape[0]

    hidden = passed_on(memory_hidden, "tp")
    asked = others(queries, "dp")
    opened = call(
        lambda *refs: None,
        [ANY],
        jax.ShapeDtypeStruct((8, HD), f32),
        [],
        1 << 36,
        64 * D * cols,
    )(hidden[1])
    heads = cols // HD
    folded = up(rows + STATS, 16 * heads) // heads
    answer = call(
        cache_kernel,
        [SMEM] * 2 + [VMEM] * 5 + [ANY],
        pltpu.VMEM((folded, cols), bf16),
        [],
        4 * rows * slots * cols * requests,
        4 * requests * slots * cols,
    )(cache_lengths, group_sections, queries, new_keys, new_values, cache_keys, cache_values, opened)
    kv = call(
        functools.partial(project_kernel, shares),
        [VMEM] * (shares + 3) + [ANY] * (groups - 1),
        pltpu.VMEM((2 * memory + folded, cols), bf16),
        [],
        4 * memory * D * cols,
        4 * D * cols,
    )(*hidden, kv_weight, kv_bias, answer, *asked[1:])
    kvs = others(kv, "dp")
    asked = call(
        functools.partial(prepare_kernel, heads),
        [VMEM] * groups,
        pltpu.VMEM((groups * rows, cols), bf16),
        [],
        groups * rows * cols,
        16 * D * cols,
    )(*asked)

    out_rows, out_cols = groups * tokens, out_weight.shape[1]
    share = out_rows // shares
    held = bf16 if memory % 16 == 0 else f32
    keep, give = call(
        functools.partial(attend_kernel, groups, shares),
        [VMEM] * (groups + 3),
        [pltpu.VMEM((shares // 2, share, out_cols), f32)] * 2,
        [
            pltpu.VMEM((every, cols), held),
            pltpu.VMEM((every, cols), held),
            pltpu.VMEM((out_rows, out_weight.shape[0]), f32),
            pltpu.VMEM((out_rows, out_cols), f32),
        ],
        2 * out_rows * out_weight.size,
        2 * out_weight.size,
    )(*kvs, asked, memory_sections.reshape(1, every), out_weight)
    bit = 1
    keep = keep + permute(give, "tp", bit)
    while keep.shape[0] > 1:
        bit *= 2
        keep = keep[0::2] + permute(keep[1::2].astype(bf16), "tp", bit).astype(f32)
    return keep[0].astype(bf16)


def solution(mesh):
    return jax.shard_map(
        body,
        mesh=mesh,
        in_specs=(
            P(("parts", "dp"), "tp"),
            P(None, None, "tp"),
            P(None, "tp"),
            P("parts"),
            P(("parts", "dp")),
            P(("parts", "dp"), "tp"),
            P(("parts", "dp"), "tp"),
            P(("parts", "dp"), "tp"),
            P(("parts", "dp"), None, "tp"),
            P(("parts", "dp"), None, "tp"),
            P(("parts", "dp")),
            P("tp", "dp"),
        ),
        out_specs=P(("parts", "tp"), "dp"),
        check_vma=False,
    )
```

```python
import functools

import jax
import jax.numpy as jnp
from jax import lax
from jax.experimental import pallas as pl
from jax.experimental.pallas import tpu as pltpu
from jax.sharding import PartitionSpec as P

D = 5120
HQ = 40
KVH = 8
HD = 128
NEW = 2
PER_HEAD = HQ // KVH
INV = 1.0 / HD**0.5

masked_score = -1e30
bf16 = jnp.bfloat16
COVER = 1 << 36
PCOVER = 1 << 30
f32 = jnp.float32

TOP, TOTAL, SECTION = 0, 3, 5
STATS = 16


def nt(a, b):
    return lax.dot_general(a, b, (((1,), (1,)), ((), ())), preferred_element_type=f32)


def nn(a, b):
    return jnp.dot(a, b, preferred_element_type=f32)


def spread(blocks):
    zeros = jnp.zeros_like(blocks[0])
    rows = [
        jnp.concatenate([b if i == j else zeros for i in range(len(blocks))], axis=1)
        if len(blocks) > 1
        else b
        for j, b in enumerate(blocks)
    ]
    return jnp.concatenate(rows, axis=0)


def split(x, pieces):
    out = []
    for _ in range(pieces):
        piece = x.astype(bf16).astype(f32)
        out.append(piece)
        x = x - piece
    return out


def eye(rows, cols):
    row = lax.broadcasted_iota(jnp.int32, (rows, cols), 0)
    return (row == lax.broadcasted_iota(jnp.int32, (rows, cols), 1)).astype(f32).astype(bf16)


def up(n, to):
    return -(-n // to) * to


def cache_kernel(lens_ref, group_ref, q_ref, nk_ref, nv_ref, ck_ref, cv_ref, after, out_ref):
    requests, slots, cols = ck_ref.shape
    heads = cols // HD
    tokens = requests * NEW
    per = PER_HEAD * tokens
    rows = heads * per
    row = lax.broadcasted_iota(jnp.int32, (rows, 1), 0)
    request = lax.rem(lax.div(row, NEW), requests)
    token = lax.rem(row, NEW)
    q = q_ref[...].astype(f32)
    blocks = []
    for j in range(heads):
        parts = [q[:, (j * PER_HEAD + g) * HD : (j * PER_HEAD + g + 1) * HD] for g in range(PER_HEAD)]
        blocks.append(jnp.concatenate(parts, axis=0))
    out_ref[0:rows, :] = jnp.concatenate(blocks, axis=0).astype(bf16)
    qs = spread(blocks).astype(bf16)
    fresh = lax.broadcasted_iota(jnp.int32, (rows, tokens), 1)
    seen = (lax.div(fresh, NEW) == request) & (lax.rem(fresh, NEW) <= token)
    s_new = jnp.where(seen, nt(qs, nk_ref[...]) * INV, masked_score)
    limit = jnp.full((rows, 1), lens_ref[0], jnp.int32)
    for r in range(1, requests):
        limit = jnp.where(request == r, lens_ref[r], limit)
    live = lax.broadcasted_iota(jnp.int32, (rows, slots), 1) < limit
    s = nt(qs, ck_ref[0])
    for r in range(1, requests):
        s = jnp.where(request == r, nt(qs, ck_ref[r]), s)
    s = jnp.where(live, s * INV, masked_score)

    top = jnp.maximum(jnp.max(s, axis=1, keepdims=True), jnp.max(s_new, axis=1, keepdims=True))
    p = jnp.where(live, jnp.exp(s - top), 0.0)
    p_new = jnp.where(seen, jnp.exp(s_new - top), 0.0)
    total = jnp.sum(p, axis=1, keepdims=True) + jnp.sum(p_new, axis=1, keepdims=True)
    p = p.astype(bf16)
    acc = nn(p, cv_ref[0])
    for r in range(1, requests):
        acc = jnp.where(request == r, nn(p, cv_ref[r]), acc)
    acc = acc + nn(p_new.astype(bf16).astype(f32), nv_ref[...].astype(f32))
    mine = jnp.concatenate([acc[j * per : (j + 1) * per, j * HD : (j + 1) * HD] for j in range(heads)], axis=0)
    seg = up(rows, 16)
    out_ref[seg : seg + rows, :] = (mine / total).astype(bf16)

    lane = lax.broadcasted_iota(jnp.int32, (rows, HD), 1)
    stats = jnp.where(lane == SECTION, group_ref[0].astype(f32), 0.0)
    for i, piece in enumerate(split(top, 3)):
        stats = jnp.where(lane == TOP + i, piece, stats)
    for i, piece in enumerate(split(total, 2)):
        stats = jnp.where(lane == TOTAL + i, piece, stats)
    if rows < HD:
        stats = jnp.concatenate([stats, jnp.zeros((HD - rows, HD), f32)], axis=0)
    out_ref[2 * seg : 2 * seg + STATS, :] = nt(eye(STATS, HD), stats.astype(bf16)).astype(bf16)


def project_kernel(bits, first, last, *refs):
    count = len(bits)
    pieces, w_ref, refs = refs[:count], refs[count], refs[count + 1 :]
    rows, depth = pieces[0].shape
    me = lax.axis_index("tp")
    if first:
        acc, squares = [None, None], None
    else:
        acc = [refs[0][s * rows : (s + 1) * rows, :] for s in range(2)]
        squares = refs[1][:, 0:1]
        refs = refs[2:]
    for k, piece in zip(bits, pieces):
        h = piece[...]
        wide = h.astype(f32)
        square = jnp.sum(wide * wide, axis=1, keepdims=True)
        squares = square if squares is None else squares + square
        at = pl.multiple_of((me ^ k) * depth, depth)
        for s in range(2):
            term = nn(h, w_ref[s, pl.ds(at, depth), :])
            acc[s] = term if acc[s] is None else acc[s] + term
    if not last:
        for s in range(2):
            refs[0][s * rows : (s + 1) * rows, :] = acc[s]
        refs[1][...] = jnp.broadcast_to(squares, refs[1].shape)
        return
    b_ref, out_ref = refs
    scale = lax.rsqrt(squares / D + 1e-06)
    for s in range(2):
        bias = b_ref[s : s + 1, :].astype(f32)
        out_ref[s * rows : (s + 1) * rows, :] = (acc[s] * scale + bias).astype(bf16)


def prepare_kernel(heads, *refs):
    parts, (section_ref, q_ref, bias_ref, old_ref, stats_ref) = refs[:-5], refs[-5:]
    groups = len(parts)
    seg = (parts[0].shape[0] - STATS) // 2
    rows = q_ref.shape[0] // groups
    per = rows // heads
    blocks = [part[0:rows, :].astype(f32) for part in parts]
    q_ref[...] = jnp.concatenate(
        [spread([b[j * per : (j + 1) * per, :] for j in range(heads)]) for b in blocks], axis=0
    ).astype(bf16)
    stats = nt(
        eye(rows, HD), jnp.concatenate([part[2 * seg : 2 * seg + STATS, :] for part in parts], axis=0)
    )

    def column(at, pieces):
        columns = []
        for k in range(groups):
            c = k * STATS + at
            columns.append(sum([stats[:, c + i : c + i + 1] for i in range(pieces)]))
        return jnp.concatenate(columns, axis=0)

    top, total = column(TOP, 3), column(TOTAL, 2)
    bias_ref[...] = jnp.where(column(SECTION, 1) == section_ref[...].astype(f32), 0.0, masked_score)
    old = jnp.concatenate([part[seg : seg + rows, :] for part in parts], axis=0).astype(f32)
    old_ref[...] = old * total
    lane = lax.broadcasted_iota(jnp.int32, stats_ref.shape, 1)
    stats_ref[...] = jnp.where(lane == 0, top, total)


def attend_kernel(groups, shares, *refs):
    kvs, (q_ref, bias_ref, old_ref, stats_ref, w_ref) = refs[:groups], refs[groups : groups + 5]
    outs = refs[groups + 5 : groups + 5 + shares]
    k_ref, v_ref, attended_ref, sums_ref = refs[groups + 5 + shares :]
    me_dp, me_tp = lax.axis_index("dp"), lax.axis_index("tp")
    memory = kvs[0].shape[0] // 2
    heads = kvs[0].shape[1] // HD
    tokens = attended_ref.shape[0] // groups
    per = PER_HEAD * tokens
    rows = heads * per
    for k, kv in enumerate(kvs):
        first = pl.multiple_of((me_dp ^ k) * memory, memory)
        k_ref[pl.ds(first, memory), :] = kv[0:memory, :].astype(k_ref.dtype)
        v_ref[pl.ds(first, memory), :] = kv[memory : 2 * memory, :].astype(v_ref.dtype)
    s = nt(q_ref[...], k_ref[...].astype(bf16)) * INV + bias_ref[...]
    old_top, old_total = stats_ref[:, 0:1], stats_ref[:, 1:2]
    top = jnp.maximum(jnp.max(s, axis=1, keepdims=True), old_top)
    p = jnp.exp(s - top)
    shrink = jnp.exp(old_top - top)
    total = jnp.sum(p, axis=1, keepdims=True) + shrink * old_total
    acc = nn(p.astype(bf16), v_ref[...].astype(bf16))
    for k in range(groups):
        at = pl.multiple_of((me_dp ^ k) * tokens, tokens)
        for j in range(heads):
            a = k * rows + j * per
            block = acc[a : a + per, j * HD : (j + 1) * HD] + old_ref[a : a + per, :] * shrink[a : a + per]
            block = block / total[a : a + per]
            for g in range(PER_HEAD):
                c = (j * PER_HEAD + g) * HD
                attended_ref[pl.ds(at, tokens), c : c + HD] = block[g * tokens : (g + 1) * tokens, :]
    sums_ref[...] = nn(attended_ref[...].astype(bf16), w_ref[...])
    share = sums_ref.shape[0] // shares
    for k, out in enumerate(outs):
        at = pl.multiple_of((me_tp ^ k) * share, share)
        out[...] = sums_ref[pl.ds(at, share), :].astype(out.dtype)


SMEM = pl.BlockSpec(memory_space=pltpu.SMEM)
VMEM = pl.BlockSpec(memory_space=pltpu.VMEM)
ANY = pl.BlockSpec(memory_space=pl.ANY)
HBM = pl.BlockSpec(memory_space=pltpu.HBM)
PARAMS = pltpu.CompilerParams(vmem_limit_bytes=24 * 1024 * 1024)


def call(kernel, in_specs, out_shape, scratch, flops, bytes_accessed):
    return pl.pallas_call(
        kernel,
        in_specs=in_specs,
        out_shape=out_shape,
        out_specs=jax.tree.map(lambda _: VMEM, out_shape),
        scratch_shapes=scratch,
        compiler_params=PARAMS,
        cost_estimate=pl.CostEstimate(flops=flops, bytes_accessed=bytes_accessed, transcendentals=0),
    )


def in_hbm(*arrays):
    return [pltpu.with_memory_space_constraint(x, pltpu.HBM) for x in arrays]


def permute(x, axis, bits):
    return lax.ppermute(x, axis, [(i, i ^ bits) for i in range(lax.axis_size(axis))])


def others(x, axis):
    return [x] + [permute(x, axis, bits) for bits in range(1, lax.axis_size(axis))]


def passed_on(x, axis):
    n = lax.axis_size(axis)
    held = {0: x}
    bit = n // 2
    while bit:
        for bits in sorted(held):
            held[bits | bit] = permute(held[bits], axis, bit)
        bit //= 2
    return [held[bits] for bits in range(n)]


def body(
    memory_hidden,
    kv_weight,
    kv_bias,
    memory_sections,
    group_sections,
    queries,
    new_keys,
    new_values,
    cache_keys,
    cache_values,
    cache_lengths,
    out_weight,
):
    groups, shares = lax.axis_size("dp"), lax.axis_size("tp")
    memory, depth = memory_hidden.shape
    requests, slots, cols = cache_keys.shape
    tokens = requests * NEW
    rows = (cols // HD) * PER_HEAD * tokens
    every = memory_sections.shape[0]

    hidden = passed_on(memory_hidden, "tp")
    opened = call(
        lambda *refs: None,
        [ANY],
        jax.ShapeDtypeStruct((8, HD), f32),
        [],
        COVER,
        0,
    )(hidden[1])
    part = call(
        cache_kernel,
        [SMEM] * 2 + [VMEM] * 5 + [ANY],
        pltpu.VMEM((2 * up(rows, 16) + STATS, HD), bf16),
        [],
        4 * rows * slots * cols * requests,
        4 * requests * slots * cols,
    )(cache_lengths, group_sections, queries, new_keys, new_values, cache_keys, cache_values, opened)
    parts = others(part, "dp")
    near, far = list(range(shares - 1)), [shares - 1]
    partial = call(
        functools.partial(project_kernel, near, True, False),
        [VMEM] * (len(near) + 1),
        [pltpu.VMEM((2 * memory, cols), f32), pltpu.VMEM((memory, HD), f32)],
        [],
        COVER,
        4 * D * cols,
    )(*[hidden[k] for k in near], kv_weight)
    kv = call(
        functools.partial(project_kernel, far, False, True),
        [VMEM] * 5,
        pltpu.VMEM((2 * memory, cols), bf16),
        [],
        4 * memory * D * cols // shares,
        4 * D * cols // shares,
    )(hidden[far[0]], kv_weight, *partial, kv_bias)
    kvs = others(kv, "dp")
    prepared = call(
        functools.partial(prepare_kernel, cols // HD),
        [VMEM] * (groups + 1),
        [
            pltpu.VMEM((groups * rows, cols), bf16),
            pltpu.VMEM((groups * rows, every), f32),
            pltpu.VMEM((groups * rows, HD), f32),
            pltpu.VMEM((groups * rows, HD), f32),
        ],
        [],
        PCOVER,
        0,
    )(*parts, memory_sections.reshape(1, every))

    out_rows, out_cols = groups * tokens, out_weight.shape[1]
    share = out_rows // shares
    held = bf16 if memory % 16 == 0 else f32
    pieces = call(
        functools.partial(attend_kernel, groups, shares),
        [VMEM] * (groups + 5),
        [pltpu.VMEM((share, out_cols), f32 if k == 0 else bf16) for k in range(shares)],
        [
            pltpu.VMEM((every, cols), held),
            pltpu.VMEM((every, cols), held),
            pltpu.VMEM((out_rows, out_weight.shape[0]), f32),
            pltpu.VMEM((out_rows, out_cols), f32),
        ],
        2 * out_rows * out_weight.size,
        2 * out_weight.size,
    )(*kvs, *prepared, out_weight)
    summed = pieces[0]
    for bits in range(1, shares):
        summed = summed + permute(pieces[bits], "tp", bits).astype(f32)
    return summed.astype(bf16)


def solution(mesh):
    return jax.shard_map(
        body,
        mesh=mesh,
        in_specs=(
            P(("parts", "dp"), "tp"),
            P(None, None, "tp"),
            P(None, "tp"),
            P("parts"),
            P(("parts", "dp")),
            P(("parts", "dp"), "tp"),
            P(("parts", "dp"), "tp"),
            P(("parts", "dp"), "tp"),
            P(("parts", "dp"), None, "tp"),
            P(("parts", "dp"), None, "tp"),
            P(("parts", "dp")),
            P("tp", "dp"),
        ),
        out_specs=P(("parts", "tp"), "dp"),
        check_vma=False,
    )
```

```python
import functools

import jax
import jax.numpy as jnp
from jax import lax
from jax.experimental import pallas as pl
from jax.experimental.pallas import tpu as pltpu
from jax.sharding import PartitionSpec as P

D = 5120
HQ = 40
KVH = 8
HD = 128
NEW = 2
PER_HEAD = HQ // KVH
INV = 1.0 / HD**0.5

masked_score = -1e30
bf16 = jnp.bfloat16
COVER = 1 << 36
PCOVER = 1 << 30
f32 = jnp.float32

TOP, TOTAL, SECTION = 0, 3, 5
STATS = 16


def nt(a, b):
    return lax.dot_general(a, b, (((1,), (1,)), ((), ())), preferred_element_type=f32)


def nn(a, b):
    return jnp.dot(a, b, preferred_element_type=f32)


def spread(blocks):
    zeros = jnp.zeros_like(blocks[0])
    rows = [
        jnp.concatenate([b if i == j else zeros for i in range(len(blocks))], axis=1)
        if len(blocks) > 1
        else b
        for j, b in enumerate(blocks)
    ]
    return jnp.concatenate(rows, axis=0)


def split(x, pieces):
    out = []
    for _ in range(pieces):
        piece = x.astype(bf16).astype(f32)
        out.append(piece)
        x = x - piece
    return out


def eye(rows, cols):
    row = lax.broadcasted_iota(jnp.int32, (rows, cols), 0)
    return (row == lax.broadcasted_iota(jnp.int32, (rows, cols), 1)).astype(f32).astype(bf16)


def up(n, to):
    return -(-n // to) * to


def cache_kernel(lens_ref, group_ref, q_ref, nk_ref, nv_ref, ck_ref, cv_ref, after, out_ref):
    requests, slots, cols = ck_ref.shape
    heads = cols // HD
    tokens = requests * NEW
    per = PER_HEAD * tokens
    rows = heads * per
    row = lax.broadcasted_iota(jnp.int32, (rows, 1), 0)
    request = lax.rem(lax.div(row, NEW), requests)
    token = lax.rem(row, NEW)
    q = q_ref[...].astype(f32)
    blocks = []
    for j in range(heads):
        parts = [q[:, (j * PER_HEAD + g) * HD : (j * PER_HEAD + g + 1) * HD] for g in range(PER_HEAD)]
        blocks.append(jnp.concatenate(parts, axis=0))
    out_ref[0:rows, :] = jnp.concatenate(blocks, axis=0).astype(bf16)
    qs = spread(blocks).astype(bf16)
    fresh = lax.broadcasted_iota(jnp.int32, (rows, tokens), 1)
    seen = (lax.div(fresh, NEW) == request) & (lax.rem(fresh, NEW) <= token)
    s_new = jnp.where(seen, nt(qs, nk_ref[...]) * INV, masked_score)
    limit = jnp.full((rows, 1), lens_ref[0], jnp.int32)
    for r in range(1, requests):
        limit = jnp.where(request == r, lens_ref[r], limit)
    live = lax.broadcasted_iota(jnp.int32, (rows, slots), 1) < limit
    s = nt(qs, ck_ref[0])
    for r in range(1, requests):
        s = jnp.where(request == r, nt(qs, ck_ref[r]), s)
    s = jnp.where(live, s * INV, masked_score)

    top = jnp.maximum(jnp.max(s, axis=1, keepdims=True), jnp.max(s_new, axis=1, keepdims=True))
    p = jnp.where(live, jnp.exp(s - top), 0.0)
    p_new = jnp.where(seen, jnp.exp(s_new - top), 0.0)
    total = jnp.sum(p, axis=1, keepdims=True) + jnp.sum(p_new, axis=1, keepdims=True)
    p = p.astype(bf16)
    acc = nn(p, cv_ref[0])
    for r in range(1, requests):
        acc = jnp.where(request == r, nn(p, cv_ref[r]), acc)
    acc = acc + nn(p_new.astype(bf16).astype(f32), nv_ref[...].astype(f32))
    mine = jnp.concatenate([acc[j * per : (j + 1) * per, j * HD : (j + 1) * HD] for j in range(heads)], axis=0)
    seg = up(rows, 16)
    out_ref[seg : seg + rows, :] = (mine / total).astype(bf16)

    lane = lax.broadcasted_iota(jnp.int32, (rows, HD), 1)
    stats = jnp.where(lane == SECTION, group_ref[0].astype(f32), 0.0)
    for i, piece in enumerate(split(top, 3)):
        stats = jnp.where(lane == TOP + i, piece, stats)
    for i, piece in enumerate(split(total, 2)):
        stats = jnp.where(lane == TOTAL + i, piece, stats)
    if rows < HD:
        stats = jnp.concatenate([stats, jnp.zeros((HD - rows, HD), f32)], axis=0)
    out_ref[2 * seg : 2 * seg + STATS, :] = nt(eye(STATS, HD), stats.astype(bf16)).astype(bf16)


def project_kernel(bits, first, last, *refs):
    count = len(bits)
    pieces, w_ref, refs = refs[:count], refs[count], refs[count + 1 :]
    rows, depth = pieces[0].shape
    me = lax.axis_index("tp")
    if first:
        acc, squares = [None, None], None
    else:
        acc = [refs[0][s * rows : (s + 1) * rows, :] for s in range(2)]
        squares = refs[1][:, 0:1]
        refs = refs[2:]
    for k, piece in zip(bits, pieces):
        h = piece[...]
        wide = h.astype(f32)
        square = jnp.sum(wide * wide, axis=1, keepdims=True)
        squares = square if squares is None else squares + square
        at = pl.multiple_of((me ^ k) * depth, depth)
        for s in range(2):
            term = nn(h, w_ref[s, pl.ds(at, depth), :])
            acc[s] = term if acc[s] is None else acc[s] + term
    if not last:
        for s in range(2):
            refs[0][s * rows : (s + 1) * rows, :] = acc[s]
        refs[1][...] = jnp.broadcast_to(squares, refs[1].shape)
        return
    b_ref, out_ref = refs
    scale = lax.rsqrt(squares / D + 1e-06)
    for s in range(2):
        bias = b_ref[s : s + 1, :].astype(f32)
        out_ref[s * rows : (s + 1) * rows, :] = (acc[s] * scale + bias).astype(bf16)


def prepare_kernel(heads, *refs):
    parts, (section_ref, q_ref, bias_ref, old_ref, stats_ref) = refs[:-5], refs[-5:]
    groups = len(parts)
    seg = (parts[0].shape[0] - STATS) // 2
    rows = q_ref.shape[0] // groups
    per = rows // heads
    blocks = [part[0:rows, :].astype(f32) for part in parts]
    q_ref[...] = jnp.concatenate(
        [spread([b[j * per : (j + 1) * per, :] for j in range(heads)]) for b in blocks], axis=0
    ).astype(bf16)
    stats = nt(
        eye(rows, HD), jnp.concatenate([part[2 * seg : 2 * seg + STATS, :] for part in parts], axis=0)
    )

    def column(at, pieces):
        columns = []
        for k in range(groups):
            c = k * STATS + at
            columns.append(sum([stats[:, c + i : c + i + 1] for i in range(pieces)]))
        return jnp.concatenate(columns, axis=0)

    top, total = column(TOP, 3), column(TOTAL, 2)
    bias_ref[...] = jnp.where(column(SECTION, 1) == section_ref[...].astype(f32), 0.0, masked_score)
    old = jnp.concatenate([part[seg : seg + rows, :] for part in parts], axis=0).astype(f32)
    old_ref[...] = old * total
    lane = lax.broadcasted_iota(jnp.int32, stats_ref.shape, 1)
    stats_ref[...] = jnp.where(lane == 0, top, total)


def attend_kernel(groups, shares, *refs):
    kvs, (q_ref, bias_ref, old_ref, stats_ref, w_ref) = refs[:groups], refs[groups : groups + 5]
    outs = refs[groups + 5 : groups + 5 + shares]
    k_ref, v_ref, attended_ref, sums_ref = refs[groups + 5 + shares :]
    me_dp, me_tp = lax.axis_index("dp"), lax.axis_index("tp")
    memory = kvs[0].shape[0] // 2
    heads = kvs[0].shape[1] // HD
    tokens = attended_ref.shape[0] // groups
    per = PER_HEAD * tokens
    rows = heads * per
    for bits, kv in zip(relatives(groups), kvs):
        first = pl.multiple_of((me_dp ^ bits) * memory, memory)
        k_ref[pl.ds(first, memory), :] = kv[0:memory, :].astype(k_ref.dtype)
        v_ref[pl.ds(first, memory), :] = kv[memory : 2 * memory, :].astype(v_ref.dtype)
    s = nt(q_ref[...], k_ref[...].astype(bf16)) * INV + bias_ref[...]
    old_top, old_total = stats_ref[:, 0:1], stats_ref[:, 1:2]
    top = jnp.maximum(jnp.max(s, axis=1, keepdims=True), old_top)
    p = jnp.exp(s - top)
    shrink = jnp.exp(old_top - top)
    total = jnp.sum(p, axis=1, keepdims=True) + shrink * old_total
    acc = nn(p.astype(bf16), v_ref[...].astype(bf16))
    for k, bits in enumerate(relatives(groups)):
        at = pl.multiple_of((me_dp ^ bits) * tokens, tokens)
        for j in range(heads):
            a = k * rows + j * per
            block = acc[a : a + per, j * HD : (j + 1) * HD] + old_ref[a : a + per, :] * shrink[a : a + per]
            block = block / total[a : a + per]
            for g in range(PER_HEAD):
                c = (j * PER_HEAD + g) * HD
                attended_ref[pl.ds(at, tokens), c : c + HD] = block[g * tokens : (g + 1) * tokens, :]
    sums_ref[...] = nn(attended_ref[...].astype(bf16), w_ref[...])
    share = sums_ref.shape[0] // shares
    for k, out in enumerate(outs):
        at = pl.multiple_of((me_tp ^ k) * share, share)
        out[...] = sums_ref[pl.ds(at, share), :].astype(out.dtype)


SMEM = pl.BlockSpec(memory_space=pltpu.SMEM)
VMEM = pl.BlockSpec(memory_space=pltpu.VMEM)
ANY = pl.BlockSpec(memory_space=pl.ANY)
HBM = pl.BlockSpec(memory_space=pltpu.HBM)
PARAMS = pltpu.CompilerParams(vmem_limit_bytes=24 * 1024 * 1024)


def call(kernel, in_specs, out_shape, scratch, flops, bytes_accessed):
    return pl.pallas_call(
        kernel,
        in_specs=in_specs,
        out_shape=out_shape,
        out_specs=jax.tree.map(lambda _: VMEM, out_shape),
        scratch_shapes=scratch,
        compiler_params=PARAMS,
        cost_estimate=pl.CostEstimate(flops=flops, bytes_accessed=bytes_accessed, transcendentals=0),
    )


def in_hbm(*arrays):
    return [pltpu.with_memory_space_constraint(x, pltpu.HBM) for x in arrays]


def relatives(n):
    return [*range(n // 2), *range(n - 1, n // 2 - 1, -1)]


def permute(x, axis, bits):
    return lax.ppermute(x, axis, [(i, i ^ bits) for i in range(lax.axis_size(axis))])


def others(x, axis):
    return [permute(x, axis, bits) if bits else x for bits in relatives(lax.axis_size(axis))]


def passed_on(x, axis):
    n = lax.axis_size(axis)
    held = {0: x}
    bit = n // 2
    while bit:
        for bits in sorted(held):
            held[bits | bit] = permute(held[bits], axis, bit)
        bit //= 2
    return [held[bits] for bits in range(n)]


def body(
    memory_hidden,
    kv_weight,
    kv_bias,
    memory_sections,
    group_sections,
    queries,
    new_keys,
    new_values,
    cache_keys,
    cache_values,
    cache_lengths,
    out_weight,
):
    groups, shares = lax.axis_size("dp"), lax.axis_size("tp")
    memory, depth = memory_hidden.shape
    requests, slots, cols = cache_keys.shape
    tokens = requests * NEW
    rows = (cols // HD) * PER_HEAD * tokens
    every = memory_sections.shape[0]

    gate = call(lambda *refs: None, [], jax.ShapeDtypeStruct((8, HD), f32), [], COVER, 0)()
    own, gate = lax.optimization_barrier((memory_hidden, gate))
    hidden = passed_on(own, "tp")
    part = call(
        cache_kernel,
        [SMEM] * 2 + [VMEM] * 5 + [ANY],
        pltpu.VMEM((2 * up(rows, 16) + STATS, HD), bf16),
        [],
        4 * rows * slots * cols * requests,
        4 * requests * slots * cols,
    )(cache_lengths, group_sections, queries, new_keys, new_values, cache_keys, cache_values, gate)
    parts = others(part, "dp")
    near, far = list(range(shares - 1)), [shares - 1]
    partial = call(
        functools.partial(project_kernel, near, True, False),
        [VMEM] * (len(near) + 1),
        [pltpu.VMEM((2 * memory, cols), f32), pltpu.VMEM((memory, HD), f32)],
        [],
        COVER,
        4 * D * cols,
    )(*[hidden[k] for k in near], kv_weight)
    kv = call(
        functools.partial(project_kernel, far, False, True),
        [VMEM] * 5,
        pltpu.VMEM((2 * memory, cols), bf16),
        [],
        4 * memory * D * cols // shares,
        4 * D * cols // shares,
    )(hidden[far[0]], kv_weight, *partial, kv_bias)
    kvs = others(kv, "dp")
    prepared = call(
        functools.partial(prepare_kernel, cols // HD),
        [VMEM] * (groups + 1),
        [
            pltpu.VMEM((groups * rows, cols), bf16),
            pltpu.VMEM((groups * rows, every), f32),
            pltpu.VMEM((groups * rows, HD), f32),
            pltpu.VMEM((groups * rows, HD), f32),
        ],
        [],
        PCOVER,
        0,
    )(*parts, memory_sections.reshape(1, every))

    out_rows, out_cols = groups * tokens, out_weight.shape[1]
    share = out_rows // shares
    held = bf16 if memory % 16 == 0 else f32
    pieces = call(
        functools.partial(attend_kernel, groups, shares),
        [VMEM] * (groups + 5),
        [pltpu.VMEM((share, out_cols), f32 if k == 0 else bf16) for k in range(shares)],
        [
            pltpu.VMEM((every, cols), held),
            pltpu.VMEM((every, cols), held),
            pltpu.VMEM((out_rows, out_weight.shape[0]), f32),
            pltpu.VMEM((out_rows, out_cols), f32),
        ],
        2 * out_rows * out_weight.size,
        2 * out_weight.size,
    )(*kvs, *prepared, out_weight)
    summed = pieces[0]
    for bits in range(shares - 1, 0, -1):
        summed = summed + permute(pieces[bits], "tp", bits).astype(f32)
    return summed.astype(bf16)


def solution(mesh):
    return jax.shard_map(
        body,
        mesh=mesh,
        in_specs=(
            P(("parts", "dp"), "tp"),
            P(None, None, "tp"),
            P(None, "tp"),
            P("parts"),
            P(("parts", "dp")),
            P(("parts", "dp"), "tp"),
            P(("parts", "dp"), "tp"),
            P(("parts", "dp"), "tp"),
            P(("parts", "dp"), None, "tp"),
            P(("parts", "dp"), None, "tp"),
            P(("parts", "dp")),
            P("tp", "dp"),
        ),
        out_specs=P(("parts", "tp"), "dp"),
        check_vma=False,
    )
```

```python
import functools

import jax
import jax.numpy as jnp
from jax import lax
from jax.experimental import pallas as pl
from jax.experimental.pallas import tpu as pltpu
from jax.sharding import PartitionSpec as P

D = 5120
HQ = 40
KVH = 8
HD = 128
NEW = 2
PER_HEAD = HQ // KVH
INV = 1.0 / HD**0.5

masked_score = -1e30
bf16 = jnp.bfloat16
COVER = 1 << 36
PCOVER = 1 << 10
f32 = jnp.float32

TOP, TOTAL, SECTION = 0, 3, 5
STATS = 16


def nt(a, b):
    return lax.dot_general(a, b, (((1,), (1,)), ((), ())), preferred_element_type=f32)


def nn(a, b):
    return jnp.dot(a, b, preferred_element_type=f32)


def spread(blocks):
    zeros = jnp.zeros_like(blocks[0])
    rows = [
        jnp.concatenate([b if i == j else zeros for i in range(len(blocks))], axis=1)
        if len(blocks) > 1
        else b
        for j, b in enumerate(blocks)
    ]
    return jnp.concatenate(rows, axis=0)


def split(x, pieces):
    out = []
    for _ in range(pieces):
        piece = x.astype(bf16).astype(f32)
        out.append(piece)
        x = x - piece
    return out


def eye(rows, cols):
    row = lax.broadcasted_iota(jnp.int32, (rows, cols), 0)
    return (row == lax.broadcasted_iota(jnp.int32, (rows, cols), 1)).astype(f32).astype(bf16)


def up(n, to):
    return -(-n // to) * to


def open_kernel(group_ref, after, out_ref):
    out_ref[...] = jnp.full(out_ref.shape, group_ref[0].astype(f32))


def cache_kernel(lens_ref, section_ref, q_ref, nk_ref, nv_ref, ck_ref, cv_ref, out_ref):
    requests, slots, cols = ck_ref.shape
    heads = cols // HD
    tokens = requests * NEW
    per = PER_HEAD * tokens
    rows = heads * per
    row = lax.broadcasted_iota(jnp.int32, (rows, 1), 0)
    request = lax.rem(lax.div(row, NEW), requests)
    token = lax.rem(row, NEW)
    q = q_ref[...].astype(f32)
    blocks = []
    for j in range(heads):
        parts = [q[:, (j * PER_HEAD + g) * HD : (j * PER_HEAD + g + 1) * HD] for g in range(PER_HEAD)]
        blocks.append(jnp.concatenate(parts, axis=0))
    out_ref[0:rows, :] = jnp.concatenate(blocks, axis=0).astype(bf16)
    qs = spread(blocks).astype(bf16)
    fresh = lax.broadcasted_iota(jnp.int32, (rows, tokens), 1)
    seen = (lax.div(fresh, NEW) == request) & (lax.rem(fresh, NEW) <= token)
    s_new = jnp.where(seen, nt(qs, nk_ref[...]) * INV, masked_score)
    limit = jnp.full((rows, 1), lens_ref[0], jnp.int32)
    for r in range(1, requests):
        limit = jnp.where(request == r, lens_ref[r], limit)
    live = lax.broadcasted_iota(jnp.int32, (rows, slots), 1) < limit
    s = nt(qs, ck_ref[0])
    for r in range(1, requests):
        s = jnp.where(request == r, nt(qs, ck_ref[r]), s)
    s = jnp.where(live, s * INV, masked_score)

    top = jnp.maximum(jnp.max(s, axis=1, keepdims=True), jnp.max(s_new, axis=1, keepdims=True))
    p = jnp.where(live, jnp.exp(s - top), 0.0)
    p_new = jnp.where(seen, jnp.exp(s_new - top), 0.0)
    total = jnp.sum(p, axis=1, keepdims=True) + jnp.sum(p_new, axis=1, keepdims=True)
    p = p.astype(bf16)
    acc = nn(p, cv_ref[0])
    for r in range(1, requests):
        acc = jnp.where(request == r, nn(p, cv_ref[r]), acc)
    acc = acc + nn(p_new.astype(bf16).astype(f32), nv_ref[...].astype(f32))
    mine = jnp.concatenate([acc[j * per : (j + 1) * per, j * HD : (j + 1) * HD] for j in range(heads)], axis=0)
    seg = up(rows, 16)
    out_ref[seg : seg + rows, :] = (mine / total).astype(bf16)

    lane = lax.broadcasted_iota(jnp.int32, (rows, HD), 1)
    stats = jnp.where(lane == SECTION, section_ref[0:1, :], 0.0)
    for i, piece in enumerate(split(top, 3)):
        stats = jnp.where(lane == TOP + i, piece, stats)
    for i, piece in enumerate(split(total, 2)):
        stats = jnp.where(lane == TOTAL + i, piece, stats)
    if rows < HD:
        stats = jnp.concatenate([stats, jnp.zeros((HD - rows, HD), f32)], axis=0)
    out_ref[2 * seg : 2 * seg + STATS, :] = nt(eye(STATS, HD), stats.astype(bf16)).astype(bf16)


def project_kernel(bits, first, last, *refs):
    count = len(bits)
    pieces, w_ref, refs = refs[:count], refs[count], refs[count + 1 :]
    rows, depth = pieces[0].shape
    me = lax.axis_index("tp")
    if first:
        acc, squares = [None, None], None
    else:
        acc = [refs[0][s * rows : (s + 1) * rows, :] for s in range(2)]
        squares = refs[1][:, 0:1]
        refs = refs[2:]
    for k, piece in zip(bits, pieces):
        h = piece[...]
        wide = h.astype(f32)
        square = jnp.sum(wide * wide, axis=1, keepdims=True)
        squares = square if squares is None else squares + square
        at = pl.multiple_of((me ^ k) * depth, depth)
        for s in range(2):
            term = nn(h, w_ref[s, pl.ds(at, depth), :])
            acc[s] = term if acc[s] is None else acc[s] + term
    if not last:
        for s in range(2):
            refs[0][s * rows : (s + 1) * rows, :] = acc[s]
        refs[1][...] = jnp.broadcast_to(squares, refs[1].shape)
        return
    b_ref, out_ref = refs
    scale = lax.rsqrt(squares / D + 1e-06)
    for s in range(2):
        bias = b_ref[s : s + 1, :].astype(f32)
        out_ref[s * rows : (s + 1) * rows, :] = (acc[s] * scale + bias).astype(bf16)


def prepare_kernel(heads, *refs):
    parts, (section_ref, q_ref, bias_ref, old_ref, stats_ref) = refs[:-5], refs[-5:]
    groups = len(parts)
    seg = (parts[0].shape[0] - STATS) // 2
    rows = q_ref.shape[0] // groups
    per = rows // heads
    blocks = [part[0:rows, :].astype(f32) for part in parts]
    q_ref[...] = jnp.concatenate(
        [spread([b[j * per : (j + 1) * per, :] for j in range(heads)]) for b in blocks], axis=0
    ).astype(bf16)
    stats = nt(
        eye(rows, HD), jnp.concatenate([part[2 * seg : 2 * seg + STATS, :] for part in parts], axis=0)
    )

    def column(at, pieces):
        columns = []
        for k in range(groups):
            c = k * STATS + at
            columns.append(sum([stats[:, c + i : c + i + 1] for i in range(pieces)]))
        return jnp.concatenate(columns, axis=0)

    top, total = column(TOP, 3), column(TOTAL, 2)
    bias_ref[...] = jnp.where(column(SECTION, 1) == section_ref[...].astype(f32), 0.0, masked_score)
    old = jnp.concatenate([part[seg : seg + rows, :] for part in parts], axis=0).astype(f32)
    old_ref[...] = old * total
    lane = lax.broadcasted_iota(jnp.int32, stats_ref.shape, 1)
    stats_ref[...] = jnp.where(lane == 0, top, total)


def attend_kernel(groups, shares, *refs):
    kvs, (q_ref, bias_ref, old_ref, stats_ref, w_ref) = refs[:groups], refs[groups : groups + 5]
    outs = refs[groups + 5 : groups + 5 + shares]
    k_ref, v_ref, attended_ref, sums_ref = refs[groups + 5 + shares :]
    me_dp, me_tp = lax.axis_index("dp"), lax.axis_index("tp")
    memory = kvs[0].shape[0] // 2
    heads = kvs[0].shape[1] // HD
    tokens = attended_ref.shape[0] // groups
    per = PER_HEAD * tokens
    rows = heads * per
    for bits, kv in zip(relatives(groups), kvs):
        first = pl.multiple_of((me_dp ^ bits) * memory, memory)
        k_ref[pl.ds(first, memory), :] = kv[0:memory, :].astype(k_ref.dtype)
        v_ref[pl.ds(first, memory), :] = kv[memory : 2 * memory, :].astype(v_ref.dtype)
    s = nt(q_ref[...], k_ref[...].astype(bf16)) * INV + bias_ref[...]
    old_top, old_total = stats_ref[:, 0:1], stats_ref[:, 1:2]
    top = jnp.maximum(jnp.max(s, axis=1, keepdims=True), old_top)
    p = jnp.exp(s - top)
    shrink = jnp.exp(old_top - top)
    total = jnp.sum(p, axis=1, keepdims=True) + shrink * old_total
    acc = nn(p.astype(bf16), v_ref[...].astype(bf16))
    for k, bits in enumerate(relatives(groups)):
        at = pl.multiple_of((me_dp ^ bits) * tokens, tokens)
        for j in range(heads):
            a = k * rows + j * per
            block = acc[a : a + per, j * HD : (j + 1) * HD] + old_ref[a : a + per, :] * shrink[a : a + per]
            block = block / total[a : a + per]
            for g in range(PER_HEAD):
                c = (j * PER_HEAD + g) * HD
                attended_ref[pl.ds(at, tokens), c : c + HD] = block[g * tokens : (g + 1) * tokens, :]
    sums_ref[...] = nn(attended_ref[...].astype(bf16), w_ref[...])
    share = sums_ref.shape[0] // shares
    for k, out in enumerate(outs):
        at = pl.multiple_of((me_tp ^ k) * share, share)
        out[...] = sums_ref[pl.ds(at, share), :].astype(out.dtype)


SMEM = pl.BlockSpec(memory_space=pltpu.SMEM)
VMEM = pl.BlockSpec(memory_space=pltpu.VMEM)
ANY = pl.BlockSpec(memory_space=pl.ANY)
HBM = pl.BlockSpec(memory_space=pltpu.HBM)
PARAMS = pltpu.CompilerParams(vmem_limit_bytes=24 * 1024 * 1024)


def call(kernel, in_specs, out_shape, scratch, flops, bytes_accessed, aliases={}):
    return pl.pallas_call(
        kernel,
        in_specs=in_specs,
        out_shape=out_shape,
        out_specs=jax.tree.map(lambda _: VMEM, out_shape),
        scratch_shapes=scratch,
        input_output_aliases=aliases,
        compiler_params=PARAMS,
        cost_estimate=pl.CostEstimate(flops=flops, bytes_accessed=bytes_accessed, transcendentals=0),
    )


def in_hbm(*arrays):
    return [pltpu.with_memory_space_constraint(x, pltpu.HBM) for x in arrays]


def relatives(n):
    return [0, *range(n // 2, n), *range(1, n // 2)]


def permute(x, axis, bits):
    return lax.ppermute(x, axis, [(i, i ^ bits) for i in range(lax.axis_size(axis))])


def others(x, axis):
    return [permute(x, axis, bits) if bits else x for bits in relatives(lax.axis_size(axis))]


def passed_on(x, axis):
    n = lax.axis_size(axis)
    held = {0: x}
    bit = n // 2
    while bit:
        for bits in sorted(held):
            held[bits | bit] = permute(held[bits], axis, bit)
        bit //= 2
    return [held[bits] for bits in range(n)]


def body(
    memory_hidden,
    kv_weight,
    kv_bias,
    memory_sections,
    group_sections,
    queries,
    new_keys,
    new_values,
    cache_keys,
    cache_values,
    cache_lengths,
    out_weight,
):
    groups, shares = lax.axis_size("dp"), lax.axis_size("tp")
    memory, depth = memory_hidden.shape
    requests, slots, cols = cache_keys.shape
    tokens = requests * NEW
    rows = (cols // HD) * PER_HEAD * tokens
    every = memory_sections.shape[0]

    gate = call(lambda *refs: None, [], jax.ShapeDtypeStruct((8, HD), f32), [], COVER, 0)()
    group, gate = lax.optimization_barrier((group_sections, gate))
    section = call(open_kernel, [SMEM, ANY], pltpu.VMEM((8, HD), f32), [], 1 << 10, 0)(group, gate)
    own, section = lax.optimization_barrier((memory_hidden, section))
    hidden = passed_on(own, "tp")
    part = call(
        cache_kernel,
        [SMEM] + [VMEM] * 6,
        pltpu.VMEM((2 * up(rows, 16) + STATS, HD), bf16),
        [],
        4 * rows * slots * cols * requests,
        4 * requests * slots * cols,
    )(cache_lengths, section, queries, new_keys, new_values, cache_keys, cache_values)
    part_far = permute(part, "dp", groups // 2)
    part_near = {bits: permute(part, "dp", bits) for bits in range(1, groups // 2)}
    near, far = list(range(shares - 1)), [shares - 1]
    partial = call(
        functools.partial(project_kernel, near, True, False),
        [VMEM] * (len(near) + 1),
        [pltpu.VMEM((2 * memory, cols), f32), pltpu.VMEM((memory, HD), f32)],
        [],
        COVER,
        4 * D * cols,
    )(*[hidden[k] for k in near], kv_weight)
    kv = call(
        functools.partial(project_kernel, far, False, True),
        [VMEM] * 5,
        pltpu.VMEM((2 * memory, cols), bf16),
        [],
        4 * memory * D * cols // shares,
        4 * D * cols // shares,
    )(hidden[far[0]], kv_weight, *partial, kv_bias)
    kvs = others(kv, "dp")
    part_far = call(
        lambda x, after, out: None,
        [VMEM, ANY],
        pltpu.VMEM(part.shape, bf16),
        [],
        COVER,
        0,
        {0: 0},
    )(part_far, kv)
    parts = {0: part, **part_near}
    for bits in range(groups // 2):
        parts[groups // 2 + bits] = permute(part_far, "dp", bits) if bits else part_far
    parts = [parts[bits] for bits in relatives(groups)]
    prepared = call(
        functools.partial(prepare_kernel, cols // HD),
        [VMEM] * (groups + 1),
        [
            pltpu.VMEM((groups * rows, cols), bf16),
            pltpu.VMEM((groups * rows, every), f32),
            pltpu.VMEM((groups * rows, HD), f32),
            pltpu.VMEM((groups * rows, HD), f32),
        ],
        [],
        PCOVER,
        0,
    )(*parts, memory_sections.reshape(1, every))

    out_rows, out_cols = groups * tokens, out_weight.shape[1]
    share = out_rows // shares
    held = bf16 if memory % 16 == 0 else f32
    pieces = call(
        functools.partial(attend_kernel, groups, shares),
        [VMEM] * (groups + 5),
        [pltpu.VMEM((share, out_cols), f32 if k == 0 else bf16) for k in range(shares)],
        [
            pltpu.VMEM((every, cols), held),
            pltpu.VMEM((every, cols), held),
            pltpu.VMEM((out_rows, out_weight.shape[0]), f32),
            pltpu.VMEM((out_rows, out_cols), f32),
        ],
        2 * out_rows * out_weight.size,
        2 * out_weight.size,
    )(*kvs, *prepared, out_weight)
    summed = pieces[0]
    for bits in range(shares - 1, 0, -1):
        summed = summed + permute(pieces[bits], "tp", bits).astype(f32)
    return summed.astype(bf16)


def solution(mesh):
    return jax.shard_map(
        body,
        mesh=mesh,
        in_specs=(
            P(("parts", "dp"), "tp"),
            P(None, None, "tp"),
            P(None, "tp"),
            P("parts"),
            P(("parts", "dp")),
            P(("parts", "dp"), "tp"),
            P(("parts", "dp"), "tp"),
            P(("parts", "dp"), "tp"),
            P(("parts", "dp"), None, "tp"),
            P(("parts", "dp"), None, "tp"),
            P(("parts", "dp")),
            P("tp", "dp"),
        ),
        out_specs=P(("parts", "tp"), "dp"),
        check_vma=False,
    )
```

```python
import functools

import jax
import jax.numpy as jnp
from jax import lax
from jax.experimental import pallas as pl
from jax.experimental.pallas import tpu as pltpu
from jax.sharding import PartitionSpec as P

D = 5120
HQ = 40
KVH = 8
HD = 128
NEW = 2
PER_HEAD = HQ // KVH
INV = 1.0 / HD**0.5

masked_score = -1e30
bf16 = jnp.bfloat16
COVER = 1 << 36
PCOVER = 1 << 30
f32 = jnp.float32

TOP, TOTAL, SECTION = 0, 3, 5
STATS = 16


def nt(a, b):
    return lax.dot_general(a, b, (((1,), (1,)), ((), ())), preferred_element_type=f32)


def nn(a, b):
    return jnp.dot(a, b, preferred_element_type=f32)


def spread(blocks):
    zeros = jnp.zeros_like(blocks[0])
    rows = [
        jnp.concatenate([b if i == j else zeros for i in range(len(blocks))], axis=1)
        if len(blocks) > 1
        else b
        for j, b in enumerate(blocks)
    ]
    return jnp.concatenate(rows, axis=0)


def split(x, pieces):
    out = []
    for _ in range(pieces):
        piece = x.astype(bf16).astype(f32)
        out.append(piece)
        x = x - piece
    return out


def eye(rows, cols):
    row = lax.broadcasted_iota(jnp.int32, (rows, cols), 0)
    return (row == lax.broadcasted_iota(jnp.int32, (rows, cols), 1)).astype(f32).astype(bf16)


def up(n, to):
    return -(-n // to) * to


def open_kernel(group_ref, after, out_ref):
    out_ref[...] = jnp.full(out_ref.shape, group_ref[0].astype(f32))


def cache_kernel(lens_ref, section_ref, q_ref, nk_ref, nv_ref, ck_ref, cv_ref, out_ref):
    requests, slots, cols = ck_ref.shape
    heads = cols // HD
    tokens = requests * NEW
    per = PER_HEAD * tokens
    rows = heads * per
    row = lax.broadcasted_iota(jnp.int32, (rows, 1), 0)
    request = lax.rem(lax.div(row, NEW), requests)
    token = lax.rem(row, NEW)
    q = q_ref[...].astype(f32)
    blocks = []
    for j in range(heads):
        parts = [q[:, (j * PER_HEAD + g) * HD : (j * PER_HEAD + g + 1) * HD] for g in range(PER_HEAD)]
        blocks.append(jnp.concatenate(parts, axis=0))
    out_ref[0:rows, :] = jnp.concatenate(blocks, axis=0).astype(bf16)
    qs = spread(blocks).astype(bf16)
    fresh = lax.broadcasted_iota(jnp.int32, (rows, tokens), 1)
    seen = (lax.div(fresh, NEW) == request) & (lax.rem(fresh, NEW) <= token)
    s_new = jnp.where(seen, nt(qs, nk_ref[...]) * INV, masked_score)
    limit = jnp.full((rows, 1), lens_ref[0], jnp.int32)
    for r in range(1, requests):
        limit = jnp.where(request == r, lens_ref[r], limit)
    live = lax.broadcasted_iota(jnp.int32, (rows, slots), 1) < limit
    s = nt(qs, ck_ref[0])
    for r in range(1, requests):
        s = jnp.where(request == r, nt(qs, ck_ref[r]), s)
    s = jnp.where(live, s * INV, masked_score)

    top = jnp.maximum(jnp.max(s, axis=1, keepdims=True), jnp.max(s_new, axis=1, keepdims=True))
    p = jnp.where(live, jnp.exp(s - top), 0.0)
    p_new = jnp.where(seen, jnp.exp(s_new - top), 0.0)
    total = jnp.sum(p, axis=1, keepdims=True) + jnp.sum(p_new, axis=1, keepdims=True)
    p = p.astype(bf16)
    acc = nn(p, cv_ref[0])
    for r in range(1, requests):
        acc = jnp.where(request == r, nn(p, cv_ref[r]), acc)
    acc = acc + nn(p_new.astype(bf16).astype(f32), nv_ref[...].astype(f32))
    mine = jnp.concatenate([acc[j * per : (j + 1) * per, j * HD : (j + 1) * HD] for j in range(heads)], axis=0)
    seg = up(rows, 16)
    out_ref[seg : seg + rows, :] = (mine / total).astype(bf16)

    lane = lax.broadcasted_iota(jnp.int32, (rows, HD), 1)
    stats = jnp.where(lane == SECTION, section_ref[0:1, :], 0.0)
    for i, piece in enumerate(split(top, 3)):
        stats = jnp.where(lane == TOP + i, piece, stats)
    for i, piece in enumerate(split(total, 2)):
        stats = jnp.where(lane == TOTAL + i, piece, stats)
    if rows < HD:
        stats = jnp.concatenate([stats, jnp.zeros((HD - rows, HD), f32)], axis=0)
    out_ref[2 * seg : 2 * seg + STATS, :] = nt(eye(STATS, HD), stats.astype(bf16)).astype(bf16)


def project_kernel(bits, first, last, *refs):
    count = len(bits)
    pieces, w_ref, refs = refs[:count], refs[count], refs[count + 1 :]
    rows, depth = pieces[0].shape
    me = lax.axis_index("tp")
    if first:
        acc, squares = [None, None], None
    else:
        acc = [refs[0][s * rows : (s + 1) * rows, :] for s in range(2)]
        squares = refs[1][:, 0:1]
        refs = refs[2:]
    for k, piece in zip(bits, pieces):
        h = piece[...]
        wide = h.astype(f32)
        square = jnp.sum(wide * wide, axis=1, keepdims=True)
        squares = square if squares is None else squares + square
        at = pl.multiple_of((me ^ k) * depth, depth)
        for s in range(2):
            term = nn(h, w_ref[s, pl.ds(at, depth), :])
            acc[s] = term if acc[s] is None else acc[s] + term
    if not last:
        for s in range(2):
            refs[0][s * rows : (s + 1) * rows, :] = acc[s]
        refs[1][...] = jnp.broadcast_to(squares, refs[1].shape)
        return
    b_ref, *_, far_ref, out_ref, packed_ref = refs
    scale = lax.rsqrt(squares / D + 1e-06)
    for s in range(2):
        bias = b_ref[s : s + 1, :].astype(f32)
        out = (acc[s] * scale + bias).astype(bf16)
        out_ref[s * rows : (s + 1) * rows, :] = out
        packed_ref[s * rows : (s + 1) * rows, :] = out
    heads = packed_ref.shape[1] // HD
    folded = far_ref.shape[0] // heads
    for j in range(heads):
        packed_ref[2 * rows :, j * HD : (j + 1) * HD] = far_ref[j * folded : (j + 1) * folded, :]


def prepare_kernel(heads, *refs):
    parts, (section_ref, q_ref, bias_ref, old_ref, stats_ref) = list(refs[:-5]), refs[-5:]
    groups = len(parts)
    folded = parts[0].shape[0] // heads
    for k in range(groups // 2 + 1, groups):
        kv = parts[k]
        at = kv.shape[0] - folded
        parts[k] = jnp.concatenate([kv[at:, j * HD : (j + 1) * HD] for j in range(heads)], axis=0)
    rows = q_ref.shape[0] // groups
    seg = up(rows, 16)
    per = rows // heads
    blocks = [part[0:rows, :].astype(f32) for part in parts]
    q_ref[...] = jnp.concatenate(
        [spread([b[j * per : (j + 1) * per, :] for j in range(heads)]) for b in blocks], axis=0
    ).astype(bf16)
    stats = nt(
        eye(rows, HD), jnp.concatenate([part[2 * seg : 2 * seg + STATS, :] for part in parts], axis=0)
    )

    def column(at, pieces):
        columns = []
        for k in range(groups):
            c = k * STATS + at
            columns.append(sum([stats[:, c + i : c + i + 1] for i in range(pieces)]))
        return jnp.concatenate(columns, axis=0)

    top, total = column(TOP, 3), column(TOTAL, 2)
    bias_ref[...] = jnp.where(column(SECTION, 1) == section_ref[...].astype(f32), 0.0, masked_score)
    old = jnp.concatenate([part[seg : seg + rows, :] for part in parts], axis=0).astype(f32)
    old_ref[...] = old * total
    lane = lax.broadcasted_iota(jnp.int32, stats_ref.shape, 1)
    stats_ref[...] = jnp.where(lane == 0, top, total)


def attend_kernel(groups, shares, *refs):
    kvs, (q_ref, bias_ref, old_ref, stats_ref, w_ref) = refs[:groups], refs[groups : groups + 5]
    outs = refs[groups + 5 : groups + 5 + shares]
    k_ref, v_ref, attended_ref, sums_ref = refs[groups + 5 + shares :]
    me_dp, me_tp = lax.axis_index("dp"), lax.axis_index("tp")
    memory = k_ref.shape[0] // groups
    heads = kvs[0].shape[1] // HD
    tokens = attended_ref.shape[0] // groups
    per = PER_HEAD * tokens
    rows = heads * per
    for bits, kv in enumerate(kvs):
        first = pl.multiple_of((me_dp ^ bits) * memory, memory)
        k_ref[pl.ds(first, memory), :] = kv[0:memory, :].astype(k_ref.dtype)
        v_ref[pl.ds(first, memory), :] = kv[memory : 2 * memory, :].astype(v_ref.dtype)
    s = nt(q_ref[...], k_ref[...].astype(bf16)) * INV + bias_ref[...]
    old_top, old_total = stats_ref[:, 0:1], stats_ref[:, 1:2]
    top = jnp.maximum(jnp.max(s, axis=1, keepdims=True), old_top)
    p = jnp.exp(s - top)
    shrink = jnp.exp(old_top - top)
    total = jnp.sum(p, axis=1, keepdims=True) + shrink * old_total
    acc = nn(p.astype(bf16), v_ref[...].astype(bf16))
    for k in range(groups):
        at = pl.multiple_of((me_dp ^ k) * tokens, tokens)
        for j in range(heads):
            a = k * rows + j * per
            block = acc[a : a + per, j * HD : (j + 1) * HD] + old_ref[a : a + per, :] * shrink[a : a + per]
            block = block / total[a : a + per]
            for g in range(PER_HEAD):
                c = (j * PER_HEAD + g) * HD
                attended_ref[pl.ds(at, tokens), c : c + HD] = block[g * tokens : (g + 1) * tokens, :]
    sums_ref[...] = nn(attended_ref[...].astype(bf16), w_ref[...])
    share = sums_ref.shape[0] // shares
    for k, out in enumerate(outs):
        at = pl.multiple_of((me_tp ^ k) * share, share)
        out[...] = sums_ref[pl.ds(at, share), :].astype(out.dtype)


SMEM = pl.BlockSpec(memory_space=pltpu.SMEM)
VMEM = pl.BlockSpec(memory_space=pltpu.VMEM)
ANY = pl.BlockSpec(memory_space=pl.ANY)
HBM = pl.BlockSpec(memory_space=pltpu.HBM)
PARAMS = pltpu.CompilerParams(vmem_limit_bytes=24 * 1024 * 1024)


def call(kernel, in_specs, out_shape, scratch, flops, bytes_accessed):
    return pl.pallas_call(
        kernel,
        in_specs=in_specs,
        out_shape=out_shape,
        out_specs=jax.tree.map(lambda _: VMEM, out_shape),
        scratch_shapes=scratch,
        compiler_params=PARAMS,
        cost_estimate=pl.CostEstimate(flops=flops, bytes_accessed=bytes_accessed, transcendentals=0),
    )


def in_hbm(*arrays):
    return [pltpu.with_memory_space_constraint(x, pltpu.HBM) for x in arrays]


def permute(x, axis, bits):
    return lax.ppermute(x, axis, [(i, i ^ bits) for i in range(lax.axis_size(axis))])


def passed_on(x, near, axis):
    n = lax.axis_size(axis)
    held = {0: x}
    bit = n // 2
    while bit:
        for bits in sorted(held):
            held[bits | bit] = permute(held[bits], axis, bit)
        held[0] = near
        bit //= 2
    return [held[bits] for bits in range(n)]


def body(
    memory_hidden,
    kv_weight,
    kv_bias,
    memory_sections,
    group_sections,
    queries,
    new_keys,
    new_values,
    cache_keys,
    cache_values,
    cache_lengths,
    out_weight,
):
    groups, shares = lax.axis_size("dp"), lax.axis_size("tp")
    memory, depth = memory_hidden.shape
    requests, slots, cols = cache_keys.shape
    tokens = requests * NEW
    rows = (cols // HD) * PER_HEAD * tokens
    every = memory_sections.shape[0]

    gate = call(lambda *refs: None, [], jax.ShapeDtypeStruct((8, HD), f32), [], COVER, 0)()
    group, gate = lax.optimization_barrier((group_sections, gate))
    section = call(open_kernel, [SMEM, ANY], pltpu.VMEM((8, HD), f32), [], 1 << 10, 0)(group, gate)
    own, section = lax.optimization_barrier((memory_hidden, section))
    heads = cols // HD
    height = up(2 * up(rows, 16) + STATS, 16 * heads)
    part = call(
        cache_kernel,
        [SMEM] + [VMEM] * 6,
        pltpu.VMEM((height, HD), bf16),
        [],
        4 * rows * slots * cols * requests,
        4 * requests * slots * cols,
    )(cache_lengths, section, queries, new_keys, new_values, cache_keys, cache_values)
    own_later, part = lax.optimization_barrier((own, part))
    hidden = passed_on(own, own_later, "tp")
    part_far = permute(part, "dp", groups // 2)
    part_near = {bits: permute(part, "dp", bits) for bits in range(1, groups // 2)}
    near, far = list(range(shares - 1)), [shares - 1]
    partial = call(
        functools.partial(project_kernel, near, True, False),
        [VMEM] * (len(near) + 1),
        [pltpu.VMEM((2 * memory, cols), f32), pltpu.VMEM((memory, HD), f32)],
        [],
        COVER,
        4 * D * cols,
    )(*[hidden[k] for k in near], kv_weight)
    kv, packed = call(
        functools.partial(project_kernel, far, False, True),
        [VMEM] * 5 + [ANY] * len(part_near) + [VMEM],
        [
            pltpu.VMEM((2 * memory, cols), bf16),
            pltpu.VMEM((2 * memory + height // heads, cols), bf16),
        ],
        [],
        4 * memory * D * cols // shares,
        4 * D * cols // shares,
    )(hidden[far[0]], kv_weight, *partial, kv_bias, *part_near.values(), part_far)
    half = range(1, groups // 2)
    near_kvs = [permute(packed, "dp", bits) for bits in half]
    kvs = [kv, *near_kvs, *[permute(kv, "dp", groups // 2 + bits) for bits in range(groups // 2)]]
    parts = [part, *[part_near[bits] for bits in half], part_far, *near_kvs]
    prepared = call(
        functools.partial(prepare_kernel, heads),
        [VMEM] * (groups + 1),
        [
            pltpu.VMEM((groups * rows, cols), bf16),
            pltpu.VMEM((groups * rows, every), f32),
            pltpu.VMEM((groups * rows, HD), f32),
            pltpu.VMEM((groups * rows, HD), f32),
        ],
        [],
        PCOVER,
        0,
    )(*parts, memory_sections.reshape(1, every))

    out_rows, out_cols = groups * tokens, out_weight.shape[1]
    share = out_rows // shares
    held = bf16 if memory % 16 == 0 else f32
    pieces = call(
        functools.partial(attend_kernel, groups, shares),
        [VMEM] * (groups + 5),
        [pltpu.VMEM((share, out_cols), f32 if k == 0 else bf16) for k in range(shares)],
        [
            pltpu.VMEM((every, cols), held),
            pltpu.VMEM((every, cols), held),
            pltpu.VMEM((out_rows, out_weight.shape[0]), f32),
            pltpu.VMEM((out_rows, out_cols), f32),
        ],
        2 * out_rows * out_weight.size,
        2 * out_weight.size,
    )(*kvs, *prepared, out_weight)
    summed = pieces[0]
    for bits in range(shares - 1, 0, -1):
        summed = summed + permute(pieces[bits], "tp", bits).astype(f32)
    return summed.astype(bf16)


def solution(mesh):
    return jax.shard_map(
        body,
        mesh=mesh,
        in_specs=(
            P(("parts", "dp"), "tp"),
            P(None, None, "tp"),
            P(None, "tp"),
            P("parts"),
            P(("parts", "dp")),
            P(("parts", "dp"), "tp"),
            P(("parts", "dp"), "tp"),
            P(("parts", "dp"), "tp"),
            P(("parts", "dp"), None, "tp"),
            P(("parts", "dp"), None, "tp"),
            P(("parts", "dp")),
            P("tp", "dp"),
        ),
        out_specs=P(("parts", "tp"), "dp"),
        check_vma=False,
    )
```

```python
import functools

import jax
import jax.numpy as jnp
from jax import lax
from jax.experimental import pallas as pl
from jax.experimental.pallas import tpu as pltpu
from jax.sharding import PartitionSpec as P

D = 5120
HQ = 40
KVH = 8
HD = 128
NEW = 2
PER_HEAD = HQ // KVH
INV = 1.0 / HD**0.5

masked_score = -1e30
bf16 = jnp.bfloat16
COVER = 1 << 36
PCOVER = 1 << 10
f32 = jnp.float32

TOP, TOTAL, SECTION = 0, 3, 5
STATS = 16


def nt(a, b):
    return lax.dot_general(a, b, (((1,), (1,)), ((), ())), preferred_element_type=f32)


def nn(a, b):
    return jnp.dot(a, b, preferred_element_type=f32)


def spread(blocks):
    zeros = jnp.zeros_like(blocks[0])
    rows = [
        jnp.concatenate([b if i == j else zeros for i in range(len(blocks))], axis=1)
        if len(blocks) > 1
        else b
        for j, b in enumerate(blocks)
    ]
    return jnp.concatenate(rows, axis=0)


def split(x, pieces):
    out = []
    for _ in range(pieces):
        piece = x.astype(bf16).astype(f32)
        out.append(piece)
        x = x - piece
    return out


def eye(rows, cols):
    row = lax.broadcasted_iota(jnp.int32, (rows, cols), 0)
    return (row == lax.broadcasted_iota(jnp.int32, (rows, cols), 1)).astype(f32).astype(bf16)


def up(n, to):
    return -(-n // to) * to


def open_kernel(group_ref, after, out_ref):
    out_ref[...] = jnp.full(out_ref.shape, group_ref[0].astype(f32))


def cache_kernel(lens_ref, section_ref, q_ref, nk_ref, nv_ref, ck_ref, cv_ref, out_ref):
    requests, slots, cols = ck_ref.shape
    heads = cols // HD
    tokens = requests * NEW
    per = PER_HEAD * tokens
    rows = heads * per
    row = lax.broadcasted_iota(jnp.int32, (rows, 1), 0)
    request = lax.rem(lax.div(row, NEW), requests)
    token = lax.rem(row, NEW)
    q = q_ref[...].astype(f32)
    blocks = []
    for j in range(heads):
        parts = [q[:, (j * PER_HEAD + g) * HD : (j * PER_HEAD + g + 1) * HD] for g in range(PER_HEAD)]
        blocks.append(jnp.concatenate(parts, axis=0))
    out_ref[0:rows, :] = jnp.concatenate(blocks, axis=0).astype(bf16)
    qs = spread(blocks).astype(bf16)
    fresh = lax.broadcasted_iota(jnp.int32, (rows, tokens), 1)
    seen = (lax.div(fresh, NEW) == request) & (lax.rem(fresh, NEW) <= token)
    s_new = jnp.where(seen, nt(qs, nk_ref[...]) * INV, masked_score)
    limit = jnp.full((rows, 1), lens_ref[0], jnp.int32)
    for r in range(1, requests):
        limit = jnp.where(request == r, lens_ref[r], limit)
    live = lax.broadcasted_iota(jnp.int32, (rows, slots), 1) < limit
    s = nt(qs, ck_ref[0])
    for r in range(1, requests):
        s = jnp.where(request == r, nt(qs, ck_ref[r]), s)
    s = jnp.where(live, s * INV, masked_score)

    top = jnp.maximum(jnp.max(s, axis=1, keepdims=True), jnp.max(s_new, axis=1, keepdims=True))
    p = jnp.where(live, jnp.exp(s - top), 0.0)
    p_new = jnp.where(seen, jnp.exp(s_new - top), 0.0)
    total = jnp.sum(p, axis=1, keepdims=True) + jnp.sum(p_new, axis=1, keepdims=True)
    p = p.astype(bf16)
    acc = nn(p, cv_ref[0])
    for r in range(1, requests):
        acc = jnp.where(request == r, nn(p, cv_ref[r]), acc)
    acc = acc + nn(p_new.astype(bf16).astype(f32), nv_ref[...].astype(f32))
    mine = jnp.concatenate([acc[j * per : (j + 1) * per, j * HD : (j + 1) * HD] for j in range(heads)], axis=0)
    seg = up(rows, 16)
    out_ref[seg : seg + rows, :] = (mine / total).astype(bf16)

    lane = lax.broadcasted_iota(jnp.int32, (rows, HD), 1)
    stats = jnp.where(lane == SECTION, section_ref[0:1, :], 0.0)
    for i, piece in enumerate(split(top, 3)):
        stats = jnp.where(lane == TOP + i, piece, stats)
    for i, piece in enumerate(split(total, 2)):
        stats = jnp.where(lane == TOTAL + i, piece, stats)
    if rows < HD:
        stats = jnp.concatenate([stats, jnp.zeros((HD - rows, HD), f32)], axis=0)
    out_ref[2 * seg : 2 * seg + STATS, :] = nt(eye(STATS, HD), stats.astype(bf16)).astype(bf16)


def project_kernel(bits, first, last, *refs):
    count = len(bits)
    pieces, w_ref, refs = refs[:count], refs[count], refs[count + 1 :]
    rows, depth = pieces[0].shape
    me = lax.axis_index("tp")
    if first:
        acc, squares = [None, None], None
    else:
        acc = [refs[0][s * rows : (s + 1) * rows, :] for s in range(2)]
        squares = refs[1][:, 0:1]
        refs = refs[2:]
    for k, piece in zip(bits, pieces):
        h = piece[...]
        wide = h.astype(f32)
        square = jnp.sum(wide * wide, axis=1, keepdims=True)
        squares = square if squares is None else squares + square
        at = pl.multiple_of((me ^ k) * depth, depth)
        for s in range(2):
            term = nn(h, w_ref[s, pl.ds(at, depth), :])
            acc[s] = term if acc[s] is None else acc[s] + term
    if not last:
        for s in range(2):
            refs[0][s * rows : (s + 1) * rows, :] = acc[s]
        refs[1][...] = jnp.broadcast_to(squares, refs[1].shape)
        return
    b_ref, out_ref = refs
    scale = lax.rsqrt(squares / D + 1e-06)
    for s in range(2):
        bias = b_ref[s : s + 1, :].astype(f32)
        out_ref[s * rows : (s + 1) * rows, :] = (acc[s] * scale + bias).astype(bf16)


def pair_kernel(near_ref, far_ref, after, out_ref):
    out_ref[0] = near_ref[...]
    out_ref[1] = far_ref[...]


def prepare_kernel(heads, *refs):
    pairs, (section_ref, q_ref, bias_ref, old_ref, stats_ref) = refs[:-5], refs[-5:]
    parts = [pair.at[i] for i in range(2) for pair in pairs]
    groups = len(parts)
    seg = (parts[0].shape[0] - STATS) // 2
    rows = q_ref.shape[0] // groups
    per = rows // heads
    blocks = [part[0:rows, :].astype(f32) for part in parts]
    q_ref[...] = jnp.concatenate(
        [spread([b[j * per : (j + 1) * per, :] for j in range(heads)]) for b in blocks], axis=0
    ).astype(bf16)
    stats = nt(
        eye(rows, HD), jnp.concatenate([part[2 * seg : 2 * seg + STATS, :] for part in parts], axis=0)
    )

    def column(at, pieces):
        columns = []
        for k in range(groups):
            c = k * STATS + at
            columns.append(sum([stats[:, c + i : c + i + 1] for i in range(pieces)]))
        return jnp.concatenate(columns, axis=0)

    top, total = column(TOP, 3), column(TOTAL, 2)
    bias_ref[...] = jnp.where(column(SECTION, 1) == section_ref[...].astype(f32), 0.0, masked_score)
    old = jnp.concatenate([part[seg : seg + rows, :] for part in parts], axis=0).astype(f32)
    old_ref[...] = old * total
    lane = lax.broadcasted_iota(jnp.int32, stats_ref.shape, 1)
    stats_ref[...] = jnp.where(lane == 0, top, total)


def attend_kernel(groups, shares, *refs):
    kvs, (q_ref, bias_ref, old_ref, stats_ref, w_ref) = refs[:groups], refs[groups : groups + 5]
    outs = refs[groups + 5 : groups + 5 + shares]
    k_ref, v_ref, attended_ref, sums_ref = refs[groups + 5 + shares :]
    me_dp, me_tp = lax.axis_index("dp"), lax.axis_index("tp")
    memory = kvs[0].shape[0] // 2
    heads = kvs[0].shape[1] // HD
    tokens = attended_ref.shape[0] // groups
    per = PER_HEAD * tokens
    rows = heads * per
    for bits, kv in enumerate(kvs):
        first = pl.multiple_of((me_dp ^ bits) * memory, memory)
        k_ref[pl.ds(first, memory), :] = kv[0:memory, :].astype(k_ref.dtype)
        v_ref[pl.ds(first, memory), :] = kv[memory : 2 * memory, :].astype(v_ref.dtype)
    s = nt(q_ref[...], k_ref[...].astype(bf16)) * INV + bias_ref[...]
    old_top, old_total = stats_ref[:, 0:1], stats_ref[:, 1:2]
    top = jnp.maximum(jnp.max(s, axis=1, keepdims=True), old_top)
    p = jnp.exp(s - top)
    shrink = jnp.exp(old_top - top)
    total = jnp.sum(p, axis=1, keepdims=True) + shrink * old_total
    acc = nn(p.astype(bf16), v_ref[...].astype(bf16))
    for k in range(groups):
        at = pl.multiple_of((me_dp ^ k) * tokens, tokens)
        for j in range(heads):
            a = k * rows + j * per
            block = acc[a : a + per, j * HD : (j + 1) * HD] + old_ref[a : a + per, :] * shrink[a : a + per]
            block = block / total[a : a + per]
            for g in range(PER_HEAD):
                c = (j * PER_HEAD + g) * HD
                attended_ref[pl.ds(at, tokens), c : c + HD] = block[g * tokens : (g + 1) * tokens, :]
    sums_ref[...] = nn(attended_ref[...].astype(bf16), w_ref[...])
    share = sums_ref.shape[0] // shares
    for k, out in enumerate(outs):
        at = pl.multiple_of((me_tp ^ k) * share, share)
        out[...] = sums_ref[pl.ds(at, share), :].astype(out.dtype)


SMEM = pl.BlockSpec(memory_space=pltpu.SMEM)
VMEM = pl.BlockSpec(memory_space=pltpu.VMEM)
ANY = pl.BlockSpec(memory_space=pl.ANY)
HBM = pl.BlockSpec(memory_space=pltpu.HBM)
PARAMS = pltpu.CompilerParams(vmem_limit_bytes=24 * 1024 * 1024)


def call(kernel, in_specs, out_shape, scratch, flops, bytes_accessed):
    return pl.pallas_call(
        kernel,
        in_specs=in_specs,
        out_shape=out_shape,
        out_specs=jax.tree.map(lambda _: VMEM, out_shape),
        scratch_shapes=scratch,
        compiler_params=PARAMS,
        cost_estimate=pl.CostEstimate(flops=flops, bytes_accessed=bytes_accessed, transcendentals=0),
    )


def in_hbm(*arrays):
    return [pltpu.with_memory_space_constraint(x, pltpu.HBM) for x in arrays]


def permute(x, axis, bits):
    return lax.ppermute(x, axis, [(i, i ^ bits) for i in range(lax.axis_size(axis))])


def passed_on(x, near, axis):
    n = lax.axis_size(axis)
    held = {0: x}
    bit = n // 2
    while bit:
        for bits in sorted(held):
            held[bits | bit] = permute(held[bits], axis, bit)
        held[0] = near
        bit //= 2
    return [held[bits] for bits in range(n)]


def body(
    memory_hidden,
    kv_weight,
    kv_bias,
    memory_sections,
    group_sections,
    queries,
    new_keys,
    new_values,
    cache_keys,
    cache_values,
    cache_lengths,
    out_weight,
):
    groups, shares = lax.axis_size("dp"), lax.axis_size("tp")
    memory, depth = memory_hidden.shape
    requests, slots, cols = cache_keys.shape
    tokens = requests * NEW
    rows = (cols // HD) * PER_HEAD * tokens
    every = memory_sections.shape[0]

    gate = call(lambda *refs: None, [], jax.ShapeDtypeStruct((8, HD), f32), [], COVER, 0)()
    group, gate = lax.optimization_barrier((group_sections, gate))
    section = call(open_kernel, [SMEM, ANY], pltpu.VMEM((8, HD), f32), [], 1 << 10, 0)(group, gate)
    own, section = lax.optimization_barrier((memory_hidden, section))
    part = call(
        cache_kernel,
        [SMEM] + [VMEM] * 6,
        pltpu.VMEM((2 * up(rows, 16) + STATS, HD), bf16),
        [],
        4 * rows * slots * cols * requests,
        4 * requests * slots * cols,
    )(cache_lengths, section, queries, new_keys, new_values, cache_keys, cache_values)
    own_later, part = lax.optimization_barrier((own, part))
    hidden = passed_on(own, own_later, "tp")
    part_far = permute(part, "dp", groups // 2)
    near, far = list(range(shares - 1)), [shares - 1]
    partial = call(
        functools.partial(project_kernel, near, True, False),
        [VMEM] * (len(near) + 1),
        [pltpu.VMEM((2 * memory, cols), f32), pltpu.VMEM((memory, HD), f32)],
        [],
        COVER,
        4 * D * cols,
    )(*[hidden[k] for k in near], kv_weight)
    kv = call(
        functools.partial(project_kernel, far, False, True),
        [VMEM] * 5,
        pltpu.VMEM((2 * memory, cols), bf16),
        [],
        4 * memory * D * cols // shares,
        4 * D * cols // shares,
    )(hidden[far[0]], kv_weight, *partial, kv_bias)
    kv_far = permute(kv, "dp", groups // 2)
    pair = call(
        pair_kernel,
        [VMEM, VMEM, ANY],
        pltpu.VMEM((2,) + part.shape, bf16),
        [],
        COVER,
        0,
    )(part, part_far, kv)
    kv_on, _ = lax.optimization_barrier((kv_far, pair))
    half = range(1, groups // 2)
    pairs = [pair, *[permute(pair, "dp", bits) for bits in half]]
    kvs = [kv, *[permute(kv, "dp", bits) for bits in half], kv_far, *[permute(kv_on, "dp", bits) for bits in half]]
    prepared = call(
        functools.partial(prepare_kernel, cols // HD),
        [VMEM] * (groups // 2 + 1),
        [
            pltpu.VMEM((groups * rows, cols), bf16),
            pltpu.VMEM((groups * rows, every), f32),
            pltpu.VMEM((groups * rows, HD), f32),
            pltpu.VMEM((groups * rows, HD), f32),
        ],
        [],
        PCOVER,
        0,
    )(*pairs, memory_sections.reshape(1, every))

    out_rows, out_cols = groups * tokens, out_weight.shape[1]
    share = out_rows // shares
    held = bf16 if memory % 16 == 0 else f32
    pieces = call(
        functools.partial(attend_kernel, groups, shares),
        [VMEM] * (groups + 5),
        [pltpu.VMEM((share, out_cols), f32 if k == 0 else bf16) for k in range(shares)],
        [
            pltpu.VMEM((every, cols), held),
            pltpu.VMEM((every, cols), held),
            pltpu.VMEM((out_rows, out_weight.shape[0]), f32),
            pltpu.VMEM((out_rows, out_cols), f32),
        ],
        2 * out_rows * out_weight.size,
        2 * out_weight.size,
    )(*kvs, *prepared, out_weight)
    summed = pieces[0]
    for bits in range(shares - 1, 0, -1):
        summed = summed + permute(pieces[bits], "tp", bits).astype(f32)
    return summed.astype(bf16)


def solution(mesh):
    return jax.shard_map(
        body,
        mesh=mesh,
        in_specs=(
            P(("parts", "dp"), "tp"),
            P(None, None, "tp"),
            P(None, "tp"),
            P("parts"),
            P(("parts", "dp")),
            P(("parts", "dp"), "tp"),
            P(("parts", "dp"), "tp"),
            P(("parts", "dp"), "tp"),
            P(("parts", "dp"), None, "tp"),
            P(("parts", "dp"), None, "tp"),
            P(("parts", "dp")),
            P("tp", "dp"),
        ),
        out_specs=P(("parts", "tp"), "dp"),
        check_vma=False,
    )
```

```python
import functools

import jax
import jax.numpy as jnp
from jax import lax
from jax.experimental import pallas as pl
from jax.experimental.pallas import tpu as pltpu
from jax.sharding import PartitionSpec as P

D = 5120
HQ = 40
KVH = 8
HD = 128
NEW = 2
PER_HEAD = HQ // KVH
INV = 1.0 / HD**0.5

masked_score = -1e30
bf16 = jnp.bfloat16
COVER = 1 << 36
PCOVER = 1 << 10
f32 = jnp.float32

TOP, TOTAL, SECTION = 0, 3, 5
STATS = 16


def nt(a, b):
    return lax.dot_general(a, b, (((1,), (1,)), ((), ())), preferred_element_type=f32)


def nn(a, b):
    return jnp.dot(a, b, preferred_element_type=f32)


def spread(blocks):
    zeros = jnp.zeros_like(blocks[0])
    rows = [
        jnp.concatenate([b if i == j else zeros for i in range(len(blocks))], axis=1)
        if len(blocks) > 1
        else b
        for j, b in enumerate(blocks)
    ]
    return jnp.concatenate(rows, axis=0)


def split(x, pieces):
    out = []
    for _ in range(pieces):
        piece = x.astype(bf16).astype(f32)
        out.append(piece)
        x = x - piece
    return out


def eye(rows, cols):
    row = lax.broadcasted_iota(jnp.int32, (rows, cols), 0)
    return (row == lax.broadcasted_iota(jnp.int32, (rows, cols), 1)).astype(f32).astype(bf16)


def up(n, to):
    return -(-n // to) * to


def open_kernel(group_ref, after, out_ref):
    out_ref[...] = jnp.full(out_ref.shape, group_ref[0].astype(f32))


def cache_kernel(lens_ref, section_ref, q_ref, nk_ref, nv_ref, ck_ref, cv_ref, out_ref):
    requests, slots, cols = ck_ref.shape
    heads = cols // HD
    tokens = requests * NEW
    per = PER_HEAD * tokens
    rows = heads * per
    row = lax.broadcasted_iota(jnp.int32, (rows, 1), 0)
    request = lax.rem(lax.div(row, NEW), requests)
    token = lax.rem(row, NEW)
    q = q_ref[...].astype(f32)
    blocks = []
    for j in range(heads):
        parts = [q[:, (j * PER_HEAD + g) * HD : (j * PER_HEAD + g + 1) * HD] for g in range(PER_HEAD)]
        blocks.append(jnp.concatenate(parts, axis=0))
    out_ref[0:rows, :] = jnp.concatenate(blocks, axis=0).astype(bf16)
    qs = spread(blocks).astype(bf16)
    fresh = lax.broadcasted_iota(jnp.int32, (rows, tokens), 1)
    seen = (lax.div(fresh, NEW) == request) & (lax.rem(fresh, NEW) <= token)
    s_new = jnp.where(seen, nt(qs, nk_ref[...]) * INV, masked_score)
    limit = jnp.full((rows, 1), lens_ref[0], jnp.int32)
    for r in range(1, requests):
        limit = jnp.where(request == r, lens_ref[r], limit)
    live = lax.broadcasted_iota(jnp.int32, (rows, slots), 1) < limit
    s = nt(qs, ck_ref[0])
    for r in range(1, requests):
        s = jnp.where(request == r, nt(qs, ck_ref[r]), s)
    s = jnp.where(live, s * INV, masked_score)

    top = jnp.maximum(jnp.max(s, axis=1, keepdims=True), jnp.max(s_new, axis=1, keepdims=True))
    p = jnp.where(live, jnp.exp(s - top), 0.0)
    p_new = jnp.where(seen, jnp.exp(s_new - top), 0.0)
    total = jnp.sum(p, axis=1, keepdims=True) + jnp.sum(p_new, axis=1, keepdims=True)
    p = p.astype(bf16)
    acc = nn(p, cv_ref[0])
    for r in range(1, requests):
        acc = jnp.where(request == r, nn(p, cv_ref[r]), acc)
    acc = acc + nn(p_new.astype(bf16).astype(f32), nv_ref[...].astype(f32))
    mine = jnp.concatenate([acc[j * per : (j + 1) * per, j * HD : (j + 1) * HD] for j in range(heads)], axis=0)
    seg = up(rows, 16)
    out_ref[seg : seg + rows, :] = (mine / total).astype(bf16)

    lane = lax.broadcasted_iota(jnp.int32, (rows, HD), 1)
    stats = jnp.where(lane == SECTION, section_ref[0:1, :], 0.0)
    for i, piece in enumerate(split(top, 3)):
        stats = jnp.where(lane == TOP + i, piece, stats)
    for i, piece in enumerate(split(total, 2)):
        stats = jnp.where(lane == TOTAL + i, piece, stats)
    if rows < HD:
        stats = jnp.concatenate([stats, jnp.zeros((HD - rows, HD), f32)], axis=0)
    out_ref[2 * seg : 2 * seg + STATS, :] = nt(eye(STATS, HD), stats.astype(bf16)).astype(bf16)


def project_kernel(bits, first, last, *refs):
    count = len(bits)
    pieces, w_ref, refs = refs[:count], refs[count], refs[count + 1 :]
    rows, depth = pieces[0].shape
    me = lax.axis_index("tp")
    if first:
        acc, squares = [None, None], None
    else:
        acc = [refs[0][s * rows : (s + 1) * rows, :] for s in range(2)]
        squares = refs[1][:, 0:1]
        refs = refs[2:]
    for k, piece in zip(bits, pieces):
        h = piece[...]
        wide = h.astype(f32)
        square = jnp.sum(wide * wide, axis=1, keepdims=True)
        squares = square if squares is None else squares + square
        at = pl.multiple_of((me ^ k) * depth, depth)
        for s in range(2):
            term = nn(h, w_ref[s, pl.ds(at, depth), :])
            acc[s] = term if acc[s] is None else acc[s] + term
    if not last:
        for s in range(2):
            refs[0][s * rows : (s + 1) * rows, :] = acc[s]
        refs[1][...] = jnp.broadcast_to(squares, refs[1].shape)
        return
    b_ref, *_, out_ref = refs
    scale = lax.rsqrt(squares / D + 1e-06)
    for s in range(2):
        bias = b_ref[s : s + 1, :].astype(f32)
        out_ref[s * rows : (s + 1) * rows, :] = (acc[s] * scale + bias).astype(bf16)


def prepare_kernel(heads, *refs):
    parts, (section_ref, q_ref, bias_ref, old_ref, stats_ref) = refs[:-5], refs[-5:]
    groups = len(parts)
    seg = (parts[0].shape[0] - STATS) // 2
    rows = q_ref.shape[0] // groups
    per = rows // heads
    blocks = [part[0:rows, :].astype(f32) for part in parts]
    q_ref[...] = jnp.concatenate(
        [spread([b[j * per : (j + 1) * per, :] for j in range(heads)]) for b in blocks], axis=0
    ).astype(bf16)
    stats = nt(
        eye(rows, HD), jnp.concatenate([part[2 * seg : 2 * seg + STATS, :] for part in parts], axis=0)
    )

    def column(at, pieces):
        columns = []
        for k in range(groups):
            c = k * STATS + at
            columns.append(sum([stats[:, c + i : c + i + 1] for i in range(pieces)]))
        return jnp.concatenate(columns, axis=0)

    top, total = column(TOP, 3), column(TOTAL, 2)
    bias_ref[...] = jnp.where(column(SECTION, 1) == section_ref[...].astype(f32), 0.0, masked_score)
    old = jnp.concatenate([part[seg : seg + rows, :] for part in parts], axis=0).astype(f32)
    old_ref[...] = old * total
    lane = lax.broadcasted_iota(jnp.int32, stats_ref.shape, 1)
    stats_ref[...] = jnp.where(lane == 0, top, total)


def attend_kernel(groups, shares, *refs):
    kvs, (q_ref, bias_ref, old_ref, stats_ref, w_ref) = refs[:groups], refs[groups : groups + 5]
    outs = refs[groups + 5 : groups + 5 + shares]
    k_ref, v_ref, attended_ref, sums_ref = refs[groups + 5 + shares :]
    me_dp, me_tp = lax.axis_index("dp"), lax.axis_index("tp")
    memory = kvs[0].shape[0] // 2
    heads = kvs[0].shape[1] // HD
    tokens = attended_ref.shape[0] // groups
    per = PER_HEAD * tokens
    rows = heads * per
    for bits, kv in enumerate(kvs):
        first = pl.multiple_of((me_dp ^ bits) * memory, memory)
        k_ref[pl.ds(first, memory), :] = kv[0:memory, :].astype(k_ref.dtype)
        v_ref[pl.ds(first, memory), :] = kv[memory : 2 * memory, :].astype(v_ref.dtype)
    s = nt(q_ref[...], k_ref[...].astype(bf16)) * INV + bias_ref[...]
    old_top, old_total = stats_ref[:, 0:1], stats_ref[:, 1:2]
    top = jnp.maximum(jnp.max(s, axis=1, keepdims=True), old_top)
    p = jnp.exp(s - top)
    shrink = jnp.exp(old_top - top)
    total = jnp.sum(p, axis=1, keepdims=True) + shrink * old_total
    acc = nn(p.astype(bf16), v_ref[...].astype(bf16))
    for k in range(groups):
        at = pl.multiple_of((me_dp ^ k) * tokens, tokens)
        for j in range(heads):
            a = k * rows + j * per
            block = acc[a : a + per, j * HD : (j + 1) * HD] + old_ref[a : a + per, :] * shrink[a : a + per]
            block = block / total[a : a + per]
            for g in range(PER_HEAD):
                c = (j * PER_HEAD + g) * HD
                attended_ref[pl.ds(at, tokens), c : c + HD] = block[g * tokens : (g + 1) * tokens, :]
    sums_ref[...] = nn(attended_ref[...].astype(bf16), w_ref[...])
    share = sums_ref.shape[0] // shares
    for k, out in enumerate(outs):
        at = pl.multiple_of((me_tp ^ k) * share, share)
        out[...] = sums_ref[pl.ds(at, share), :].astype(out.dtype)


SMEM = pl.BlockSpec(memory_space=pltpu.SMEM)
VMEM = pl.BlockSpec(memory_space=pltpu.VMEM)
ANY = pl.BlockSpec(memory_space=pl.ANY)
HBM = pl.BlockSpec(memory_space=pltpu.HBM)
PARAMS = pltpu.CompilerParams(vmem_limit_bytes=24 * 1024 * 1024)


def call(kernel, in_specs, out_shape, scratch, flops, bytes_accessed):
    return pl.pallas_call(
        kernel,
        in_specs=in_specs,
        out_shape=out_shape,
        out_specs=jax.tree.map(lambda _: VMEM, out_shape),
        scratch_shapes=scratch,
        compiler_params=PARAMS,
        cost_estimate=pl.CostEstimate(flops=flops, bytes_accessed=bytes_accessed, transcendentals=0),
    )


def in_hbm(*arrays):
    return [pltpu.with_memory_space_constraint(x, pltpu.HBM) for x in arrays]


def permute(x, axis, bits):
    return lax.ppermute(x, axis, [(i, i ^ bits) for i in range(lax.axis_size(axis))])


def passed_on(x, near, axis):
    n = lax.axis_size(axis)
    held = {0: x}
    bit = n // 2
    while bit:
        for bits in sorted(held):
            held[bits | bit] = permute(held[bits], axis, bit)
        held[0] = near
        bit //= 2
    return [held[bits] for bits in range(n)]


def body(
    memory_hidden,
    kv_weight,
    kv_bias,
    memory_sections,
    group_sections,
    queries,
    new_keys,
    new_values,
    cache_keys,
    cache_values,
    cache_lengths,
    out_weight,
):
    groups, shares = lax.axis_size("dp"), lax.axis_size("tp")
    memory, depth = memory_hidden.shape
    requests, slots, cols = cache_keys.shape
    tokens = requests * NEW
    rows = (cols // HD) * PER_HEAD * tokens
    every = memory_sections.shape[0]

    gate = call(lambda *refs: None, [], jax.ShapeDtypeStruct((8, HD), f32), [], COVER, 0)()
    group, gate = lax.optimization_barrier((group_sections, gate))
    section = call(open_kernel, [SMEM, ANY], pltpu.VMEM((8, HD), f32), [], 1 << 10, 0)(group, gate)
    own, section = lax.optimization_barrier((memory_hidden, section))
    part = call(
        cache_kernel,
        [SMEM] + [VMEM] * 6,
        pltpu.VMEM((2 * up(rows, 16) + STATS, HD), bf16),
        [],
        4 * rows * slots * cols * requests,
        4 * requests * slots * cols,
    )(cache_lengths, section, queries, new_keys, new_values, cache_keys, cache_values)
    own_later, part = lax.optimization_barrier((own, part))
    hidden = passed_on(own, own_later, "tp")
    half = range(1, groups // 2)
    part_far = permute(part, "dp", groups // 2)
    part_near = [permute(part, "dp", bits) for bits in half]
    near, far = list(range(shares - 1)), [shares - 1]
    partial = call(
        functools.partial(project_kernel, near, True, False),
        [VMEM] * (len(near) + 1),
        [pltpu.VMEM((2 * memory, cols), f32), pltpu.VMEM((memory, HD), f32)],
        [],
        COVER,
        4 * D * cols,
    )(*[hidden[k] for k in near], kv_weight)
    kv = call(
        functools.partial(project_kernel, far, False, True),
        [VMEM] * 5 + [ANY] * len(part_near),
        pltpu.VMEM((2 * memory, cols), bf16),
        [],
        4 * memory * D * cols // shares,
        4 * D * cols // shares,
    )(hidden[far[0]], kv_weight, *partial, kv_bias, *part_near)
    kv_far = permute(kv, "dp", groups // 2)
    part_far = pl.pallas_call(
        lambda *refs: None,
        in_specs=[VMEM, ANY],
        out_shape=pltpu.VMEM(part.shape, bf16),
        out_specs=VMEM,
        input_output_aliases={0: 0},
        compiler_params=PARAMS,
        cost_estimate=pl.CostEstimate(flops=COVER, bytes_accessed=0, transcendentals=0),
    )(part_far, kv)
    parts = [part, *part_near, part_far, *[permute(part_far, "dp", bits) for bits in half]]
    kv_on, *_ = lax.optimization_barrier((kv_far, *parts[groups // 2 :]))
    kvs = [kv, *[permute(kv, "dp", bits) for bits in half], kv_far, *[permute(kv_on, "dp", bits) for bits in half]]
    prepared = call(
        functools.partial(prepare_kernel, cols // HD),
        [VMEM] * (groups + 1),
        [
            pltpu.VMEM((groups * rows, cols), bf16),
            pltpu.VMEM((groups * rows, every), f32),
            pltpu.VMEM((groups * rows, HD), f32),
            pltpu.VMEM((groups * rows, HD), f32),
        ],
        [],
        PCOVER,
        0,
    )(*parts, memory_sections.reshape(1, every))

    out_rows, out_cols = groups * tokens, out_weight.shape[1]
    share = out_rows // shares
    held = bf16 if memory % 16 == 0 else f32
    pieces = call(
        functools.partial(attend_kernel, groups, shares),
        [VMEM] * (groups + 5),
        [pltpu.VMEM((share, out_cols), f32 if k == 0 else bf16) for k in range(shares)],
        [
            pltpu.VMEM((every, cols), held),
            pltpu.VMEM((every, cols), held),
            pltpu.VMEM((out_rows, out_weight.shape[0]), f32),
            pltpu.VMEM((out_rows, out_cols), f32),
        ],
        2 * out_rows * out_weight.size,
        2 * out_weight.size,
    )(*kvs, *prepared, out_weight)
    summed = pieces[0]
    for bits in [*range(1, shares - 2), *range(shares - 1, shares - 3, -1)]:
        summed = summed + permute(pieces[bits], "tp", bits).astype(f32)
    return summed.astype(bf16)


def solution(mesh):
    return jax.shard_map(
        body,
        mesh=mesh,
        in_specs=(
            P(("parts", "dp"), "tp"),
            P(None, None, "tp"),
            P(None, "tp"),
            P("parts"),
            P(("parts", "dp")),
            P(("parts", "dp"), "tp"),
            P(("parts", "dp"), "tp"),
            P(("parts", "dp"), "tp"),
            P(("parts", "dp"), None, "tp"),
            P(("parts", "dp"), None, "tp"),
            P(("parts", "dp")),
            P("tp", "dp"),
        ),
        out_specs=P(("parts", "tp"), "dp"),
        check_vma=False,
    )
```

```python
import functools

import jax
import jax.numpy as jnp
from jax import lax
from jax.experimental import pallas as pl
from jax.experimental.pallas import tpu as pltpu
from jax.sharding import PartitionSpec as P

D = 5120
HQ = 40
KVH = 8
HD = 128
NEW = 2
PER_HEAD = HQ // KVH
INV = 1.0 / HD**0.5

masked_score = -1e30
bf16 = jnp.bfloat16
COVER = 1 << 36
PCOVER = 1 << 10
f32 = jnp.float32

TOP, TOTAL, SECTION = 0, 3, 5
STATS = 16


def nt(a, b):
    return lax.dot_general(a, b, (((1,), (1,)), ((), ())), preferred_element_type=f32)


def nn(a, b):
    return jnp.dot(a, b, preferred_element_type=f32)


def spread(blocks):
    zeros = jnp.zeros_like(blocks[0])
    rows = [
        jnp.concatenate([b if i == j else zeros for i in range(len(blocks))], axis=1)
        if len(blocks) > 1
        else b
        for j, b in enumerate(blocks)
    ]
    return jnp.concatenate(rows, axis=0)


def split(x, pieces):
    out = []
    for _ in range(pieces):
        piece = x.astype(bf16).astype(f32)
        out.append(piece)
        x = x - piece
    return out


def eye(rows, cols):
    row = lax.broadcasted_iota(jnp.int32, (rows, cols), 0)
    return (row == lax.broadcasted_iota(jnp.int32, (rows, cols), 1)).astype(f32).astype(bf16)


def up(n, to):
    return -(-n // to) * to


def open_kernel(group_ref, after, out_ref):
    out_ref[...] = jnp.full(out_ref.shape, group_ref[0].astype(f32))


def cache_kernel(lens_ref, section_ref, q_ref, nk_ref, nv_ref, ck_ref, cv_ref, out_ref):
    requests, slots, cols = ck_ref.shape
    heads = cols // HD
    tokens = requests * NEW
    per = PER_HEAD * tokens
    rows = heads * per
    row = lax.broadcasted_iota(jnp.int32, (rows, 1), 0)
    request = lax.rem(lax.div(row, NEW), requests)
    token = lax.rem(row, NEW)
    q = q_ref[...].astype(f32)
    blocks = []
    for j in range(heads):
        parts = [q[:, (j * PER_HEAD + g) * HD : (j * PER_HEAD + g + 1) * HD] for g in range(PER_HEAD)]
        blocks.append(jnp.concatenate(parts, axis=0))
    out_ref[0:rows, :] = jnp.concatenate(blocks, axis=0).astype(bf16)
    qs = spread(blocks).astype(bf16)
    fresh = lax.broadcasted_iota(jnp.int32, (rows, tokens), 1)
    seen = (lax.div(fresh, NEW) == request) & (lax.rem(fresh, NEW) <= token)
    s_new = jnp.where(seen, nt(qs, nk_ref[...]) * INV, masked_score)
    limit = jnp.full((rows, 1), lens_ref[0], jnp.int32)
    for r in range(1, requests):
        limit = jnp.where(request == r, lens_ref[r], limit)
    live = lax.broadcasted_iota(jnp.int32, (rows, slots), 1) < limit
    s = nt(qs, ck_ref[0])
    for r in range(1, requests):
        s = jnp.where(request == r, nt(qs, ck_ref[r]), s)
    s = jnp.where(live, s * INV, masked_score)

    top = jnp.maximum(jnp.max(s, axis=1, keepdims=True), jnp.max(s_new, axis=1, keepdims=True))
    p = jnp.where(live, jnp.exp(s - top), 0.0)
    p_new = jnp.where(seen, jnp.exp(s_new - top), 0.0)
    total = jnp.sum(p, axis=1, keepdims=True) + jnp.sum(p_new, axis=1, keepdims=True)
    p = p.astype(bf16)
    acc = nn(p, cv_ref[0])
    for r in range(1, requests):
        acc = jnp.where(request == r, nn(p, cv_ref[r]), acc)
    acc = acc + nn(p_new.astype(bf16).astype(f32), nv_ref[...].astype(f32))
    mine = jnp.concatenate([acc[j * per : (j + 1) * per, j * HD : (j + 1) * HD] for j in range(heads)], axis=0)
    seg = up(rows, 16)
    out_ref[seg : seg + rows, :] = (mine / total).astype(bf16)

    lane = lax.broadcasted_iota(jnp.int32, (rows, HD), 1)
    stats = jnp.where(lane == SECTION, section_ref[0:1, :], 0.0)
    for i, piece in enumerate(split(top, 3)):
        stats = jnp.where(lane == TOP + i, piece, stats)
    for i, piece in enumerate(split(total, 2)):
        stats = jnp.where(lane == TOTAL + i, piece, stats)
    if rows < HD:
        stats = jnp.concatenate([stats, jnp.zeros((HD - rows, HD), f32)], axis=0)
    out_ref[2 * seg : 2 * seg + STATS, :] = nt(eye(STATS, HD), stats.astype(bf16)).astype(bf16)


def project_kernel(bits, first, last, *refs):
    count = len(bits)
    pieces, w_ref, refs = refs[:count], refs[count], refs[count + 1 :]
    rows, depth = pieces[0].shape
    me = lax.axis_index("tp")
    if first:
        acc, squares = [None, None], None
    else:
        acc = [refs[0][s * rows : (s + 1) * rows, :] for s in range(2)]
        squares = refs[1][:, 0:1]
        refs = refs[2:]
    for k, piece in zip(bits, pieces):
        h = piece[...]
        wide = h.astype(f32)
        square = jnp.sum(wide * wide, axis=1, keepdims=True)
        squares = square if squares is None else squares + square
        at = pl.multiple_of((me ^ k) * depth, depth)
        for s in range(2):
            term = nn(h, w_ref[s, pl.ds(at, depth), :])
            acc[s] = term if acc[s] is None else acc[s] + term
    if not last:
        for s in range(2):
            refs[0][s * rows : (s + 1) * rows, :] = acc[s]
        refs[1][...] = jnp.broadcast_to(squares, refs[1].shape)
        return
    b_ref, out_ref = refs
    scale = lax.rsqrt(squares / D + 1e-06)
    for s in range(2):
        bias = b_ref[s : s + 1, :].astype(f32)
        out_ref[s * rows : (s + 1) * rows, :] = (acc[s] * scale + bias).astype(bf16)


def pair_kernel(near_ref, far_ref, after, out_ref):
    out_ref[0] = near_ref[...]
    out_ref[1] = far_ref[...]


def prepare_kernel(heads, *refs):
    pairs, (section_ref, q_ref, bias_ref, old_ref, stats_ref) = refs[:-5], refs[-5:]
    parts = [pair.at[i] for i in range(2) for pair in pairs]
    groups = len(parts)
    seg = (parts[0].shape[0] - STATS) // 2
    rows = q_ref.shape[0] // groups
    per = rows // heads
    blocks = [part[0:rows, :].astype(f32) for part in parts]
    q_ref[...] = jnp.concatenate(
        [spread([b[j * per : (j + 1) * per, :] for j in range(heads)]) for b in blocks], axis=0
    ).astype(bf16)
    stats = nt(
        eye(rows, HD), jnp.concatenate([part[2 * seg : 2 * seg + STATS, :] for part in parts], axis=0)
    )

    def column(at, pieces):
        columns = []
        for k in range(groups):
            c = k * STATS + at
            columns.append(sum([stats[:, c + i : c + i + 1] for i in range(pieces)]))
        return jnp.concatenate(columns, axis=0)

    top, total = column(TOP, 3), column(TOTAL, 2)
    bias_ref[...] = jnp.where(column(SECTION, 1) == section_ref[...].astype(f32), 0.0, masked_score)
    old = jnp.concatenate([part[seg : seg + rows, :] for part in parts], axis=0).astype(f32)
    old_ref[...] = old * total
    lane = lax.broadcasted_iota(jnp.int32, stats_ref.shape, 1)
    stats_ref[...] = jnp.where(lane == 0, top, total)


def attend_kernel(groups, shares, *refs):
    kvs, (q_ref, bias_ref, old_ref, stats_ref, w_ref) = refs[:groups], refs[groups : groups + 5]
    outs = refs[groups + 5 : groups + 5 + shares]
    k_ref, v_ref, attended_ref, sums_ref = refs[groups + 5 + shares :]
    me_dp, me_tp = lax.axis_index("dp"), lax.axis_index("tp")
    memory = kvs[0].shape[0] // 2
    heads = kvs[0].shape[1] // HD
    tokens = attended_ref.shape[0] // groups
    per = PER_HEAD * tokens
    rows = heads * per
    for bits, kv in enumerate(kvs):
        first = pl.multiple_of((me_dp ^ bits) * memory, memory)
        k_ref[pl.ds(first, memory), :] = kv[0:memory, :].astype(k_ref.dtype)
        v_ref[pl.ds(first, memory), :] = kv[memory : 2 * memory, :].astype(v_ref.dtype)
    s = nt(q_ref[...], k_ref[...].astype(bf16)) * INV + bias_ref[...]
    old_top, old_total = stats_ref[:, 0:1], stats_ref[:, 1:2]
    top = jnp.maximum(jnp.max(s, axis=1, keepdims=True), old_top)
    p = jnp.exp(s - top)
    shrink = jnp.exp(old_top - top)
    total = jnp.sum(p, axis=1, keepdims=True) + shrink * old_total
    acc = nn(p.astype(bf16), v_ref[...].astype(bf16))
    for k in range(groups):
        at = pl.multiple_of((me_dp ^ k) * tokens, tokens)
        for j in range(heads):
            a = k * rows + j * per
            block = acc[a : a + per, j * HD : (j + 1) * HD] + old_ref[a : a + per, :] * shrink[a : a + per]
            block = block / total[a : a + per]
            for g in range(PER_HEAD):
                c = (j * PER_HEAD + g) * HD
                attended_ref[pl.ds(at, tokens), c : c + HD] = block[g * tokens : (g + 1) * tokens, :]
    sums_ref[...] = nn(attended_ref[...].astype(bf16), w_ref[...])
    share = sums_ref.shape[0] // shares
    for k, out in enumerate(outs):
        at = pl.multiple_of((me_tp ^ k) * share, share)
        out[...] = sums_ref[pl.ds(at, share), :].astype(out.dtype)


SMEM = pl.BlockSpec(memory_space=pltpu.SMEM)
VMEM = pl.BlockSpec(memory_space=pltpu.VMEM)
ANY = pl.BlockSpec(memory_space=pl.ANY)
HBM = pl.BlockSpec(memory_space=pltpu.HBM)
PARAMS = pltpu.CompilerParams(vmem_limit_bytes=24 * 1024 * 1024)


def call(kernel, in_specs, out_shape, scratch, flops, bytes_accessed):
    return pl.pallas_call(
        kernel,
        in_specs=in_specs,
        out_shape=out_shape,
        out_specs=jax.tree.map(lambda _: VMEM, out_shape),
        scratch_shapes=scratch,
        compiler_params=PARAMS,
        cost_estimate=pl.CostEstimate(flops=flops, bytes_accessed=bytes_accessed, transcendentals=0),
    )


def in_hbm(*arrays):
    return [pltpu.with_memory_space_constraint(x, pltpu.HBM) for x in arrays]


def permute(x, axis, bits):
    return lax.ppermute(x, axis, [(i, i ^ bits) for i in range(lax.axis_size(axis))])


def passed_on(x, near, axis):
    n = lax.axis_size(axis)
    held = {0: x}
    bit = n // 2
    while bit:
        for bits in sorted(held):
            held[bits | bit] = permute(held[bits], axis, bit)
        held[0] = near
        bit //= 2
    return [held[bits] for bits in range(n)]


def body(
    memory_hidden,
    kv_weight,
    kv_bias,
    memory_sections,
    group_sections,
    queries,
    new_keys,
    new_values,
    cache_keys,
    cache_values,
    cache_lengths,
    out_weight,
):
    groups, shares = lax.axis_size("dp"), lax.axis_size("tp")
    memory, depth = memory_hidden.shape
    requests, slots, cols = cache_keys.shape
    tokens = requests * NEW
    rows = (cols // HD) * PER_HEAD * tokens
    every = memory_sections.shape[0]

    gate = call(lambda *refs: None, [], jax.ShapeDtypeStruct((8, HD), f32), [], COVER, 0)()
    group, gate = lax.optimization_barrier((group_sections, gate))
    section = call(open_kernel, [SMEM, ANY], pltpu.VMEM((8, HD), f32), [], 1 << 10, 0)(group, gate)
    own, section = lax.optimization_barrier((memory_hidden, section))
    part = call(
        cache_kernel,
        [SMEM] + [VMEM] * 6,
        pltpu.VMEM((2 * up(rows, 16) + STATS, HD), bf16),
        [],
        4 * rows * slots * cols * requests,
        4 * requests * slots * cols,
    )(cache_lengths, section, queries, new_keys, new_values, cache_keys, cache_values)
    own_later, part = lax.optimization_barrier((own, part))
    hidden = passed_on(own, own_later, "tp")
    part_far = permute(part, "dp", groups // 2)
    near, far = list(range(shares - 1)), [shares - 1]
    partial = call(
        functools.partial(project_kernel, near, True, False),
        [VMEM] * (len(near) + 1),
        [pltpu.VMEM((2 * memory, cols), f32), pltpu.VMEM((memory, HD), f32)],
        [],
        COVER,
        4 * D * cols,
    )(*[hidden[k] for k in near], kv_weight)
    kv = call(
        functools.partial(project_kernel, far, False, True),
        [VMEM] * 5,
        pltpu.VMEM((2 * memory, cols), bf16),
        [],
        4 * memory * D * cols // shares,
        4 * D * cols // shares,
    )(hidden[far[0]], kv_weight, *partial, kv_bias)
    kv_far = permute(kv, "dp", groups // 2)
    pair = call(
        pair_kernel,
        [VMEM, VMEM, ANY],
        pltpu.VMEM((2,) + part.shape, bf16),
        [],
        COVER,
        0,
    )(part, part_far, kv)
    kv_on, _ = lax.optimization_barrier((kv_far, pair))
    half = range(1, groups // 2)
    pairs = [pair, *[permute(pair, "dp", bits) for bits in half]]
    kvs = [kv, *[permute(kv, "dp", bits) for bits in half], kv_far, *[permute(kv_on, "dp", bits) for bits in half]]
    prepared = call(
        functools.partial(prepare_kernel, cols // HD),
        [VMEM] * (groups // 2 + 1),
        [
            pltpu.VMEM((groups * rows, cols), bf16),
            pltpu.VMEM((groups * rows, every), f32),
            pltpu.VMEM((groups * rows, HD), f32),
            pltpu.VMEM((groups * rows, HD), f32),
        ],
        [],
        PCOVER,
        0,
    )(*pairs, memory_sections.reshape(1, every))

    out_rows, out_cols = groups * tokens, out_weight.shape[1]
    share = out_rows // shares
    held = bf16 if memory % 16 == 0 else f32
    pieces = call(
        functools.partial(attend_kernel, groups, shares),
        [VMEM] * (groups + 5),
        [pltpu.VMEM((share, out_cols), f32 if k == 0 else bf16) for k in range(shares)],
        [
            pltpu.VMEM((every, cols), held),
            pltpu.VMEM((every, cols), held),
            pltpu.VMEM((out_rows, out_weight.shape[0]), f32),
            pltpu.VMEM((out_rows, out_cols), f32),
        ],
        2 * out_rows * out_weight.size,
        2 * out_weight.size,
    )(*kvs, *prepared, out_weight)
    summed = pieces[0]
    for bits in [*range(shares - 2, 0, -1), shares - 1]:
        summed = summed + permute(pieces[bits], "tp", bits).astype(f32)
    return summed.astype(bf16)


def solution(mesh):
    return jax.shard_map(
        body,
        mesh=mesh,
        in_specs=(
            P(("parts", "dp"), "tp"),
            P(None, None, "tp"),
            P(None, "tp"),
            P("parts"),
            P(("parts", "dp")),
            P(("parts", "dp"), "tp"),
            P(("parts", "dp"), "tp"),
            P(("parts", "dp"), "tp"),
            P(("parts", "dp"), None, "tp"),
            P(("parts", "dp"), None, "tp"),
            P(("parts", "dp")),
            P("tp", "dp"),
        ),
        out_specs=P(("parts", "tp"), "dp"),
        check_vma=False,
    )
```

```python
import functools

import jax
import jax.numpy as jnp
from jax import lax
from jax.experimental import pallas as pl
from jax.experimental.pallas import tpu as pltpu
from jax.sharding import PartitionSpec as P

D = 5120
HQ = 40
KVH = 8
HD = 128
NEW = 2
PER_HEAD = HQ // KVH
INV = 1.0 / HD**0.5

masked_score = -1e30
bf16 = jnp.bfloat16
COVER = 1 << 36
f32 = jnp.float32

TOP, TOTAL, SECTION = 0, 3, 5
STATS = 16


def nt(a, b):
    return lax.dot_general(a, b, (((1,), (1,)), ((), ())), preferred_element_type=f32)


def nn(a, b):
    return jnp.dot(a, b, preferred_element_type=f32)


def spread(blocks):
    zeros = jnp.zeros_like(blocks[0])
    rows = [
        jnp.concatenate([b if i == j else zeros for i in range(len(blocks))], axis=1)
        if len(blocks) > 1
        else b
        for j, b in enumerate(blocks)
    ]
    return jnp.concatenate(rows, axis=0)


def split(x, pieces):
    out = []
    for _ in range(pieces):
        piece = x.astype(bf16).astype(f32)
        out.append(piece)
        x = x - piece
    return out


def eye(rows, cols):
    row = lax.broadcasted_iota(jnp.int32, (rows, cols), 0)
    return (row == lax.broadcasted_iota(jnp.int32, (rows, cols), 1)).astype(f32).astype(bf16)


def up(n, to):
    return -(-n // to) * to


def open_kernel(group_ref, after, out_ref):
    out_ref[...] = jnp.full(out_ref.shape, group_ref[0].astype(f32))


def cache_kernel(lens_ref, section_ref, q_ref, nk_ref, nv_ref, ck_ref, cv_ref, out_ref):
    requests, slots, cols = ck_ref.shape
    heads = cols // HD
    tokens = requests * NEW
    per = PER_HEAD * tokens
    rows = heads * per
    row = lax.broadcasted_iota(jnp.int32, (rows, 1), 0)
    request = lax.rem(lax.div(row, NEW), requests)
    token = lax.rem(row, NEW)
    q = q_ref[...].astype(f32)
    blocks = []
    for j in range(heads):
        parts = [q[:, (j * PER_HEAD + g) * HD : (j * PER_HEAD + g + 1) * HD] for g in range(PER_HEAD)]
        blocks.append(jnp.concatenate(parts, axis=0))
    out_ref[0:rows, :] = jnp.concatenate(blocks, axis=0).astype(bf16)
    qs = spread(blocks).astype(bf16)
    fresh = lax.broadcasted_iota(jnp.int32, (rows, tokens), 1)
    seen = (lax.div(fresh, NEW) == request) & (lax.rem(fresh, NEW) <= token)
    s_new = jnp.where(seen, nt(qs, nk_ref[...]) * INV, masked_score)
    limit = jnp.full((rows, 1), lens_ref[0], jnp.int32)
    for r in range(1, requests):
        limit = jnp.where(request == r, lens_ref[r], limit)
    live = lax.broadcasted_iota(jnp.int32, (rows, slots), 1) < limit
    s = nt(qs, ck_ref[0])
    for r in range(1, requests):
        s = jnp.where(request == r, nt(qs, ck_ref[r]), s)
    s = jnp.where(live, s * INV, masked_score)

    top = jnp.maximum(jnp.max(s, axis=1, keepdims=True), jnp.max(s_new, axis=1, keepdims=True))
    p = jnp.where(live, jnp.exp(s - top), 0.0)
    p_new = jnp.where(seen, jnp.exp(s_new - top), 0.0)
    total = jnp.sum(p, axis=1, keepdims=True) + jnp.sum(p_new, axis=1, keepdims=True)
    p = p.astype(bf16)
    acc = nn(p, cv_ref[0])
    for r in range(1, requests):
        acc = jnp.where(request == r, nn(p, cv_ref[r]), acc)
    acc = acc + nn(p_new.astype(bf16).astype(f32), nv_ref[...].astype(f32))
    mine = jnp.concatenate([acc[j * per : (j + 1) * per, j * HD : (j + 1) * HD] for j in range(heads)], axis=0)
    seg = up(rows, 16)
    out_ref[seg : seg + rows, :] = (mine / total).astype(bf16)

    lane = lax.broadcasted_iota(jnp.int32, (rows, HD), 1)
    stats = jnp.where(lane == SECTION, section_ref[0:1, :], 0.0)
    for i, piece in enumerate(split(top, 3)):
        stats = jnp.where(lane == TOP + i, piece, stats)
    for i, piece in enumerate(split(total, 2)):
        stats = jnp.where(lane == TOTAL + i, piece, stats)
    if rows < HD:
        stats = jnp.concatenate([stats, jnp.zeros((HD - rows, HD), f32)], axis=0)
    out_ref[2 * seg : 2 * seg + STATS, :] = nt(eye(STATS, HD), stats.astype(bf16)).astype(bf16)


def project_kernel(bits, first, last, *refs):
    count = len(bits)
    pieces, w_ref, refs = refs[:count], refs[count], refs[count + 1 :]
    rows, depth = pieces[0].shape
    me = lax.axis_index("tp")
    if first:
        acc, squares = [None, None], None
    else:
        acc = [refs[0][s * rows : (s + 1) * rows, :] for s in range(2)]
        squares = refs[1][:, 0:1]
        refs = refs[2:]
    for k, piece in zip(bits, pieces):
        h = piece[...]
        wide = h.astype(f32)
        square = jnp.sum(wide * wide, axis=1, keepdims=True)
        squares = square if squares is None else squares + square
        at = pl.multiple_of((me ^ k) * depth, depth)
        for s in range(2):
            term = nn(h, w_ref[s, pl.ds(at, depth), :])
            acc[s] = term if acc[s] is None else acc[s] + term
    if not last:
        for s in range(2):
            refs[0][s * rows : (s + 1) * rows, :] = acc[s]
        refs[1][...] = jnp.broadcast_to(squares, refs[1].shape)
        return
    b_ref, out_ref = refs
    scale = lax.rsqrt(squares / D + 1e-06)
    for s in range(2):
        bias = b_ref[s : s + 1, :].astype(f32)
        out_ref[s * rows : (s + 1) * rows, :] = (acc[s] * scale + bias).astype(bf16)


def prepare_kernel(heads, *refs):
    parts, (section_ref, q_ref, bias_ref, old_ref, stats_ref) = refs[:-5], refs[-5:]
    groups = len(parts)
    seg = (parts[0].shape[0] - STATS) // 2
    rows = q_ref.shape[0] // groups
    per = rows // heads
    blocks = [part[0:rows, :].astype(f32) for part in parts]
    q_ref[...] = jnp.concatenate(
        [spread([b[j * per : (j + 1) * per, :] for j in range(heads)]) for b in blocks], axis=0
    ).astype(bf16)
    stats = nt(
        eye(rows, HD), jnp.concatenate([part[2 * seg : 2 * seg + STATS, :] for part in parts], axis=0)
    )

    def column(at, pieces):
        columns = []
        for k in range(groups):
            c = k * STATS + at
            columns.append(sum([stats[:, c + i : c + i + 1] for i in range(pieces)]))
        return jnp.concatenate(columns, axis=0)

    top, total = column(TOP, 3), column(TOTAL, 2)
    bias_ref[...] = jnp.where(column(SECTION, 1) == section_ref[...].astype(f32), 0.0, masked_score)
    old = jnp.concatenate([part[seg : seg + rows, :] for part in parts], axis=0).astype(f32)
    old_ref[...] = old * total
    lane = lax.broadcasted_iota(jnp.int32, stats_ref.shape, 1)
    stats_ref[...] = jnp.where(lane == 0, top, total)


def attend_kernel(groups, shares, *refs):
    kvs, (q_ref, bias_ref, old_ref, stats_ref, w_ref) = refs[:groups], refs[groups : groups + 5]
    outs = refs[groups + 5 : groups + 5 + shares]
    k_ref, v_ref, attended_ref, sums_ref = refs[groups + 5 + shares :]
    me_dp, me_tp = lax.axis_index("dp"), lax.axis_index("tp")
    memory = kvs[0].shape[0] // 2
    heads = kvs[0].shape[1] // HD
    tokens = attended_ref.shape[0] // groups
    per = PER_HEAD * tokens
    rows = heads * per
    for bits, kv in enumerate(kvs):
        first = pl.multiple_of((me_dp ^ bits) * memory, memory)
        k_ref[pl.ds(first, memory), :] = kv[0:memory, :].astype(k_ref.dtype)
        v_ref[pl.ds(first, memory), :] = kv[memory : 2 * memory, :].astype(v_ref.dtype)
    s = nt(q_ref[...], k_ref[...].astype(bf16)) * INV + bias_ref[...]
    old_top, old_total = stats_ref[:, 0:1], stats_ref[:, 1:2]
    top = jnp.maximum(jnp.max(s, axis=1, keepdims=True), old_top)
    p = jnp.exp(s - top)
    shrink = jnp.exp(old_top - top)
    total = jnp.sum(p, axis=1, keepdims=True) + shrink * old_total
    acc = nn(p.astype(bf16), v_ref[...].astype(bf16))
    for k in range(groups):
        at = pl.multiple_of((me_dp ^ k) * tokens, tokens)
        for j in range(heads):
            a = k * rows + j * per
            block = acc[a : a + per, j * HD : (j + 1) * HD] + old_ref[a : a + per, :] * shrink[a : a + per]
            block = block / total[a : a + per]
            for g in range(PER_HEAD):
                c = (j * PER_HEAD + g) * HD
                attended_ref[pl.ds(at, tokens), c : c + HD] = block[g * tokens : (g + 1) * tokens, :]
    sums_ref[...] = nn(attended_ref[...].astype(bf16), w_ref[...])
    share = sums_ref.shape[0] // shares
    for k, out in enumerate(outs):
        at = pl.multiple_of((me_tp ^ k) * share, share)
        out[...] = sums_ref[pl.ds(at, share), :].astype(out.dtype)


SMEM = pl.BlockSpec(memory_space=pltpu.SMEM)
VMEM = pl.BlockSpec(memory_space=pltpu.VMEM)
ANY = pl.BlockSpec(memory_space=pl.ANY)
HBM = pl.BlockSpec(memory_space=pltpu.HBM)
PARAMS = pltpu.CompilerParams(vmem_limit_bytes=24 * 1024 * 1024)


def call(kernel, in_specs, out_shape, scratch, flops, bytes_accessed):
    return pl.pallas_call(
        kernel,
        in_specs=in_specs,
        out_shape=out_shape,
        out_specs=jax.tree.map(lambda _: VMEM, out_shape),
        scratch_shapes=scratch,
        compiler_params=PARAMS,
        cost_estimate=pl.CostEstimate(flops=flops, bytes_accessed=bytes_accessed, transcendentals=0),
    )


def in_hbm(*arrays):
    return [pltpu.with_memory_space_constraint(x, pltpu.HBM) for x in arrays]


def permute(x, axis, bits):
    return lax.ppermute(x, axis, [(i, i ^ bits) for i in range(lax.axis_size(axis))])


def passed_on(x, near, axis):
    n = lax.axis_size(axis)
    held = {0: x}
    bit = n // 2
    while bit:
        for bits in sorted(held):
            held[bits | bit] = permute(held[bits], axis, bit)
        held[0] = near
        bit //= 2
    return [held[bits] for bits in range(n)]


def body(
    memory_hidden,
    kv_weight,
    kv_bias,
    memory_sections,
    group_sections,
    queries,
    new_keys,
    new_values,
    cache_keys,
    cache_values,
    cache_lengths,
    out_weight,
):
    groups, shares = lax.axis_size("dp"), lax.axis_size("tp")
    memory, depth = memory_hidden.shape
    requests, slots, cols = cache_keys.shape
    tokens = requests * NEW
    rows = (cols // HD) * PER_HEAD * tokens
    every = memory_sections.shape[0]

    gate = call(lambda *refs: None, [], jax.ShapeDtypeStruct((8, HD), f32), [], COVER, 0)()
    group, gate = lax.optimization_barrier((group_sections, gate))
    section = call(open_kernel, [SMEM, ANY], pltpu.VMEM((8, HD), f32), [], 1 << 10, 0)(group, gate)
    own, section = lax.optimization_barrier((memory_hidden, section))
    part = call(
        cache_kernel,
        [SMEM] + [VMEM] * 6,
        pltpu.VMEM((2 * up(rows, 16) + STATS, HD), bf16),
        [],
        4 * rows * slots * cols * requests,
        4 * requests * slots * cols,
    )(cache_lengths, section, queries, new_keys, new_values, cache_keys, cache_values)
    own_later, part = lax.optimization_barrier((own, part))
    hidden = passed_on(own, own_later, "tp")
    parts = [permute(part, "dp", bits) if bits else part for bits in range(groups)]
    near, far = list(range(shares - 1)), [shares - 1]
    partial = call(
        functools.partial(project_kernel, near, True, False),
        [VMEM] * (len(near) + 1),
        [pltpu.VMEM((2 * memory, cols), f32), pltpu.VMEM((memory, HD), f32)],
        [],
        COVER,
        4 * D * cols,
    )(*[hidden[k] for k in near], kv_weight)
    kv = call(
        functools.partial(project_kernel, far, False, True),
        [VMEM] * 5,
        pltpu.VMEM((2 * memory, cols), bf16),
        [],
        4 * memory * D * cols // shares,
        4 * D * cols // shares,
    )(hidden[far[0]], kv_weight, *partial, kv_bias)
    kv_far = permute(kv, "dp", groups // 2)
    prepared = call(
        functools.partial(prepare_kernel, cols // HD),
        [VMEM] * (groups + 1),
        [
            pltpu.VMEM((groups * rows, cols), bf16),
            pltpu.VMEM((groups * rows, every), f32),
            pltpu.VMEM((groups * rows, HD), f32),
            pltpu.VMEM((groups * rows, HD), f32),
        ],
        [],
        COVER,
        0,
    )(*parts, memory_sections.reshape(1, every))
    half = range(1, groups // 2)
    kv_on, *_ = lax.optimization_barrier((kv_far, *prepared))
    kvs = [kv, *[permute(kv, "dp", bits) for bits in half], kv_far, *[permute(kv_on, "dp", bits) for bits in half]]

    out_rows, out_cols = groups * tokens, out_weight.shape[1]
    share = out_rows // shares
    held = bf16 if memory % 16 == 0 else f32
    pieces = call(
        functools.partial(attend_kernel, groups, shares),
        [VMEM] * (groups + 5),
        [pltpu.VMEM((share, out_cols), f32 if k == 0 else bf16) for k in range(shares)],
        [
            pltpu.VMEM((every, cols), held),
            pltpu.VMEM((every, cols), held),
            pltpu.VMEM((out_rows, out_weight.shape[0]), f32),
            pltpu.VMEM((out_rows, out_cols), f32),
        ],
        2 * out_rows * out_weight.size,
        2 * out_weight.size,
    )(*kvs, *prepared, out_weight)
    summed = pieces[0]
    for bits in [*range(1, shares - 2), *range(shares - 1, shares - 3, -1)]:
        summed = summed + permute(pieces[bits], "tp", bits).astype(f32)
    return summed.astype(bf16)


def solution(mesh):
    return jax.shard_map(
        body,
        mesh=mesh,
        in_specs=(
            P(("parts", "dp"), "tp"),
            P(None, None, "tp"),
            P(None, "tp"),
            P("parts"),
            P(("parts", "dp")),
            P(("parts", "dp"), "tp"),
            P(("parts", "dp"), "tp"),
            P(("parts", "dp"), "tp"),
            P(("parts", "dp"), None, "tp"),
            P(("parts", "dp"), None, "tp"),
            P(("parts", "dp")),
            P("tp", "dp"),
        ),
        out_specs=P(("parts", "tp"), "dp"),
        check_vma=False,
    )
```

```python
import functools

import jax
import jax.numpy as jnp
from jax import lax
from jax.experimental import pallas as pl
from jax.experimental.pallas import tpu as pltpu
from jax.sharding import PartitionSpec as P

D = 5120
HQ = 40
KVH = 8
HD = 128
NEW = 2
PER_HEAD = HQ // KVH
INV = 1.0 / HD**0.5

masked_score = -1e30
bf16 = jnp.bfloat16
COVER = 1 << 36
PCOVER = 1 << 10
f32 = jnp.float32

TOP, TOTAL, SECTION = 0, 3, 5
STATS = 16


def nt(a, b):
    return lax.dot_general(a, b, (((1,), (1,)), ((), ())), preferred_element_type=f32)


def nn(a, b):
    return jnp.dot(a, b, preferred_element_type=f32)


def spread(blocks):
    zeros = jnp.zeros_like(blocks[0])
    rows = [
        jnp.concatenate([b if i == j else zeros for i in range(len(blocks))], axis=1)
        if len(blocks) > 1
        else b
        for j, b in enumerate(blocks)
    ]
    return jnp.concatenate(rows, axis=0)


def split(x, pieces):
    out = []
    for _ in range(pieces):
        piece = x.astype(bf16).astype(f32)
        out.append(piece)
        x = x - piece
    return out


def eye(rows, cols):
    row = lax.broadcasted_iota(jnp.int32, (rows, cols), 0)
    return (row == lax.broadcasted_iota(jnp.int32, (rows, cols), 1)).astype(f32).astype(bf16)


def up(n, to):
    return -(-n // to) * to


def open_kernel(group_ref, after, out_ref):
    out_ref[...] = jnp.full(out_ref.shape, group_ref[0].astype(f32))


def cache_kernel(lens_ref, section_ref, q_ref, nk_ref, nv_ref, ck_ref, cv_ref, out_ref):
    requests, slots, cols = ck_ref.shape
    heads = cols // HD
    tokens = requests * NEW
    per = PER_HEAD * tokens
    rows = heads * per
    row = lax.broadcasted_iota(jnp.int32, (rows, 1), 0)
    request = lax.rem(lax.div(row, NEW), requests)
    token = lax.rem(row, NEW)
    q = q_ref[...].astype(f32)
    blocks = []
    for j in range(heads):
        parts = [q[:, (j * PER_HEAD + g) * HD : (j * PER_HEAD + g + 1) * HD] for g in range(PER_HEAD)]
        blocks.append(jnp.concatenate(parts, axis=0))
    out_ref[0:rows, :] = jnp.concatenate(blocks, axis=0).astype(bf16)
    qs = spread(blocks).astype(bf16)
    fresh = lax.broadcasted_iota(jnp.int32, (rows, tokens), 1)
    seen = (lax.div(fresh, NEW) == request) & (lax.rem(fresh, NEW) <= token)
    s_new = jnp.where(seen, nt(qs, nk_ref[...]) * INV, masked_score)
    limit = jnp.full((rows, 1), lens_ref[0], jnp.int32)
    for r in range(1, requests):
        limit = jnp.where(request == r, lens_ref[r], limit)
    live = lax.broadcasted_iota(jnp.int32, (rows, slots), 1) < limit
    s = nt(qs, ck_ref[0])
    for r in range(1, requests):
        s = jnp.where(request == r, nt(qs, ck_ref[r]), s)
    s = jnp.where(live, s * INV, masked_score)

    top = jnp.maximum(jnp.max(s, axis=1, keepdims=True), jnp.max(s_new, axis=1, keepdims=True))
    p = jnp.where(live, jnp.exp(s - top), 0.0)
    p_new = jnp.where(seen, jnp.exp(s_new - top), 0.0)
    total = jnp.sum(p, axis=1, keepdims=True) + jnp.sum(p_new, axis=1, keepdims=True)
    p = p.astype(bf16)
    acc = nn(p, cv_ref[0])
    for r in range(1, requests):
        acc = jnp.where(request == r, nn(p, cv_ref[r]), acc)
    acc = acc + nn(p_new.astype(bf16).astype(f32), nv_ref[...].astype(f32))
    mine = jnp.concatenate([acc[j * per : (j + 1) * per, j * HD : (j + 1) * HD] for j in range(heads)], axis=0)
    seg = up(rows, 16)
    out_ref[seg : seg + rows, :] = (mine / total).astype(bf16)

    lane = lax.broadcasted_iota(jnp.int32, (rows, HD), 1)
    stats = jnp.where(lane == SECTION, section_ref[0:1, :], 0.0)
    for i, piece in enumerate(split(top, 3)):
        stats = jnp.where(lane == TOP + i, piece, stats)
    for i, piece in enumerate(split(total, 2)):
        stats = jnp.where(lane == TOTAL + i, piece, stats)
    if rows < HD:
        stats = jnp.concatenate([stats, jnp.zeros((HD - rows, HD), f32)], axis=0)
    out_ref[2 * seg : 2 * seg + STATS, :] = nt(eye(STATS, HD), stats.astype(bf16)).astype(bf16)


def project_kernel(bits, first, last, *refs):
    count = len(bits)
    pieces, w_ref, refs = refs[:count], refs[count], refs[count + 1 :]
    rows, depth = pieces[0].shape
    me = lax.axis_index("tp")
    if first:
        acc, squares = [None, None], None
    else:
        acc = [refs[0][s * rows : (s + 1) * rows, :] for s in range(2)]
        squares = refs[1][:, 0:1]
        refs = refs[2:]
    for k, piece in zip(bits, pieces):
        h = piece[...]
        wide = h.astype(f32)
        square = jnp.sum(wide * wide, axis=1, keepdims=True)
        squares = square if squares is None else squares + square
        at = pl.multiple_of((me ^ k) * depth, depth)
        for s in range(2):
            term = nn(h, w_ref[s, pl.ds(at, depth), :])
            acc[s] = term if acc[s] is None else acc[s] + term
    if not last:
        for s in range(2):
            refs[0][s * rows : (s + 1) * rows, :] = acc[s]
        refs[1][...] = jnp.broadcast_to(squares, refs[1].shape)
        return
    b_ref, out_ref = refs
    scale = lax.rsqrt(squares / D + 1e-06)
    for s in range(2):
        bias = b_ref[s : s + 1, :].astype(f32)
        out_ref[s * rows : (s + 1) * rows, :] = (acc[s] * scale + bias).astype(bf16)


def pack_kernel(kv_ref, part_ref, *refs):
    out_ref = refs[-1]
    rows, heads = kv_ref.shape[0], kv_ref.shape[1] // HD
    folded = part_ref.shape[0] // heads
    out_ref[0:rows, :] = kv_ref[...]
    for j in range(heads):
        out_ref[rows:, j * HD : (j + 1) * HD] = part_ref[j * folded : (j + 1) * folded, :]


def prepare_kernel(heads, *refs):
    parts, (section_ref, q_ref, bias_ref, old_ref, stats_ref) = list(refs[:-5]), refs[-5:]
    groups = len(parts)
    folded = parts[0].shape[0] // heads
    for k in range(groups // 2 + 1, groups):
        packed = parts[k]
        at = packed.shape[0] - folded
        parts[k] = jnp.concatenate([packed[at:, j * HD : (j + 1) * HD] for j in range(heads)], axis=0)
    rows = q_ref.shape[0] // groups
    seg = up(rows, 16)
    per = rows // heads
    blocks = [part[0:rows, :].astype(f32) for part in parts]
    q_ref[...] = jnp.concatenate(
        [spread([b[j * per : (j + 1) * per, :] for j in range(heads)]) for b in blocks], axis=0
    ).astype(bf16)
    stats = nt(
        eye(rows, HD), jnp.concatenate([part[2 * seg : 2 * seg + STATS, :] for part in parts], axis=0)
    )

    def column(at, pieces):
        columns = []
        for k in range(groups):
            c = k * STATS + at
            columns.append(sum([stats[:, c + i : c + i + 1] for i in range(pieces)]))
        return jnp.concatenate(columns, axis=0)

    top, total = column(TOP, 3), column(TOTAL, 2)
    bias_ref[...] = jnp.where(column(SECTION, 1) == section_ref[...].astype(f32), 0.0, masked_score)
    old = jnp.concatenate([part[seg : seg + rows, :] for part in parts], axis=0).astype(f32)
    old_ref[...] = old * total
    lane = lax.broadcasted_iota(jnp.int32, stats_ref.shape, 1)
    stats_ref[...] = jnp.where(lane == 0, top, total)


def attend_kernel(groups, shares, *refs):
    kvs, (q_ref, bias_ref, old_ref, stats_ref, w_ref) = refs[:groups], refs[groups : groups + 5]
    outs = refs[groups + 5 : groups + 5 + shares]
    k_ref, v_ref, attended_ref, sums_ref = refs[groups + 5 + shares :]
    me_dp, me_tp = lax.axis_index("dp"), lax.axis_index("tp")
    memory = k_ref.shape[0] // groups
    heads = kvs[0].shape[1] // HD
    tokens = attended_ref.shape[0] // groups
    per = PER_HEAD * tokens
    rows = heads * per
    for bits, kv in enumerate(kvs):
        first = pl.multiple_of((me_dp ^ bits) * memory, memory)
        k_ref[pl.ds(first, memory), :] = kv[0:memory, :].astype(k_ref.dtype)
        v_ref[pl.ds(first, memory), :] = kv[memory : 2 * memory, :].astype(v_ref.dtype)
    s = nt(q_ref[...], k_ref[...].astype(bf16)) * INV + bias_ref[...]
    old_top, old_total = stats_ref[:, 0:1], stats_ref[:, 1:2]
    top = jnp.maximum(jnp.max(s, axis=1, keepdims=True), old_top)
    p = jnp.exp(s - top)
    shrink = jnp.exp(old_top - top)
    total = jnp.sum(p, axis=1, keepdims=True) + shrink * old_total
    acc = nn(p.astype(bf16), v_ref[...].astype(bf16))
    for k in range(groups):
        at = pl.multiple_of((me_dp ^ k) * tokens, tokens)
        for j in range(heads):
            a = k * rows + j * per
            block = acc[a : a + per, j * HD : (j + 1) * HD] + old_ref[a : a + per, :] * shrink[a : a + per]
            block = block / total[a : a + per]
            for g in range(PER_HEAD):
                c = (j * PER_HEAD + g) * HD
                attended_ref[pl.ds(at, tokens), c : c + HD] = block[g * tokens : (g + 1) * tokens, :]
    sums_ref[...] = nn(attended_ref[...].astype(bf16), w_ref[...])
    share = sums_ref.shape[0] // shares
    for k, out in enumerate(outs):
        at = pl.multiple_of((me_tp ^ k) * share, share)
        out[...] = sums_ref[pl.ds(at, share), :].astype(out.dtype)


SMEM = pl.BlockSpec(memory_space=pltpu.SMEM)
VMEM = pl.BlockSpec(memory_space=pltpu.VMEM)
ANY = pl.BlockSpec(memory_space=pl.ANY)
HBM = pl.BlockSpec(memory_space=pltpu.HBM)
PARAMS = pltpu.CompilerParams(vmem_limit_bytes=24 * 1024 * 1024)


def call(kernel, in_specs, out_shape, scratch, flops, bytes_accessed):
    return pl.pallas_call(
        kernel,
        in_specs=in_specs,
        out_shape=out_shape,
        out_specs=jax.tree.map(lambda _: VMEM, out_shape),
        scratch_shapes=scratch,
        compiler_params=PARAMS,
        cost_estimate=pl.CostEstimate(flops=flops, bytes_accessed=bytes_accessed, transcendentals=0),
    )


def in_hbm(*arrays):
    return [pltpu.with_memory_space_constraint(x, pltpu.HBM) for x in arrays]


def permute(x, axis, bits):
    return lax.ppermute(x, axis, [(i, i ^ bits) for i in range(lax.axis_size(axis))])


def passed_on(x, near, axis):
    n = lax.axis_size(axis)
    held = {0: x}
    bit = n // 2
    while bit:
        for bits in sorted(held):
            held[bits | bit] = permute(held[bits], axis, bit)
        held[0] = near
        bit //= 2
    return [held[bits] for bits in range(n)]


def body(
    memory_hidden,
    kv_weight,
    kv_bias,
    memory_sections,
    group_sections,
    queries,
    new_keys,
    new_values,
    cache_keys,
    cache_values,
    cache_lengths,
    out_weight,
):
    groups, shares = lax.axis_size("dp"), lax.axis_size("tp")
    memory, depth = memory_hidden.shape
    requests, slots, cols = cache_keys.shape
    tokens = requests * NEW
    rows = (cols // HD) * PER_HEAD * tokens
    every = memory_sections.shape[0]

    gate = call(lambda *refs: None, [], jax.ShapeDtypeStruct((8, HD), f32), [], COVER, 0)()
    group, gate = lax.optimization_barrier((group_sections, gate))
    section = call(open_kernel, [SMEM, ANY], pltpu.VMEM((8, HD), f32), [], 1 << 10, 0)(group, gate)
    own, section = lax.optimization_barrier((memory_hidden, section))
    heads = cols // HD
    height = up(2 * up(rows, 16) + STATS, 16 * heads)
    part = call(
        cache_kernel,
        [SMEM] + [VMEM] * 6,
        pltpu.VMEM((height, HD), bf16),
        [],
        4 * rows * slots * cols * requests,
        4 * requests * slots * cols,
    )(cache_lengths, section, queries, new_keys, new_values, cache_keys, cache_values)
    own_later, part = lax.optimization_barrier((own, part))
    hidden = passed_on(own, own_later, "tp")
    half = range(1, groups // 2)
    part_far = permute(part, "dp", groups // 2)
    part_near = [permute(part, "dp", bits) for bits in half]
    near, far = list(range(shares - 1)), [shares - 1]
    partial = call(
        functools.partial(project_kernel, near, True, False),
        [VMEM] * (len(near) + 1),
        [pltpu.VMEM((2 * memory, cols), f32), pltpu.VMEM((memory, HD), f32)],
        [],
        COVER,
        4 * D * cols,
    )(*[hidden[k] for k in near], kv_weight)
    kv = call(
        functools.partial(project_kernel, far, False, True),
        [VMEM] * 5,
        pltpu.VMEM((2 * memory, cols), bf16),
        [],
        4 * memory * D * cols // shares,
        4 * D * cols // shares,
    )(hidden[far[0]], kv_weight, *partial, kv_bias)
    kv_far = permute(kv, "dp", groups // 2)
    packed = call(
        pack_kernel,
        [VMEM, VMEM] + [ANY] * len(part_near),
        pltpu.VMEM((2 * memory + height // heads, cols), bf16),
        [],
        COVER,
        0,
    )(kv, part_far, *part_near)
    kv_on, _ = lax.optimization_barrier((kv_far, packed))
    near = [permute(packed, "dp", bits) for bits in half]
    parts = [part, *part_near, part_far, *near]
    kvs = [kv, *near, kv_far, *[permute(kv_on, "dp", bits) for bits in half]]
    prepared = call(
        functools.partial(prepare_kernel, heads),
        [VMEM] * (groups + 1),
        [
            pltpu.VMEM((groups * rows, cols), bf16),
            pltpu.VMEM((groups * rows, every), f32),
            pltpu.VMEM((groups * rows, HD), f32),
            pltpu.VMEM((groups * rows, HD), f32),
        ],
        [],
        PCOVER,
        0,
    )(*parts, memory_sections.reshape(1, every))

    out_rows, out_cols = groups * tokens, out_weight.shape[1]
    share = out_rows // shares
    held = bf16 if memory % 16 == 0 else f32
    pieces = call(
        functools.partial(attend_kernel, groups, shares),
        [VMEM] * (groups + 5),
        [pltpu.VMEM((share, out_cols), f32 if k == 0 else bf16) for k in range(shares)],
        [
            pltpu.VMEM((every, cols), held),
            pltpu.VMEM((every, cols), held),
            pltpu.VMEM((out_rows, out_weight.shape[0]), f32),
            pltpu.VMEM((out_rows, out_cols), f32),
        ],
        2 * out_rows * out_weight.size,
        2 * out_weight.size,
    )(*kvs, *prepared, out_weight)
    summed = pieces[0]
    for bits in [*range(shares - 2, 0, -1), shares - 1]:
        summed = summed + permute(pieces[bits], "tp", bits).astype(f32)
    return summed.astype(bf16)


def solution(mesh):
    return jax.shard_map(
        body,
        mesh=mesh,
        in_specs=(
            P(("parts", "dp"), "tp"),
            P(None, None, "tp"),
            P(None, "tp"),
            P("parts"),
            P(("parts", "dp")),
            P(("parts", "dp"), "tp"),
            P(("parts", "dp"), "tp"),
            P(("parts", "dp"), "tp"),
            P(("parts", "dp"), None, "tp"),
            P(("parts", "dp"), None, "tp"),
            P(("parts", "dp")),
            P("tp", "dp"),
        ),
        out_specs=P(("parts", "tp"), "dp"),
        check_vma=False,
    )
```

```python
import functools

import jax
import jax.numpy as jnp
from jax import lax
from jax.experimental import pallas as pl
from jax.experimental.pallas import tpu as pltpu
from jax.sharding import PartitionSpec as P

D = 5120
HQ = 40
KVH = 8
HD = 128
NEW = 2
PER_HEAD = HQ // KVH
INV = 1.0 / HD**0.5

masked_score = -1e30
bf16 = jnp.bfloat16
COVER = 1 << 36
PCOVER = 1 << 10
f32 = jnp.float32

TOP, TOTAL, SECTION = 0, 3, 5
STATS = 16


def nt(a, b):
    return lax.dot_general(a, b, (((1,), (1,)), ((), ())), preferred_element_type=f32)


def nn(a, b):
    return jnp.dot(a, b, preferred_element_type=f32)


def spread(blocks):
    zeros = jnp.zeros_like(blocks[0])
    rows = [
        jnp.concatenate([b if i == j else zeros for i in range(len(blocks))], axis=1)
        if len(blocks) > 1
        else b
        for j, b in enumerate(blocks)
    ]
    return jnp.concatenate(rows, axis=0)


def split(x, pieces):
    out = []
    for _ in range(pieces):
        piece = x.astype(bf16).astype(f32)
        out.append(piece)
        x = x - piece
    return out


def eye(rows, cols):
    row = lax.broadcasted_iota(jnp.int32, (rows, cols), 0)
    return (row == lax.broadcasted_iota(jnp.int32, (rows, cols), 1)).astype(f32).astype(bf16)


def up(n, to):
    return -(-n // to) * to


def open_kernel(group_ref, after, out_ref):
    out_ref[...] = jnp.full(out_ref.shape, group_ref[0].astype(f32))


def cache_kernel(lens_ref, section_ref, q_ref, nk_ref, nv_ref, ck_ref, cv_ref, out_ref):
    requests, slots, cols = ck_ref.shape
    heads = cols // HD
    tokens = requests * NEW
    per = PER_HEAD * tokens
    rows = heads * per
    row = lax.broadcasted_iota(jnp.int32, (rows, 1), 0)
    request = lax.rem(lax.div(row, NEW), requests)
    token = lax.rem(row, NEW)
    q = q_ref[...].astype(f32)
    blocks = []
    for j in range(heads):
        parts = [q[:, (j * PER_HEAD + g) * HD : (j * PER_HEAD + g + 1) * HD] for g in range(PER_HEAD)]
        blocks.append(jnp.concatenate(parts, axis=0))
    out_ref[0:rows, :] = jnp.concatenate(blocks, axis=0).astype(bf16)
    qs = spread(blocks).astype(bf16)
    fresh = lax.broadcasted_iota(jnp.int32, (rows, tokens), 1)
    seen = (lax.div(fresh, NEW) == request) & (lax.rem(fresh, NEW) <= token)
    s_new = jnp.where(seen, nt(qs, nk_ref[...]) * INV, masked_score)
    limit = jnp.full((rows, 1), lens_ref[0], jnp.int32)
    for r in range(1, requests):
        limit = jnp.where(request == r, lens_ref[r], limit)
    live = lax.broadcasted_iota(jnp.int32, (rows, slots), 1) < limit
    s = nt(qs, ck_ref[0])
    for r in range(1, requests):
        s = jnp.where(request == r, nt(qs, ck_ref[r]), s)
    s = jnp.where(live, s * INV, masked_score)

    top = jnp.maximum(jnp.max(s, axis=1, keepdims=True), jnp.max(s_new, axis=1, keepdims=True))
    p = jnp.where(live, jnp.exp(s - top), 0.0)
    p_new = jnp.where(seen, jnp.exp(s_new - top), 0.0)
    total = jnp.sum(p, axis=1, keepdims=True) + jnp.sum(p_new, axis=1, keepdims=True)
    p = p.astype(bf16)
    acc = nn(p, cv_ref[0])
    for r in range(1, requests):
        acc = jnp.where(request == r, nn(p, cv_ref[r]), acc)
    acc = acc + nn(p_new.astype(bf16).astype(f32), nv_ref[...].astype(f32))
    mine = jnp.concatenate([acc[j * per : (j + 1) * per, j * HD : (j + 1) * HD] for j in range(heads)], axis=0)
    seg = up(rows, 16)
    out_ref[seg : seg + rows, :] = (mine / total).astype(bf16)

    lane = lax.broadcasted_iota(jnp.int32, (rows, HD), 1)
    stats = jnp.where(lane == SECTION, section_ref[0:1, :], 0.0)
    for i, piece in enumerate(split(top, 3)):
        stats = jnp.where(lane == TOP + i, piece, stats)
    for i, piece in enumerate(split(total, 2)):
        stats = jnp.where(lane == TOTAL + i, piece, stats)
    if rows < HD:
        stats = jnp.concatenate([stats, jnp.zeros((HD - rows, HD), f32)], axis=0)
    out_ref[2 * seg : 2 * seg + STATS, :] = nt(eye(STATS, HD), stats.astype(bf16)).astype(bf16)


def project_kernel(bits, first, last, *refs):
    count = len(bits)
    pieces, w_ref, refs = refs[:count], refs[count], refs[count + 1 :]
    rows, depth = pieces[0].shape
    me = lax.axis_index("tp")
    if first:
        acc, squares = [None, None], None
    else:
        acc = [refs[0][s * rows : (s + 1) * rows, :] for s in range(2)]
        squares = refs[1][:, 0:1]
        refs = refs[2:]
    for k, piece in zip(bits, pieces):
        h = piece[...]
        wide = h.astype(f32)
        square = jnp.sum(wide * wide, axis=1, keepdims=True)
        squares = square if squares is None else squares + square
        at = pl.multiple_of((me ^ k) * depth, depth)
        for s in range(2):
            term = nn(h, w_ref[s, pl.ds(at, depth), :])
            acc[s] = term if acc[s] is None else acc[s] + term
    if not last:
        for s in range(2):
            refs[0][s * rows : (s + 1) * rows, :] = acc[s]
        refs[1][...] = jnp.broadcast_to(squares, refs[1].shape)
        return
    b_ref, out_ref = refs
    scale = lax.rsqrt(squares / D + 1e-06)
    for s in range(2):
        bias = b_ref[s : s + 1, :].astype(f32)
        out_ref[s * rows : (s + 1) * rows, :] = (acc[s] * scale + bias).astype(bf16)


def pair_kernel(near_ref, far_ref, after, out_ref):
    out_ref[0] = near_ref[...]
    out_ref[1] = far_ref[...]


def prepare_kernel(heads, *refs):
    pairs, (section_ref, q_ref, bias_ref, old_ref, stats_ref) = refs[:-5], refs[-5:]
    parts = [pair.at[i] for i in range(2) for pair in pairs]
    groups = len(parts)
    seg = (parts[0].shape[0] - STATS) // 2
    rows = q_ref.shape[0] // groups
    per = rows // heads
    blocks = [part[0:rows, :].astype(f32) for part in parts]
    q_ref[...] = jnp.concatenate(
        [spread([b[j * per : (j + 1) * per, :] for j in range(heads)]) for b in blocks], axis=0
    ).astype(bf16)
    stats = nt(
        eye(rows, HD), jnp.concatenate([part[2 * seg : 2 * seg + STATS, :] for part in parts], axis=0)
    )

    def column(at, pieces):
        columns = []
        for k in range(groups):
            c = k * STATS + at
            columns.append(sum([stats[:, c + i : c + i + 1] for i in range(pieces)]))
        return jnp.concatenate(columns, axis=0)

    top, total = column(TOP, 3), column(TOTAL, 2)
    bias_ref[...] = jnp.where(column(SECTION, 1) == section_ref[...].astype(f32), 0.0, masked_score)
    old = jnp.concatenate([part[seg : seg + rows, :] for part in parts], axis=0).astype(f32)
    old_ref[...] = old * total
    lane = lax.broadcasted_iota(jnp.int32, stats_ref.shape, 1)
    stats_ref[...] = jnp.where(lane == 0, top, total)


def attend_kernel(groups, shares, *refs):
    kvs, (q_ref, bias_ref, old_ref, stats_ref, w_ref) = refs[:groups], refs[groups : groups + 5]
    outs = refs[groups + 5 : groups + 5 + shares]
    k_ref, v_ref, attended_ref, sums_ref = refs[groups + 5 + shares :]
    me_dp, me_tp = lax.axis_index("dp"), lax.axis_index("tp")
    memory = kvs[0].shape[0] // 2
    heads = kvs[0].shape[1] // HD
    tokens = attended_ref.shape[0] // groups
    per = PER_HEAD * tokens
    rows = heads * per
    for bits, kv in enumerate(kvs):
        first = pl.multiple_of((me_dp ^ bits) * memory, memory)
        k_ref[pl.ds(first, memory), :] = kv[0:memory, :].astype(k_ref.dtype)
        v_ref[pl.ds(first, memory), :] = kv[memory : 2 * memory, :].astype(v_ref.dtype)
    s = nt(q_ref[...], k_ref[...].astype(bf16)) * INV + bias_ref[...]
    old_top, old_total = stats_ref[:, 0:1], stats_ref[:, 1:2]
    top = jnp.maximum(jnp.max(s, axis=1, keepdims=True), old_top)
    p = jnp.exp(s - top)
    shrink = jnp.exp(old_top - top)
    total = jnp.sum(p, axis=1, keepdims=True) + shrink * old_total
    acc = nn(p.astype(bf16), v_ref[...].astype(bf16))
    for k in range(groups):
        at = pl.multiple_of((me_dp ^ k) * tokens, tokens)
        for j in range(heads):
            a = k * rows + j * per
            block = acc[a : a + per, j * HD : (j + 1) * HD] + old_ref[a : a + per, :] * shrink[a : a + per]
            block = block / total[a : a + per]
            for g in range(PER_HEAD):
                c = (j * PER_HEAD + g) * HD
                attended_ref[pl.ds(at, tokens), c : c + HD] = block[g * tokens : (g + 1) * tokens, :]
    sums_ref[...] = nn(attended_ref[...].astype(bf16), w_ref[...])
    share = sums_ref.shape[0] // shares
    for k, out in enumerate(outs):
        at = pl.multiple_of((me_tp ^ k) * share, share)
        out[...] = sums_ref[pl.ds(at, share), :].astype(out.dtype)


SMEM = pl.BlockSpec(memory_space=pltpu.SMEM)
VMEM = pl.BlockSpec(memory_space=pltpu.VMEM)
ANY = pl.BlockSpec(memory_space=pl.ANY)
HBM = pl.BlockSpec(memory_space=pltpu.HBM)
PARAMS = pltpu.CompilerParams(vmem_limit_bytes=24 * 1024 * 1024)


def call(kernel, in_specs, out_shape, scratch, flops, bytes_accessed):
    return pl.pallas_call(
        kernel,
        in_specs=in_specs,
        out_shape=out_shape,
        out_specs=jax.tree.map(lambda _: VMEM, out_shape),
        scratch_shapes=scratch,
        compiler_params=PARAMS,
        cost_estimate=pl.CostEstimate(flops=flops, bytes_accessed=bytes_accessed, transcendentals=0),
    )


def in_hbm(*arrays):
    return [pltpu.with_memory_space_constraint(x, pltpu.HBM) for x in arrays]


def permute(x, axis, bits):
    return lax.ppermute(x, axis, [(i, i ^ bits) for i in range(lax.axis_size(axis))])


def passed_on(x, near, axis):
    n = lax.axis_size(axis)
    held = {0: x}
    bit = n // 2
    while bit:
        for bits in sorted(held):
            held[bits | bit] = permute(held[bits], axis, bit)
        held[0] = near
        bit //= 2
    return [held[bits] for bits in range(n)]


def body(
    memory_hidden,
    kv_weight,
    kv_bias,
    memory_sections,
    group_sections,
    queries,
    new_keys,
    new_values,
    cache_keys,
    cache_values,
    cache_lengths,
    out_weight,
):
    groups, shares = lax.axis_size("dp"), lax.axis_size("tp")
    memory, depth = memory_hidden.shape
    requests, slots, cols = cache_keys.shape
    tokens = requests * NEW
    rows = (cols // HD) * PER_HEAD * tokens
    every = memory_sections.shape[0]

    gate = call(lambda *refs: None, [], jax.ShapeDtypeStruct((8, HD), f32), [], COVER, 0)()
    group, gate = lax.optimization_barrier((group_sections, gate))
    section = call(open_kernel, [SMEM, ANY], pltpu.VMEM((8, HD), f32), [], 1 << 10, 0)(group, gate)
    own, section = lax.optimization_barrier((memory_hidden, section))
    part = call(
        cache_kernel,
        [SMEM] + [VMEM] * 6,
        pltpu.VMEM((2 * up(rows, 16) + STATS, HD), bf16),
        [],
        4 * rows * slots * cols * requests,
        4 * requests * slots * cols,
    )(cache_lengths, section, queries, new_keys, new_values, cache_keys, cache_values)
    own_later, part = lax.optimization_barrier((own, part))
    hidden = passed_on(memory_hidden, own_later, "tp")
    part_far = permute(part, "dp", groups // 2)
    near, far = list(range(shares - 1)), [shares - 1]
    partial = call(
        functools.partial(project_kernel, near, True, False),
        [VMEM] * (len(near) + 1),
        [pltpu.VMEM((2 * memory, cols), f32), pltpu.VMEM((memory, HD), f32)],
        [],
        COVER,
        4 * D * cols,
    )(*[hidden[k] for k in near], kv_weight)
    kv = call(
        functools.partial(project_kernel, far, False, True),
        [VMEM] * 5,
        pltpu.VMEM((2 * memory, cols), bf16),
        [],
        4 * memory * D * cols // shares,
        4 * D * cols // shares,
    )(hidden[far[0]], kv_weight, *partial, kv_bias)
    kv_far = permute(kv, "dp", groups // 2)
    pair = call(
        pair_kernel,
        [VMEM, VMEM, ANY],
        pltpu.VMEM((2,) + part.shape, bf16),
        [],
        COVER,
        0,
    )(part, part_far, kv)
    kv_on, _ = lax.optimization_barrier((kv_far, pair))
    half = range(1, groups // 2)
    pairs = [pair, *[permute(pair, "dp", bits) for bits in half]]
    kvs = [kv, *[permute(kv, "dp", bits) for bits in half], kv_far, *[permute(kv_on, "dp", bits) for bits in half]]
    prepared = call(
        functools.partial(prepare_kernel, cols // HD),
        [VMEM] * (groups // 2 + 1),
        [
            pltpu.VMEM((groups * rows, cols), bf16),
            pltpu.VMEM((groups * rows, every), f32),
            pltpu.VMEM((groups * rows, HD), f32),
            pltpu.VMEM((groups * rows, HD), f32),
        ],
        [],
        PCOVER,
        0,
    )(*pairs, memory_sections.reshape(1, every))

    out_rows, out_cols = groups * tokens, out_weight.shape[1]
    share = out_rows // shares
    held = bf16 if memory % 16 == 0 else f32
    pieces = call(
        functools.partial(attend_kernel, groups, shares),
        [VMEM] * (groups + 5),
        [pltpu.VMEM((share, out_cols), f32 if k == 0 else bf16) for k in range(shares)],
        [
            pltpu.VMEM((every, cols), held),
            pltpu.VMEM((every, cols), held),
            pltpu.VMEM((out_rows, out_weight.shape[0]), f32),
            pltpu.VMEM((out_rows, out_cols), f32),
        ],
        2 * out_rows * out_weight.size,
        2 * out_weight.size,
    )(*kvs, *prepared, out_weight)
    summed = pieces[0]
    for bits in [*range(shares - 2, 0, -1), shares - 1]:
        summed = summed + permute(pieces[bits], "tp", bits).astype(f32)
    return summed.astype(bf16)


def solution(mesh):
    return jax.shard_map(
        body,
        mesh=mesh,
        in_specs=(
            P(("parts", "dp"), "tp"),
            P(None, None, "tp"),
            P(None, "tp"),
            P("parts"),
            P(("parts", "dp")),
            P(("parts", "dp"), "tp"),
            P(("parts", "dp"), "tp"),
            P(("parts", "dp"), "tp"),
            P(("parts", "dp"), None, "tp"),
            P(("parts", "dp"), None, "tp"),
            P(("parts", "dp")),
            P("tp", "dp"),
        ),
        out_specs=P(("parts", "tp"), "dp"),
        check_vma=False,
    )
```

```python
import functools

import jax
import jax.numpy as jnp
from jax import lax
from jax.experimental import pallas as pl
from jax.experimental.pallas import tpu as pltpu
from jax.sharding import PartitionSpec as P

D = 5120
HQ = 40
KVH = 8
HD = 128
NEW = 2
PER_HEAD = HQ // KVH
INV = 1.0 / HD**0.5

masked_score = -1e30
bf16 = jnp.bfloat16
COVER = 1 << 36
PCOVER = 1 << 10
f32 = jnp.float32

TOP, TOTAL, SECTION = 0, 3, 5
STATS = 16


def nt(a, b):
    return lax.dot_general(a, b, (((1,), (1,)), ((), ())), preferred_element_type=f32)


def nn(a, b):
    return jnp.dot(a, b, preferred_element_type=f32)


def spread(blocks):
    zeros = jnp.zeros_like(blocks[0])
    rows = [
        jnp.concatenate([b if i == j else zeros for i in range(len(blocks))], axis=1)
        if len(blocks) > 1
        else b
        for j, b in enumerate(blocks)
    ]
    return jnp.concatenate(rows, axis=0)


def split(x, pieces):
    out = []
    for _ in range(pieces):
        piece = x.astype(bf16).astype(f32)
        out.append(piece)
        x = x - piece
    return out


def eye(rows, cols):
    row = lax.broadcasted_iota(jnp.int32, (rows, cols), 0)
    return (row == lax.broadcasted_iota(jnp.int32, (rows, cols), 1)).astype(f32).astype(bf16)


def up(n, to):
    return -(-n // to) * to


def open_kernel(group_ref, after, out_ref):
    out_ref[...] = jnp.full(out_ref.shape, group_ref[0].astype(f32))


def cache_kernel(lens_ref, section_ref, q_ref, nk_ref, nv_ref, ck_ref, cv_ref, out_ref):
    requests, slots, cols = ck_ref.shape
    heads = cols // HD
    tokens = requests * NEW
    per = PER_HEAD * tokens
    rows = heads * per
    row = lax.broadcasted_iota(jnp.int32, (rows, 1), 0)
    request = lax.rem(lax.div(row, NEW), requests)
    token = lax.rem(row, NEW)
    q = q_ref[...].astype(f32)
    blocks = []
    for j in range(heads):
        parts = [q[:, (j * PER_HEAD + g) * HD : (j * PER_HEAD + g + 1) * HD] for g in range(PER_HEAD)]
        blocks.append(jnp.concatenate(parts, axis=0))
    out_ref[0:rows, :] = jnp.concatenate(blocks, axis=0).astype(bf16)
    qs = spread(blocks).astype(bf16)
    fresh = lax.broadcasted_iota(jnp.int32, (rows, tokens), 1)
    seen = (lax.div(fresh, NEW) == request) & (lax.rem(fresh, NEW) <= token)
    s_new = jnp.where(seen, nt(qs, nk_ref[...]) * INV, masked_score)
    limit = jnp.full((rows, 1), lens_ref[0], jnp.int32)
    for r in range(1, requests):
        limit = jnp.where(request == r, lens_ref[r], limit)
    live = lax.broadcasted_iota(jnp.int32, (rows, slots), 1) < limit
    s = nt(qs, ck_ref[0])
    for r in range(1, requests):
        s = jnp.where(request == r, nt(qs, ck_ref[r]), s)
    s = jnp.where(live, s * INV, masked_score)

    top = jnp.maximum(jnp.max(s, axis=1, keepdims=True), jnp.max(s_new, axis=1, keepdims=True))
    p = jnp.where(live, jnp.exp(s - top), 0.0)
    p_new = jnp.where(seen, jnp.exp(s_new - top), 0.0)
    total = jnp.sum(p, axis=1, keepdims=True) + jnp.sum(p_new, axis=1, keepdims=True)
    p = p.astype(bf16)
    acc = nn(p, cv_ref[0])
    for r in range(1, requests):
        acc = jnp.where(request == r, nn(p, cv_ref[r]), acc)
    acc = acc + nn(p_new.astype(bf16).astype(f32), nv_ref[...].astype(f32))
    mine = jnp.concatenate([acc[j * per : (j + 1) * per, j * HD : (j + 1) * HD] for j in range(heads)], axis=0)
    seg = up(rows, 16)
    out_ref[seg : seg + rows, :] = (mine / total).astype(bf16)

    lane = lax.broadcasted_iota(jnp.int32, (rows, HD), 1)
    stats = jnp.where(lane == SECTION, section_ref[0:1, :], 0.0)
    for i, piece in enumerate(split(top, 3)):
        stats = jnp.where(lane == TOP + i, piece, stats)
    for i, piece in enumerate(split(total, 2)):
        stats = jnp.where(lane == TOTAL + i, piece, stats)
    if rows < HD:
        stats = jnp.concatenate([stats, jnp.zeros((HD - rows, HD), f32)], axis=0)
    out_ref[2 * seg : 2 * seg + STATS, :] = nt(eye(STATS, HD), stats.astype(bf16)).astype(bf16)


def project_kernel(bits, first, last, *refs):
    count = len(bits)
    pieces, w_ref, refs = refs[:count], refs[count], refs[count + 1 :]
    rows, depth = pieces[0].shape
    me = lax.axis_index("tp")
    if first:
        acc, squares = [None, None], None
    else:
        acc = [refs[0][s * rows : (s + 1) * rows, :] for s in range(2)]
        squares = refs[1][:, 0:1]
        refs = refs[2:]
    for k, piece in zip(bits, pieces):
        h = piece[...]
        wide = h.astype(f32)
        square = jnp.sum(wide * wide, axis=1, keepdims=True)
        squares = square if squares is None else squares + square
        at = pl.multiple_of((me ^ k) * depth, depth)
        for s in range(2):
            term = nn(h, w_ref[s, pl.ds(at, depth), :])
            acc[s] = term if acc[s] is None else acc[s] + term
    if not last:
        for s in range(2):
            refs[0][s * rows : (s + 1) * rows, :] = acc[s]
        refs[1][...] = jnp.broadcast_to(squares, refs[1].shape)
        return
    b_ref, out_ref = refs
    scale = lax.rsqrt(squares / D + 1e-06)
    for s in range(2):
        bias = b_ref[s : s + 1, :].astype(f32)
        out_ref[s * rows : (s + 1) * rows, :] = (acc[s] * scale + bias).astype(bf16)


def pack_kernel(kv_ref, part_ref, *refs):
    out_ref = refs[-1]
    rows, heads = kv_ref.shape[0], kv_ref.shape[1] // HD
    folded = part_ref.shape[0] // heads
    out_ref[0:rows, :] = kv_ref[...]
    for j in range(heads):
        out_ref[rows:, j * HD : (j + 1) * HD] = part_ref[j * folded : (j + 1) * folded, :]


def prepare_kernel(heads, *refs):
    parts, (section_ref, q_ref, bias_ref, old_ref, stats_ref) = list(refs[:-5]), refs[-5:]
    groups = len(parts)
    folded = parts[0].shape[0] // heads
    for k in range(groups // 2 + 1, groups):
        packed = parts[k]
        at = packed.shape[0] - folded
        parts[k] = jnp.concatenate([packed[at:, j * HD : (j + 1) * HD] for j in range(heads)], axis=0)
    rows = q_ref.shape[0] // groups
    seg = up(rows, 16)
    per = rows // heads
    blocks = [part[0:rows, :].astype(f32) for part in parts]
    q_ref[...] = jnp.concatenate(
        [spread([b[j * per : (j + 1) * per, :] for j in range(heads)]) for b in blocks], axis=0
    ).astype(bf16)
    stats = nt(
        eye(rows, HD), jnp.concatenate([part[2 * seg : 2 * seg + STATS, :] for part in parts], axis=0)
    )

    def column(at, pieces):
        columns = []
        for k in range(groups):
            c = k * STATS + at
            columns.append(sum([stats[:, c + i : c + i + 1] for i in range(pieces)]))
        return jnp.concatenate(columns, axis=0)

    top, total = column(TOP, 3), column(TOTAL, 2)
    bias_ref[...] = jnp.where(column(SECTION, 1) == section_ref[...].astype(f32), 0.0, masked_score)
    old = jnp.concatenate([part[seg : seg + rows, :] for part in parts], axis=0).astype(f32)
    old_ref[...] = old * total
    lane = lax.broadcasted_iota(jnp.int32, stats_ref.shape, 1)
    stats_ref[...] = jnp.where(lane == 0, top, total)


def attend_kernel(groups, shares, *refs):
    kvs, (q_ref, bias_ref, old_ref, stats_ref, w_ref) = refs[:groups], refs[groups : groups + 5]
    outs = refs[groups + 5 : groups + 5 + shares]
    k_ref, v_ref, attended_ref, sums_ref = refs[groups + 5 + shares :]
    me_dp, me_tp = lax.axis_index("dp"), lax.axis_index("tp")
    memory = k_ref.shape[0] // groups
    heads = kvs[0].shape[1] // HD
    tokens = attended_ref.shape[0] // groups
    per = PER_HEAD * tokens
    rows = heads * per
    for bits, kv in enumerate(kvs):
        first = pl.multiple_of((me_dp ^ bits) * memory, memory)
        k_ref[pl.ds(first, memory), :] = kv[0:memory, :].astype(k_ref.dtype)
        v_ref[pl.ds(first, memory), :] = kv[memory : 2 * memory, :].astype(v_ref.dtype)
    s = nt(q_ref[...], k_ref[...].astype(bf16)) * INV + bias_ref[...]
    old_top, old_total = stats_ref[:, 0:1], stats_ref[:, 1:2]
    top = jnp.maximum(jnp.max(s, axis=1, keepdims=True), old_top)
    p = jnp.exp(s - top)
    shrink = jnp.exp(old_top - top)
    total = jnp.sum(p, axis=1, keepdims=True) + shrink * old_total
    acc = nn(p.astype(bf16), v_ref[...].astype(bf16))
    for k in range(groups):
        at = pl.multiple_of((me_dp ^ k) * tokens, tokens)
        for j in range(heads):
            a = k * rows + j * per
            block = acc[a : a + per, j * HD : (j + 1) * HD] + old_ref[a : a + per, :] * shrink[a : a + per]
            block = block / total[a : a + per]
            for g in range(PER_HEAD):
                c = (j * PER_HEAD + g) * HD
                attended_ref[pl.ds(at, tokens), c : c + HD] = block[g * tokens : (g + 1) * tokens, :]
    sums_ref[...] = nn(attended_ref[...].astype(bf16), w_ref[...])
    share = sums_ref.shape[0] // shares
    for k, out in enumerate(outs):
        at = pl.multiple_of((me_tp ^ k) * share, share)
        out[...] = sums_ref[pl.ds(at, share), :].astype(out.dtype)


SMEM = pl.BlockSpec(memory_space=pltpu.SMEM)
VMEM = pl.BlockSpec(memory_space=pltpu.VMEM)
ANY = pl.BlockSpec(memory_space=pl.ANY)
HBM = pl.BlockSpec(memory_space=pltpu.HBM)
PARAMS = pltpu.CompilerParams(vmem_limit_bytes=24 * 1024 * 1024)


def call(kernel, in_specs, out_shape, scratch, flops, bytes_accessed):
    return pl.pallas_call(
        kernel,
        in_specs=in_specs,
        out_shape=out_shape,
        out_specs=jax.tree.map(lambda _: VMEM, out_shape),
        scratch_shapes=scratch,
        compiler_params=PARAMS,
        cost_estimate=pl.CostEstimate(flops=flops, bytes_accessed=bytes_accessed, transcendentals=0),
    )


def in_hbm(*arrays):
    return [pltpu.with_memory_space_constraint(x, pltpu.HBM) for x in arrays]


def permute(x, axis, bits):
    return lax.ppermute(x, axis, [(i, i ^ bits) for i in range(lax.axis_size(axis))])


def passed_on(x, near, axis):
    n = lax.axis_size(axis)
    held = {0: x}
    bit = n // 2
    while bit:
        for bits in sorted(held):
            held[bits | bit] = permute(held[bits], axis, bit)
        held[0] = near
        bit //= 2
    return [held[bits] for bits in range(n)]


def body(
    memory_hidden,
    kv_weight,
    kv_bias,
    memory_sections,
    group_sections,
    queries,
    new_keys,
    new_values,
    cache_keys,
    cache_values,
    cache_lengths,
    out_weight,
):
    groups, shares = lax.axis_size("dp"), lax.axis_size("tp")
    memory, depth = memory_hidden.shape
    requests, slots, cols = cache_keys.shape
    tokens = requests * NEW
    rows = (cols // HD) * PER_HEAD * tokens
    every = memory_sections.shape[0]

    gate = call(lambda *refs: None, [], jax.ShapeDtypeStruct((8, HD), f32), [], COVER, 0)()
    group, gate = lax.optimization_barrier((group_sections, gate))
    section = call(open_kernel, [SMEM, ANY], pltpu.VMEM((8, HD), f32), [], 1 << 10, 0)(group, gate)
    own, section = lax.optimization_barrier((memory_hidden, section))
    heads = cols // HD
    height = up(2 * up(rows, 16) + STATS, 16 * heads)
    part = call(
        cache_kernel,
        [SMEM] + [VMEM] * 6,
        pltpu.VMEM((height, HD), bf16),
        [],
        4 * rows * slots * cols * requests,
        4 * requests * slots * cols,
    )(cache_lengths, section, queries, new_keys, new_values, cache_keys, cache_values)
    own_later, part = lax.optimization_barrier((own, part))
    hidden = passed_on(memory_hidden, own_later, "tp")
    half = range(1, groups // 2)
    part_far = permute(part, "dp", groups // 2)
    near, far = list(range(shares - 1)), [shares - 1]
    partial = call(
        functools.partial(project_kernel, near, True, False),
        [VMEM] * (len(near) + 1),
        [pltpu.VMEM((2 * memory, cols), f32), pltpu.VMEM((memory, HD), f32)],
        [],
        COVER,
        4 * D * cols,
    )(*[hidden[k] for k in near], kv_weight)
    part_later, *_ = lax.optimization_barrier((part, *partial))
    part_near = [permute(part_later, "dp", bits) for bits in half]
    kv = call(
        functools.partial(project_kernel, far, False, True),
        [VMEM] * 5,
        pltpu.VMEM((2 * memory, cols), bf16),
        [],
        4 * memory * D * cols // shares,
        4 * D * cols // shares,
    )(hidden[far[0]], kv_weight, *partial, kv_bias)
    kv_far = permute(kv, "dp", groups // 2)
    packed = call(
        pack_kernel,
        [VMEM, VMEM] + [ANY] * len(part_near),
        pltpu.VMEM((2 * memory + height // heads, cols), bf16),
        [],
        COVER,
        0,
    )(kv, part_far, *part_near)
    kv_on, _ = lax.optimization_barrier((kv_far, packed))
    near = [permute(packed, "dp", bits) for bits in half]
    parts = [part, *part_near, part_far, *near]
    kvs = [kv, *near, kv_far, *[permute(kv_on, "dp", bits) for bits in half]]
    prepared = call(
        functools.partial(prepare_kernel, heads),
        [VMEM] * (groups + 1),
        [
            pltpu.VMEM((groups * rows, cols), bf16),
            pltpu.VMEM((groups * rows, every), f32),
            pltpu.VMEM((groups * rows, HD), f32),
            pltpu.VMEM((groups * rows, HD), f32),
        ],
        [],
        PCOVER,
        0,
    )(*parts, memory_sections.reshape(1, every))

    out_rows, out_cols = groups * tokens, out_weight.shape[1]
    share = out_rows // shares
    held = bf16 if memory % 16 == 0 else f32
    pieces = call(
        functools.partial(attend_kernel, groups, shares),
        [VMEM] * (groups + 5),
        [pltpu.VMEM((share, out_cols), f32 if k == 0 else bf16) for k in range(shares)],
        [
            pltpu.VMEM((every, cols), held),
            pltpu.VMEM((every, cols), held),
            pltpu.VMEM((out_rows, out_weight.shape[0]), f32),
            pltpu.VMEM((out_rows, out_cols), f32),
        ],
        2 * out_rows * out_weight.size,
        2 * out_weight.size,
    )(*kvs, *prepared, out_weight)
    summed = pieces[0]
    for bits in [*range(shares - 2, 0, -1), shares - 1]:
        summed = summed + permute(pieces[bits], "tp", bits).astype(f32)
    return summed.astype(bf16)


def solution(mesh):
    return jax.shard_map(
        body,
        mesh=mesh,
        in_specs=(
            P(("parts", "dp"), "tp"),
            P(None, None, "tp"),
            P(None, "tp"),
            P("parts"),
            P(("parts", "dp")),
            P(("parts", "dp"), "tp"),
            P(("parts", "dp"), "tp"),
            P(("parts", "dp"), "tp"),
            P(("parts", "dp"), None, "tp"),
            P(("parts", "dp"), None, "tp"),
            P(("parts", "dp")),
            P("tp", "dp"),
        ),
        out_specs=P(("parts", "tp"), "dp"),
        check_vma=False,
    )
```

```python
import functools

import jax
import jax.numpy as jnp
from jax import lax
from jax.experimental import pallas as pl
from jax.experimental.pallas import tpu as pltpu
from jax.sharding import PartitionSpec as P

D = 5120
HQ = 40
KVH = 8
HD = 128
NEW = 2
PER_HEAD = HQ // KVH
INV = 1.0 / HD**0.5

masked_score = -1e30
bf16 = jnp.bfloat16
COVER = 1 << 36
PCOVER = 1 << 10
f32 = jnp.float32

TOP, TOTAL, SECTION = 0, 3, 5
STATS = 16


def nt(a, b):
    return lax.dot_general(a, b, (((1,), (1,)), ((), ())), preferred_element_type=f32)


def nn(a, b):
    return jnp.dot(a, b, preferred_element_type=f32)


def spread(blocks):
    zeros = jnp.zeros_like(blocks[0])
    rows = [
        jnp.concatenate([b if i == j else zeros for i in range(len(blocks))], axis=1)
        if len(blocks) > 1
        else b
        for j, b in enumerate(blocks)
    ]
    return jnp.concatenate(rows, axis=0)


def split(x, pieces):
    out = []
    for _ in range(pieces):
        piece = x.astype(bf16).astype(f32)
        out.append(piece)
        x = x - piece
    return out


def eye(rows, cols):
    row = lax.broadcasted_iota(jnp.int32, (rows, cols), 0)
    return (row == lax.broadcasted_iota(jnp.int32, (rows, cols), 1)).astype(f32).astype(bf16)


def up(n, to):
    return -(-n // to) * to


def open_kernel(group_ref, after, out_ref):
    out_ref[...] = jnp.full(out_ref.shape, group_ref[0].astype(f32))


def cache_kernel(lens_ref, section_ref, q_ref, nk_ref, nv_ref, ck_ref, cv_ref, out_ref):
    requests, slots, cols = ck_ref.shape
    heads = cols // HD
    tokens = requests * NEW
    per = PER_HEAD * tokens
    rows = heads * per
    row = lax.broadcasted_iota(jnp.int32, (rows, 1), 0)
    request = lax.rem(lax.div(row, NEW), requests)
    token = lax.rem(row, NEW)
    q = q_ref[...].astype(f32)
    blocks = []
    for j in range(heads):
        parts = [q[:, (j * PER_HEAD + g) * HD : (j * PER_HEAD + g + 1) * HD] for g in range(PER_HEAD)]
        blocks.append(jnp.concatenate(parts, axis=0))
    out_ref[0:rows, :] = jnp.concatenate(blocks, axis=0).astype(bf16)
    qs = spread(blocks).astype(bf16)
    fresh = lax.broadcasted_iota(jnp.int32, (rows, tokens), 1)
    seen = (lax.div(fresh, NEW) == request) & (lax.rem(fresh, NEW) <= token)
    s_new = jnp.where(seen, nt(qs, nk_ref[...]) * INV, masked_score)
    limit = jnp.full((rows, 1), lens_ref[0], jnp.int32)
    for r in range(1, requests):
        limit = jnp.where(request == r, lens_ref[r], limit)
    live = lax.broadcasted_iota(jnp.int32, (rows, slots), 1) < limit
    s = nt(qs, ck_ref[0])
    for r in range(1, requests):
        s = jnp.where(request == r, nt(qs, ck_ref[r]), s)
    s = jnp.where(live, s * INV, masked_score)

    top = jnp.maximum(jnp.max(s, axis=1, keepdims=True), jnp.max(s_new, axis=1, keepdims=True))
    p = jnp.where(live, jnp.exp(s - top), 0.0)
    p_new = jnp.where(seen, jnp.exp(s_new - top), 0.0)
    total = jnp.sum(p, axis=1, keepdims=True) + jnp.sum(p_new, axis=1, keepdims=True)
    p = p.astype(bf16)
    acc = nn(p, cv_ref[0])
    for r in range(1, requests):
        acc = jnp.where(request == r, nn(p, cv_ref[r]), acc)
    acc = acc + nn(p_new.astype(bf16).astype(f32), nv_ref[...].astype(f32))
    mine = jnp.concatenate([acc[j * per : (j + 1) * per, j * HD : (j + 1) * HD] for j in range(heads)], axis=0)
    seg = up(rows, 16)
    out_ref[seg : seg + rows, :] = (mine / total).astype(bf16)

    lane = lax.broadcasted_iota(jnp.int32, (rows, HD), 1)
    stats = jnp.where(lane == SECTION, section_ref[0:1, :], 0.0)
    for i, piece in enumerate(split(top, 3)):
        stats = jnp.where(lane == TOP + i, piece, stats)
    for i, piece in enumerate(split(total, 2)):
        stats = jnp.where(lane == TOTAL + i, piece, stats)
    if rows < HD:
        stats = jnp.concatenate([stats, jnp.zeros((HD - rows, HD), f32)], axis=0)
    out_ref[2 * seg : 2 * seg + STATS, :] = nt(eye(STATS, HD), stats.astype(bf16)).astype(bf16)


def project_kernel(bits, first, last, *refs):
    count = len(bits)
    pieces, w_ref, refs = refs[:count], refs[count], refs[count + 1 :]
    rows, depth = pieces[0].shape
    me = lax.axis_index("tp")
    if first:
        acc, squares = [None, None], None
    else:
        acc = [refs[0][s * rows : (s + 1) * rows, :] for s in range(2)]
        squares = refs[1][:, 0:1]
        refs = refs[2:]
    for k, piece in zip(bits, pieces):
        h = piece[...]
        wide = h.astype(f32)
        square = jnp.sum(wide * wide, axis=1, keepdims=True)
        squares = square if squares is None else squares + square
        at = pl.multiple_of((me ^ k) * depth, depth)
        for s in range(2):
            term = nn(h, w_ref[s, pl.ds(at, depth), :])
            acc[s] = term if acc[s] is None else acc[s] + term
    if not last:
        for s in range(2):
            refs[0][s * rows : (s + 1) * rows, :] = acc[s]
        refs[1][...] = jnp.broadcast_to(squares, refs[1].shape)
        return
    b_ref, out_ref = refs
    scale = lax.rsqrt(squares / D + 1e-06)
    for s in range(2):
        bias = b_ref[s : s + 1, :].astype(f32)
        out_ref[s * rows : (s + 1) * rows, :] = (acc[s] * scale + bias).astype(bf16)


def pack_kernel(kv_ref, *refs):
    part_ref, out_ref = refs[-2:]
    rows, heads = kv_ref.shape[0], kv_ref.shape[1] // HD
    folded = part_ref.shape[0] // heads
    out_ref[0:rows, :] = kv_ref[...]
    for j in range(heads):
        out_ref[rows:, j * HD : (j + 1) * HD] = part_ref[j * folded : (j + 1) * folded, :]


def prepare_kernel(heads, *refs):
    parts, (section_ref, q_ref, bias_ref, old_ref, stats_ref) = list(refs[:-5]), refs[-5:]
    groups = (len(parts) + 1) * 2 // 3
    for k in range(1, groups // 2):
        parts[k] = parts[k][...] + parts.pop(groups // 2)[...]
    folded = parts[0].shape[0] // heads
    for k in range(groups // 2 + 1, groups):
        packed = parts[k]
        at = packed.shape[0] - folded
        parts[k] = jnp.concatenate([packed[at:, j * HD : (j + 1) * HD] for j in range(heads)], axis=0)
    rows = q_ref.shape[0] // groups
    seg = up(rows, 16)
    per = rows // heads
    blocks = [part[0:rows, :].astype(f32) for part in parts]
    q_ref[...] = jnp.concatenate(
        [spread([b[j * per : (j + 1) * per, :] for j in range(heads)]) for b in blocks], axis=0
    ).astype(bf16)
    stats = nt(
        eye(rows, HD), jnp.concatenate([part[2 * seg : 2 * seg + STATS, :] for part in parts], axis=0)
    )

    def column(at, pieces):
        columns = []
        for k in range(groups):
            c = k * STATS + at
            columns.append(sum([stats[:, c + i : c + i + 1] for i in range(pieces)]))
        return jnp.concatenate(columns, axis=0)

    top, total = column(TOP, 3), column(TOTAL, 2)
    bias_ref[...] = jnp.where(column(SECTION, 1) == section_ref[...].astype(f32), 0.0, masked_score)
    old = jnp.concatenate([part[seg : seg + rows, :] for part in parts], axis=0).astype(f32)
    old_ref[...] = old * total
    lane = lax.broadcasted_iota(jnp.int32, stats_ref.shape, 1)
    stats_ref[...] = jnp.where(lane == 0, top, total)


def attend_kernel(groups, shares, *refs):
    kvs, (q_ref, bias_ref, old_ref, stats_ref, w_ref) = refs[:groups], refs[groups : groups + 5]
    outs = refs[groups + 5 : groups + 5 + shares]
    k_ref, v_ref, attended_ref, sums_ref = refs[groups + 5 + shares :]
    me_dp, me_tp = lax.axis_index("dp"), lax.axis_index("tp")
    memory = k_ref.shape[0] // groups
    heads = kvs[0].shape[1] // HD
    tokens = attended_ref.shape[0] // groups
    per = PER_HEAD * tokens
    rows = heads * per
    for bits, kv in enumerate(kvs):
        first = pl.multiple_of((me_dp ^ bits) * memory, memory)
        k_ref[pl.ds(first, memory), :] = kv[0:memory, :].astype(k_ref.dtype)
        v_ref[pl.ds(first, memory), :] = kv[memory : 2 * memory, :].astype(v_ref.dtype)
    s = nt(q_ref[...], k_ref[...].astype(bf16)) * INV + bias_ref[...]
    old_top, old_total = stats_ref[:, 0:1], stats_ref[:, 1:2]
    top = jnp.maximum(jnp.max(s, axis=1, keepdims=True), old_top)
    p = jnp.exp(s - top)
    shrink = jnp.exp(old_top - top)
    total = jnp.sum(p, axis=1, keepdims=True) + shrink * old_total
    acc = nn(p.astype(bf16), v_ref[...].astype(bf16))
    for k in range(groups):
        at = pl.multiple_of((me_dp ^ k) * tokens, tokens)
        for j in range(heads):
            a = k * rows + j * per
            block = acc[a : a + per, j * HD : (j + 1) * HD] + old_ref[a : a + per, :] * shrink[a : a + per]
            block = block / total[a : a + per]
            for g in range(PER_HEAD):
                c = (j * PER_HEAD + g) * HD
                attended_ref[pl.ds(at, tokens), c : c + HD] = block[g * tokens : (g + 1) * tokens, :]
    sums_ref[...] = nn(attended_ref[...].astype(bf16), w_ref[...])
    share = sums_ref.shape[0] // shares
    for k, out in enumerate(outs):
        at = pl.multiple_of((me_tp ^ k) * share, share)
        out[...] = sums_ref[pl.ds(at, share), :].astype(out.dtype)


SMEM = pl.BlockSpec(memory_space=pltpu.SMEM)
VMEM = pl.BlockSpec(memory_space=pltpu.VMEM)
ANY = pl.BlockSpec(memory_space=pl.ANY)
HBM = pl.BlockSpec(memory_space=pltpu.HBM)
PARAMS = pltpu.CompilerParams(vmem_limit_bytes=24 * 1024 * 1024)


def call(kernel, in_specs, out_shape, scratch, flops, bytes_accessed):
    return pl.pallas_call(
        kernel,
        in_specs=in_specs,
        out_shape=out_shape,
        out_specs=jax.tree.map(lambda _: VMEM, out_shape),
        scratch_shapes=scratch,
        compiler_params=PARAMS,
        cost_estimate=pl.CostEstimate(flops=flops, bytes_accessed=bytes_accessed, transcendentals=0),
    )


def in_hbm(*arrays):
    return [pltpu.with_memory_space_constraint(x, pltpu.HBM) for x in arrays]


def permute(x, axis, bits, among=None):
    devices = range(lax.axis_size(axis)) if among is None else among
    return lax.ppermute(x, axis, [(i, i ^ bits) for i in devices])


def passed_on(x, near, axis):
    n = lax.axis_size(axis)
    held = {0: x}
    bit = n // 2
    while bit:
        for bits in sorted(held):
            held[bits | bit] = permute(held[bits], axis, bit)
        held[0] = near
        bit //= 2
    return [held[bits] for bits in range(n)]


def body(
    memory_hidden,
    kv_weight,
    kv_bias,
    memory_sections,
    group_sections,
    queries,
    new_keys,
    new_values,
    cache_keys,
    cache_values,
    cache_lengths,
    out_weight,
):
    groups, shares = lax.axis_size("dp"), lax.axis_size("tp")
    memory, depth = memory_hidden.shape
    requests, slots, cols = cache_keys.shape
    tokens = requests * NEW
    rows = (cols // HD) * PER_HEAD * tokens
    every = memory_sections.shape[0]

    gate = call(lambda *refs: None, [], jax.ShapeDtypeStruct((8, HD), f32), [], COVER, 0)()
    group, gate = lax.optimization_barrier((group_sections, gate))
    section = call(open_kernel, [SMEM, ANY], pltpu.VMEM((8, HD), f32), [], 1 << 10, 0)(group, gate)
    own, section = lax.optimization_barrier((memory_hidden, section))
    heads = cols // HD
    height = up(2 * up(rows, 16) + STATS, 16 * heads)
    part = call(
        cache_kernel,
        [SMEM] + [VMEM] * 6,
        pltpu.VMEM((height, HD), bf16),
        [],
        4 * rows * slots * cols * requests,
        4 * requests * slots * cols,
    )(cache_lengths, section, queries, new_keys, new_values, cache_keys, cache_values)
    own_later, part = lax.optimization_barrier((own, part))
    hidden = passed_on(memory_hidden, own_later, "tp")
    half = range(1, groups // 2)
    lower, upper = range(groups // 2), range(groups // 2, groups)
    part_far = permute(part, "dp", groups // 2)
    part_near = [permute(part, "dp", bits, lower) for bits in half]
    near, far = list(range(shares - 1)), [shares - 1]
    partial = call(
        functools.partial(project_kernel, near, True, False),
        [VMEM] * (len(near) + 1),
        [pltpu.VMEM((2 * memory, cols), f32), pltpu.VMEM((memory, HD), f32)],
        [],
        COVER,
        4 * D * cols,
    )(*[hidden[k] for k in near], kv_weight)
    kv = call(
        functools.partial(project_kernel, far, False, True),
        [VMEM] * 5,
        pltpu.VMEM((2 * memory, cols), bf16),
        [],
        4 * memory * D * cols // shares,
        4 * D * cols // shares,
    )(hidden[far[0]], kv_weight, *partial, kv_bias)
    kv_far = permute(kv, "dp", groups // 2)
    packed = call(
        pack_kernel,
        [VMEM] + [ANY] * len(part_near) + [VMEM],
        pltpu.VMEM((2 * memory + height // heads, cols), bf16),
        [],
        COVER,
        0,
    )(kv, *part_near, part_far)
    kv_on, _ = lax.optimization_barrier((kv_far, packed))
    near = [permute(packed, "dp", bits) for bits in half]
    part_later, _ = lax.optimization_barrier((part, packed))
    part_late = [permute(part_later, "dp", bits, upper) for bits in half]
    parts = [part, *part_near, *part_late, part_far, *near]
    kvs = [kv, *near, kv_far, *[permute(kv_on, "dp", bits) for bits in half]]
    prepared = call(
        functools.partial(prepare_kernel, heads),
        [VMEM] * (len(parts) + 1),
        [
            pltpu.VMEM((groups * rows, cols), bf16),
            pltpu.VMEM((groups * rows, every), f32),
            pltpu.VMEM((groups * rows, HD), f32),
            pltpu.VMEM((groups * rows, HD), f32),
        ],
        [],
        PCOVER,
        0,
    )(*parts, memory_sections.reshape(1, every))

    out_rows, out_cols = groups * tokens, out_weight.shape[1]
    share = out_rows // shares
    held = bf16 if memory % 16 == 0 else f32
    pieces = call(
        functools.partial(attend_kernel, groups, shares),
        [VMEM] * (groups + 5),
        [pltpu.VMEM((share, out_cols), f32 if k == 0 else bf16) for k in range(shares)],
        [
            pltpu.VMEM((every, cols), held),
            pltpu.VMEM((every, cols), held),
            pltpu.VMEM((out_rows, out_weight.shape[0]), f32),
            pltpu.VMEM((out_rows, out_cols), f32),
        ],
        2 * out_rows * out_weight.size,
        2 * out_weight.size,
    )(*kvs, *prepared, out_weight)
    summed = pieces[0]
    for bits in [*range(1, shares - 2), *range(shares - 1, shares - 3, -1)]:
        summed = summed + permute(pieces[bits], "tp", bits).astype(f32)
    return summed.astype(bf16)


def solution(mesh):
    return jax.shard_map(
        body,
        mesh=mesh,
        in_specs=(
            P(("parts", "dp"), "tp"),
            P(None, None, "tp"),
            P(None, "tp"),
            P("parts"),
            P(("parts", "dp")),
            P(("parts", "dp"), "tp"),
            P(("parts", "dp"), "tp"),
            P(("parts", "dp"), "tp"),
            P(("parts", "dp"), None, "tp"),
            P(("parts", "dp"), None, "tp"),
            P(("parts", "dp")),
            P("tp", "dp"),
        ),
        out_specs=P(("parts", "tp"), "dp"),
        check_vma=False,
    )
```

```python
import functools

import jax
import jax.numpy as jnp
from jax import lax
from jax.experimental import pallas as pl
from jax.experimental.pallas import tpu as pltpu
from jax.sharding import PartitionSpec as P

D = 5120
HQ = 40
KVH = 8
HD = 128
NEW = 2
PER_HEAD = HQ // KVH
INV = 1.0 / HD**0.5

masked_score = -1e30
bf16 = jnp.bfloat16
COVER = 1 << 36
PCOVER = 1 << 10
f32 = jnp.float32

TOP, TOTAL, SECTION = 0, 3, 5
STATS = 16


def nt(a, b):
    return lax.dot_general(a, b, (((1,), (1,)), ((), ())), preferred_element_type=f32)


def nn(a, b):
    return jnp.dot(a, b, preferred_element_type=f32)


def spread(blocks):
    zeros = jnp.zeros_like(blocks[0])
    rows = [
        jnp.concatenate([b if i == j else zeros for i in range(len(blocks))], axis=1)
        if len(blocks) > 1
        else b
        for j, b in enumerate(blocks)
    ]
    return jnp.concatenate(rows, axis=0)


def split(x, pieces):
    out = []
    for _ in range(pieces):
        piece = x.astype(bf16).astype(f32)
        out.append(piece)
        x = x - piece
    return out


def eye(rows, cols):
    row = lax.broadcasted_iota(jnp.int32, (rows, cols), 0)
    return (row == lax.broadcasted_iota(jnp.int32, (rows, cols), 1)).astype(f32).astype(bf16)


def up(n, to):
    return -(-n // to) * to


def open_kernel(group_ref, after, out_ref):
    out_ref[...] = jnp.full(out_ref.shape, group_ref[0].astype(f32))


def cache_kernel(lens_ref, section_ref, q_ref, nk_ref, nv_ref, ck_ref, cv_ref, out_ref):
    requests, slots, cols = ck_ref.shape
    heads = cols // HD
    tokens = requests * NEW
    per = PER_HEAD * tokens
    rows = heads * per
    row = lax.broadcasted_iota(jnp.int32, (rows, 1), 0)
    request = lax.rem(lax.div(row, NEW), requests)
    token = lax.rem(row, NEW)
    q = q_ref[...].astype(f32)
    blocks = []
    for j in range(heads):
        parts = [q[:, (j * PER_HEAD + g) * HD : (j * PER_HEAD + g + 1) * HD] for g in range(PER_HEAD)]
        blocks.append(jnp.concatenate(parts, axis=0))
    out_ref[0:rows, :] = jnp.concatenate(blocks, axis=0).astype(bf16)
    qs = spread(blocks).astype(bf16)
    fresh = lax.broadcasted_iota(jnp.int32, (rows, tokens), 1)
    seen = (lax.div(fresh, NEW) == request) & (lax.rem(fresh, NEW) <= token)
    s_new = jnp.where(seen, nt(qs, nk_ref[...]) * INV, masked_score)
    limit = jnp.full((rows, 1), lens_ref[0], jnp.int32)
    for r in range(1, requests):
        limit = jnp.where(request == r, lens_ref[r], limit)
    live = lax.broadcasted_iota(jnp.int32, (rows, slots), 1) < limit
    s = nt(qs, ck_ref[0])
    for r in range(1, requests):
        s = jnp.where(request == r, nt(qs, ck_ref[r]), s)
    s = jnp.where(live, s * INV, masked_score)

    top = jnp.maximum(jnp.max(s, axis=1, keepdims=True), jnp.max(s_new, axis=1, keepdims=True))
    p = jnp.where(live, jnp.exp(s - top), 0.0)
    p_new = jnp.where(seen, jnp.exp(s_new - top), 0.0)
    total = jnp.sum(p, axis=1, keepdims=True) + jnp.sum(p_new, axis=1, keepdims=True)
    p = p.astype(bf16)
    acc = nn(p, cv_ref[0])
    for r in range(1, requests):
        acc = jnp.where(request == r, nn(p, cv_ref[r]), acc)
    acc = acc + nn(p_new.astype(bf16).astype(f32), nv_ref[...].astype(f32))
    mine = jnp.concatenate([acc[j * per : (j + 1) * per, j * HD : (j + 1) * HD] for j in range(heads)], axis=0)
    seg = up(rows, 16)
    out_ref[seg : seg + rows, :] = (mine / total).astype(bf16)

    lane = lax.broadcasted_iota(jnp.int32, (rows, HD), 1)
    stats = jnp.where(lane == SECTION, section_ref[0:1, :], 0.0)
    for i, piece in enumerate(split(top, 3)):
        stats = jnp.where(lane == TOP + i, piece, stats)
    for i, piece in enumerate(split(total, 2)):
        stats = jnp.where(lane == TOTAL + i, piece, stats)
    if rows < HD:
        stats = jnp.concatenate([stats, jnp.zeros((HD - rows, HD), f32)], axis=0)
    out_ref[2 * seg : 2 * seg + STATS, :] = nt(eye(STATS, HD), stats.astype(bf16)).astype(bf16)


def project_kernel(bits, first, last, *refs):
    count = len(bits)
    pieces, w_ref, refs = refs[:count], refs[count], refs[count + 1 :]
    rows, depth = pieces[0].shape
    me = lax.axis_index("tp")
    if first:
        acc, squares = [None, None], None
    else:
        acc = [refs[0][s * rows : (s + 1) * rows, :] for s in range(2)]
        squares = refs[1][:, 0:1]
        refs = refs[2:]
    for k, piece in zip(bits, pieces):
        h = piece[...]
        wide = h.astype(f32)
        square = jnp.sum(wide * wide, axis=1, keepdims=True)
        squares = square if squares is None else squares + square
        at = pl.multiple_of((me ^ k) * depth, depth)
        for s in range(2):
            term = nn(h, w_ref[s, pl.ds(at, depth), :])
            acc[s] = term if acc[s] is None else acc[s] + term
    if not last:
        for s in range(2):
            refs[0][s * rows : (s + 1) * rows, :] = acc[s]
        refs[1][...] = jnp.broadcast_to(squares, refs[1].shape)
        return
    b_ref, out_ref = refs
    scale = lax.rsqrt(squares / D + 1e-06)
    for s in range(2):
        bias = b_ref[s : s + 1, :].astype(f32)
        out_ref[s * rows : (s + 1) * rows, :] = (acc[s] * scale + bias).astype(bf16)


def pair_kernel(near_ref, far_ref, after, out_ref):
    out_ref[0] = near_ref[...]
    out_ref[1] = far_ref[...]


def prepare_kernel(heads, *refs):
    pairs, (section_ref, q_ref, first_bias_ref, last_bias_ref, old_ref, stats_ref) = refs[:-6], refs[-6:]
    parts = [pair.at[i] for i in range(2) for pair in pairs]
    groups = len(parts)
    seg = (parts[0].shape[0] - STATS) // 2
    rows = q_ref.shape[0] // groups
    per = rows // heads
    blocks = [part[0:rows, :].astype(f32) for part in parts]
    q_ref[...] = jnp.concatenate(
        [spread([b[j * per : (j + 1) * per, :] for j in range(heads)]) for b in blocks], axis=0
    ).astype(bf16)
    stats = nt(
        eye(rows, HD), jnp.concatenate([part[2 * seg : 2 * seg + STATS, :] for part in parts], axis=0)
    )

    def column(at, pieces):
        columns = []
        for k in range(groups):
            c = k * STATS + at
            columns.append(sum([stats[:, c + i : c + i + 1] for i in range(pieces)]))
        return jnp.concatenate(columns, axis=0)

    top, total = column(TOP, 3), column(TOTAL, 2)
    every = section_ref.shape[1]
    memory = every // groups
    sections = jnp.broadcast_to(section_ref[...].astype(f32), (8, every))
    me = lax.axis_index("dp")
    ordered = []
    for k in range(groups):
        back = lax.rem(every - (me ^ k) * memory, every)
        ordered.append(pltpu.roll(sections, back, 1)[0:1, 0:memory])
    first = groups // 2 + 1
    own_section = column(SECTION, 1)
    for bias_ref, some in ((first_bias_ref, ordered[:first]), (last_bias_ref, ordered[first:])):
        same = own_section == jnp.concatenate(some, axis=1)
        bias_ref[...] = jnp.where(same, 0.0, masked_score)
    old = jnp.concatenate([part[seg : seg + rows, :] for part in parts], axis=0).astype(f32)
    old_ref[...] = old * total
    lane = lax.broadcasted_iota(jnp.int32, stats_ref.shape, 1)
    stats_ref[...] = jnp.where(lane == 0, top, total)


def stack(blocks):
    if blocks[0].shape[0] % 16:
        return jnp.concatenate([b.astype(f32) for b in blocks], axis=0).astype(bf16)
    return jnp.concatenate(blocks, axis=0)


def join(kvs, groups, q_ref, bias_ref, old_ref, stats_ref):
    memory = kvs[0].shape[0] // 2
    heads = kvs[0].shape[1] // HD
    per = q_ref.shape[0] // (groups * heads)
    keys = stack([kv[0:memory, :] for kv in kvs])
    values = stack([kv[memory : 2 * memory, :] for kv in kvs])
    s = nt(q_ref[...], keys) * INV + bias_ref[...]
    old_top, old_total = stats_ref[:, 0:1], stats_ref[:, 1:2]
    top = jnp.maximum(jnp.max(s, axis=1, keepdims=True), old_top)
    p = jnp.exp(s - top)
    shrink = jnp.exp(old_top - top)
    total = jnp.sum(p, axis=1, keepdims=True) + shrink * old_total
    acc = nn(p.astype(bf16), values)
    own_heads = [
        acc[(k * heads + j) * per : (k * heads + j + 1) * per, j * HD : (j + 1) * HD]
        for k in range(groups)
        for j in range(heads)
    ]
    return jnp.concatenate(own_heads, axis=0) + old_ref[...] * shrink, top, total


def first_attend_kernel(groups, *refs):
    kvs, (q_ref, bias_ref, old_ref, stats_ref, out_ref, out_stats_ref) = refs[:-6], refs[-6:]
    acc, top, total = join(kvs, groups, q_ref, bias_ref, old_ref, stats_ref)
    out_ref[...] = acc
    lane = lax.broadcasted_iota(jnp.int32, out_stats_ref.shape, 1)
    out_stats_ref[...] = jnp.where(lane == 0, top, total)


def attend_kernel(count, groups, shares, *refs):
    kvs, (q_ref, bias_ref, old_ref, stats_ref, w_ref) = refs[:count], refs[count : count + 5]
    outs = refs[count + 5 : count + 5 + shares]
    attended_ref, sums_ref = refs[count + 5 + shares :]
    me_dp, me_tp = lax.axis_index("dp"), lax.axis_index("tp")
    heads = kvs[0].shape[1] // HD
    tokens = attended_ref.shape[0] // groups
    acc, _, total = join(kvs, groups, q_ref, bias_ref, old_ref, stats_ref)
    acc = acc / total
    for k in range(groups):
        at = pl.multiple_of((me_dp ^ k) * tokens, tokens)
        for c in range(heads * PER_HEAD):
            row = (k * heads * PER_HEAD + c) * tokens
            attended_ref[pl.ds(at, tokens), c * HD : (c + 1) * HD] = acc[row : row + tokens, :]
    sums_ref[...] = nn(attended_ref[...].astype(bf16), w_ref[...])
    share = sums_ref.shape[0] // shares
    for k, out in enumerate(outs):
        at = pl.multiple_of((me_tp ^ k) * share, share)
        out[...] = sums_ref[pl.ds(at, share), :].astype(out.dtype)


SMEM = pl.BlockSpec(memory_space=pltpu.SMEM)
VMEM = pl.BlockSpec(memory_space=pltpu.VMEM)
ANY = pl.BlockSpec(memory_space=pl.ANY)
HBM = pl.BlockSpec(memory_space=pltpu.HBM)
PARAMS = pltpu.CompilerParams(vmem_limit_bytes=24 * 1024 * 1024)


def call(kernel, in_specs, out_shape, scratch, flops, bytes_accessed):
    return pl.pallas_call(
        kernel,
        in_specs=in_specs,
        out_shape=out_shape,
        out_specs=jax.tree.map(lambda _: VMEM, out_shape),
        scratch_shapes=scratch,
        compiler_params=PARAMS,
        cost_estimate=pl.CostEstimate(flops=flops, bytes_accessed=bytes_accessed, transcendentals=0),
    )


def in_hbm(*arrays):
    return [pltpu.with_memory_space_constraint(x, pltpu.HBM) for x in arrays]


def permute(x, axis, bits):
    return lax.ppermute(x, axis, [(i, i ^ bits) for i in range(lax.axis_size(axis))])


def passed_on(x, near, axis):
    n = lax.axis_size(axis)
    held = {0: x}
    bit = n // 2
    while bit:
        for bits in sorted(held):
            held[bits | bit] = permute(held[bits], axis, bit)
        held[0] = near
        bit //= 2
    return [held[bits] for bits in range(n)]


def body(
    memory_hidden,
    kv_weight,
    kv_bias,
    memory_sections,
    group_sections,
    queries,
    new_keys,
    new_values,
    cache_keys,
    cache_values,
    cache_lengths,
    out_weight,
):
    groups, shares = lax.axis_size("dp"), lax.axis_size("tp")
    memory, depth = memory_hidden.shape
    requests, slots, cols = cache_keys.shape
    tokens = requests * NEW
    rows = (cols // HD) * PER_HEAD * tokens
    every = memory_sections.shape[0]

    gate = call(lambda *refs: None, [], jax.ShapeDtypeStruct((8, HD), f32), [], COVER, 0)()
    group, gate = lax.optimization_barrier((group_sections, gate))
    section = call(open_kernel, [SMEM, ANY], pltpu.VMEM((8, HD), f32), [], 1 << 10, 0)(group, gate)
    own, section = lax.optimization_barrier((memory_hidden, section))
    part = call(
        cache_kernel,
        [SMEM] + [VMEM] * 6,
        pltpu.VMEM((2 * up(rows, 16) + STATS, HD), bf16),
        [],
        4 * rows * slots * cols * requests,
        4 * requests * slots * cols,
    )(cache_lengths, section, queries, new_keys, new_values, cache_keys, cache_values)
    own_later, part = lax.optimization_barrier((own, part))
    hidden = passed_on(memory_hidden, own_later, "tp")
    part_far = permute(part, "dp", groups // 2)
    near, far = list(range(shares - 1)), [shares - 1]
    partial = call(
        functools.partial(project_kernel, near, True, False),
        [VMEM] * (len(near) + 1),
        [pltpu.VMEM((2 * memory, cols), f32), pltpu.VMEM((memory, HD), f32)],
        [],
        COVER,
        4 * D * cols,
    )(*[hidden[k] for k in near], kv_weight)
    kv = call(
        functools.partial(project_kernel, far, False, True),
        [VMEM] * 5,
        pltpu.VMEM((2 * memory, cols), bf16),
        [],
        4 * memory * D * cols // shares,
        4 * D * cols // shares,
    )(hidden[far[0]], kv_weight, *partial, kv_bias)
    kv_far = permute(kv, "dp", groups // 2)
    pair = call(
        pair_kernel,
        [VMEM, VMEM, ANY],
        pltpu.VMEM((2,) + part.shape, bf16),
        [],
        COVER,
        0,
    )(part, part_far, kv)
    kv_on, _ = lax.optimization_barrier((kv_far, pair))
    half = range(1, groups // 2)
    pairs = [pair, *[permute(pair, "dp", bits) for bits in half]]
    kvs = [kv, *[permute(kv, "dp", bits) for bits in half], kv_far, *[permute(kv_on, "dp", bits) for bits in half]]
    prepared = call(
        functools.partial(prepare_kernel, cols // HD),
        [VMEM] * (groups // 2 + 1),
        [
            pltpu.VMEM((groups * rows, cols), bf16),
            pltpu.VMEM((groups * rows, (groups // 2 + 1) * memory), f32),
            pltpu.VMEM((groups * rows, (groups // 2 - 1) * memory), f32),
            pltpu.VMEM((groups * rows, HD), f32),
            pltpu.VMEM((groups * rows, HD), f32),
        ],
        [],
        PCOVER,
        0,
    )(*pairs, memory_sections.reshape(1, every))

    out_rows, out_cols = groups * tokens, out_weight.shape[1]
    share = out_rows // shares
    asked, first_bias, last_bias, old, stats = prepared
    first = groups // 2 + 1
    old, stats = call(
        functools.partial(first_attend_kernel, groups),
        [VMEM] * (first + 4),
        [pltpu.VMEM(old.shape, f32), pltpu.VMEM(stats.shape, f32)],
        [],
        4 * groups * rows * first * memory * cols,
        4 * old.size,
    )(*kvs[:first], asked, first_bias, old, stats)
    pieces = call(
        functools.partial(attend_kernel, groups - first, groups, shares),
        [VMEM] * (groups - first + 5),
        [pltpu.VMEM((share, out_cols), f32 if k == 0 else bf16) for k in range(shares)],
        [
            pltpu.VMEM((out_rows, out_weight.shape[0]), f32),
            pltpu.VMEM((out_rows, out_cols), f32),
        ],
        2 * out_rows * out_weight.size,
        2 * out_weight.size,
    )(*kvs[first:], asked, last_bias, old, stats, out_weight)
    summed = pieces[0]
    for bits in [*range(shares // 2, shares), *range(1, shares // 2)]:
        summed = summed + permute(pieces[bits], "tp", bits).astype(f32)
    return summed.astype(bf16)


def solution(mesh):
    return jax.shard_map(
        body,
        mesh=mesh,
        in_specs=(
            P(("parts", "dp"), "tp"),
            P(None, None, "tp"),
            P(None, "tp"),
            P("parts"),
            P(("parts", "dp")),
            P(("parts", "dp"), "tp"),
            P(("parts", "dp"), "tp"),
            P(("parts", "dp"), "tp"),
            P(("parts", "dp"), None, "tp"),
            P(("parts", "dp"), None, "tp"),
            P(("parts", "dp")),
            P("tp", "dp"),
        ),
        out_specs=P(("parts", "tp"), "dp"),
        check_vma=False,
    )
```

```python
import functools

import jax
import jax.numpy as jnp
from jax import lax
from jax.experimental import pallas as pl
from jax.experimental.pallas import tpu as pltpu
from jax.sharding import PartitionSpec as P

D = 5120
HQ = 40
KVH = 8
HD = 128
NEW = 2
PER_HEAD = HQ // KVH
INV = 1.0 / HD**0.5

masked_score = -1e30
bf16 = jnp.bfloat16
COVER = 1 << 36
PCOVER = 1 << 10
f32 = jnp.float32

TOP, TOTAL, SECTION = 0, 3, 5
STATS = 16


def nt(a, b):
    return lax.dot_general(a, b, (((1,), (1,)), ((), ())), preferred_element_type=f32)


def nn(a, b):
    return jnp.dot(a, b, preferred_element_type=f32)


def spread(blocks):
    zeros = jnp.zeros_like(blocks[0])
    rows = [
        jnp.concatenate([b if i == j else zeros for i in range(len(blocks))], axis=1)
        if len(blocks) > 1
        else b
        for j, b in enumerate(blocks)
    ]
    return jnp.concatenate(rows, axis=0)


def split(x, pieces):
    out = []
    for _ in range(pieces):
        piece = x.astype(bf16).astype(f32)
        out.append(piece)
        x = x - piece
    return out


def eye(rows, cols):
    row = lax.broadcasted_iota(jnp.int32, (rows, cols), 0)
    return (row == lax.broadcasted_iota(jnp.int32, (rows, cols), 1)).astype(f32).astype(bf16)


def up(n, to):
    return -(-n // to) * to


def open_kernel(group_ref, after, out_ref):
    out_ref[...] = jnp.full(out_ref.shape, group_ref[0].astype(f32))


def cache_kernel(lens_ref, section_ref, q_ref, nk_ref, nv_ref, ck_ref, cv_ref, out_ref):
    requests, slots, cols = ck_ref.shape
    heads = cols // HD
    tokens = requests * NEW
    per = PER_HEAD * tokens
    rows = heads * per
    row = lax.broadcasted_iota(jnp.int32, (rows, 1), 0)
    request = lax.rem(lax.div(row, NEW), requests)
    token = lax.rem(row, NEW)
    q = q_ref[...].astype(f32)
    blocks = []
    for j in range(heads):
        parts = [q[:, (j * PER_HEAD + g) * HD : (j * PER_HEAD + g + 1) * HD] for g in range(PER_HEAD)]
        blocks.append(jnp.concatenate(parts, axis=0))
    out_ref[0:rows, :] = jnp.concatenate(blocks, axis=0).astype(bf16)
    qs = spread(blocks).astype(bf16)
    fresh = lax.broadcasted_iota(jnp.int32, (rows, tokens), 1)
    seen = (lax.div(fresh, NEW) == request) & (lax.rem(fresh, NEW) <= token)
    s_new = jnp.where(seen, nt(qs, nk_ref[...]) * INV, masked_score)
    limit = jnp.full((rows, 1), lens_ref[0], jnp.int32)
    for r in range(1, requests):
        limit = jnp.where(request == r, lens_ref[r], limit)
    live = lax.broadcasted_iota(jnp.int32, (rows, slots), 1) < limit
    s = nt(qs, ck_ref[0])
    for r in range(1, requests):
        s = jnp.where(request == r, nt(qs, ck_ref[r]), s)
    s = jnp.where(live, s * INV, masked_score)

    top = jnp.maximum(jnp.max(s, axis=1, keepdims=True), jnp.max(s_new, axis=1, keepdims=True))
    p = jnp.where(live, jnp.exp(s - top), 0.0)
    p_new = jnp.where(seen, jnp.exp(s_new - top), 0.0)
    total = jnp.sum(p, axis=1, keepdims=True) + jnp.sum(p_new, axis=1, keepdims=True)
    p = p.astype(bf16)
    acc = nn(p, cv_ref[0])
    for r in range(1, requests):
        acc = jnp.where(request == r, nn(p, cv_ref[r]), acc)
    acc = acc + nn(p_new.astype(bf16).astype(f32), nv_ref[...].astype(f32))
    mine = jnp.concatenate([acc[j * per : (j + 1) * per, j * HD : (j + 1) * HD] for j in range(heads)], axis=0)
    seg = up(rows, 16)
    out_ref[seg : seg + rows, :] = (mine / total).astype(bf16)

    lane = lax.broadcasted_iota(jnp.int32, (rows, HD), 1)
    stats = jnp.where(lane == SECTION, section_ref[0:1, :], 0.0)
    for i, piece in enumerate(split(top, 3)):
        stats = jnp.where(lane == TOP + i, piece, stats)
    for i, piece in enumerate(split(total, 2)):
        stats = jnp.where(lane == TOTAL + i, piece, stats)
    if rows < HD:
        stats = jnp.concatenate([stats, jnp.zeros((HD - rows, HD), f32)], axis=0)
    out_ref[2 * seg : 2 * seg + STATS, :] = nt(eye(STATS, HD), stats.astype(bf16)).astype(bf16)


def project_kernel(bits, first, last, *refs):
    count = len(bits)
    pieces, w_ref, refs = refs[:count], refs[count], refs[count + 1 :]
    rows, depth = pieces[0].shape
    me = lax.axis_index("tp")
    if first:
        acc, squares = [None, None], None
    else:
        acc = [refs[0][s * rows : (s + 1) * rows, :] for s in range(2)]
        squares = refs[1][:, 0:1]
        refs = refs[2:]
    for k, piece in zip(bits, pieces):
        h = piece[...]
        wide = h.astype(f32)
        square = jnp.sum(wide * wide, axis=1, keepdims=True)
        squares = square if squares is None else squares + square
        at = pl.multiple_of((me ^ k) * depth, depth)
        for s in range(2):
            term = nn(h, w_ref[s, pl.ds(at, depth), :])
            acc[s] = term if acc[s] is None else acc[s] + term
    if not last:
        for s in range(2):
            refs[0][s * rows : (s + 1) * rows, :] = acc[s]
        refs[1][...] = jnp.broadcast_to(squares, refs[1].shape)
        return
    b_ref, out_ref = refs
    scale = lax.rsqrt(squares / D + 1e-06)
    for s in range(2):
        bias = b_ref[s : s + 1, :].astype(f32)
        out_ref[s * rows : (s + 1) * rows, :] = (acc[s] * scale + bias).astype(bf16)


def pair_kernel(near_ref, far_ref, after, out_ref):
    out_ref[0] = near_ref[...]
    out_ref[1] = far_ref[...]


def prepare_kernel(heads, *refs):
    pairs, (section_ref, q_ref, bias_ref, old_ref, stats_ref) = refs[:-5], refs[-5:]
    parts = [pair.at[i] for i in range(2) for pair in pairs]
    groups = len(parts)
    seg = (parts[0].shape[0] - STATS) // 2
    rows = q_ref.shape[0] // groups
    per = rows // heads

    def by_head(first):
        blocks = [part[first : first + rows, :].astype(f32) for part in parts]
        return jnp.concatenate([b[j * per : (j + 1) * per, :] for j in range(heads) for b in blocks], axis=0)

    q_ref[...] = by_head(0).astype(bf16)
    stats = nt(
        eye(rows, HD), jnp.concatenate([part[2 * seg : 2 * seg + STATS, :] for part in parts], axis=0)
    )

    def column(at, pieces):
        columns = []
        for k in range(groups):
            c = k * STATS + at
            columns.append(sum([stats[:, c + i : c + i + 1] for i in range(pieces)]))
        return jnp.concatenate([c[j * per : (j + 1) * per] for j in range(heads) for c in columns], axis=0)

    top, total = column(TOP, 3), column(TOTAL, 2)
    own_section = column(SECTION, 1)[0 : groups * per]
    bias_ref[...] = jnp.where(own_section == section_ref[...].astype(f32), 0.0, masked_score)
    old_ref[...] = by_head(seg) * total
    lane = lax.broadcasted_iota(jnp.int32, stats_ref.shape, 1)
    stats_ref[...] = jnp.where(lane == 0, top, total)


def attend_kernel(groups, shares, *refs):
    kvs, (q_ref, bias_ref, old_ref, stats_ref, w_ref) = refs[:groups], refs[groups : groups + 5]
    outs = refs[groups + 5 : groups + 5 + shares]
    k_ref, v_ref, attended_ref, sums_ref = refs[groups + 5 + shares :]
    me_dp, me_tp = lax.axis_index("dp"), lax.axis_index("tp")
    memory = kvs[0].shape[0] // 2
    heads = kvs[0].shape[1] // HD
    tokens = attended_ref.shape[0] // groups
    per = PER_HEAD * tokens
    for bits, kv in enumerate(kvs):
        first = pl.multiple_of((me_dp ^ bits) * memory, memory)
        k_ref[pl.ds(first, memory), :] = kv[0:memory, :].astype(k_ref.dtype)
        v_ref[pl.ds(first, memory), :] = kv[memory : 2 * memory, :].astype(v_ref.dtype)
    some = groups * per
    sums = None
    for j in range(heads):
        at_rows, lanes = slice(j * some, (j + 1) * some), slice(j * HD, (j + 1) * HD)
        s = nt(q_ref[at_rows, :], k_ref[:, lanes].astype(bf16)) * INV + bias_ref[...]
        old_top, old_total = stats_ref[at_rows, 0:1], stats_ref[at_rows, 1:2]
        top = jnp.maximum(jnp.max(s, axis=1, keepdims=True), old_top)
        p = jnp.exp(s - top)
        shrink = jnp.exp(old_top - top)
        total = jnp.sum(p, axis=1, keepdims=True) + shrink * old_total
        acc = nn(p.astype(bf16), v_ref[:, lanes].astype(bf16))
        acc = (acc + old_ref[at_rows, :] * shrink) / total
        for k in range(groups):
            at = pl.multiple_of((me_dp ^ k) * tokens, tokens)
            for g in range(PER_HEAD):
                c = (j * PER_HEAD + g) * HD
                row = k * per + g * tokens
                attended_ref[pl.ds(at, tokens), c : c + HD] = acc[row : row + tokens, :]
        width = slice(j * PER_HEAD * HD, (j + 1) * PER_HEAD * HD)
        term = nn(attended_ref[:, width].astype(bf16), w_ref[width, :])
        sums = term if sums is None else sums + term
    sums_ref[...] = sums
    share = sums_ref.shape[0] // shares
    for k, out in enumerate(outs):
        at = pl.multiple_of((me_tp ^ k) * share, share)
        out[...] = sums_ref[pl.ds(at, share), :].astype(out.dtype)


SMEM = pl.BlockSpec(memory_space=pltpu.SMEM)
VMEM = pl.BlockSpec(memory_space=pltpu.VMEM)
ANY = pl.BlockSpec(memory_space=pl.ANY)
HBM = pl.BlockSpec(memory_space=pltpu.HBM)
PARAMS = pltpu.CompilerParams(vmem_limit_bytes=24 * 1024 * 1024)


def call(kernel, in_specs, out_shape, scratch, flops, bytes_accessed):
    return pl.pallas_call(
        kernel,
        in_specs=in_specs,
        out_shape=out_shape,
        out_specs=jax.tree.map(lambda _: VMEM, out_shape),
        scratch_shapes=scratch,
        compiler_params=PARAMS,
        cost_estimate=pl.CostEstimate(flops=flops, bytes_accessed=bytes_accessed, transcendentals=0),
    )


def in_hbm(*arrays):
    return [pltpu.with_memory_space_constraint(x, pltpu.HBM) for x in arrays]


def permute(x, axis, bits):
    return lax.ppermute(x, axis, [(i, i ^ bits) for i in range(lax.axis_size(axis))])


def passed_on(x, near, axis):
    n = lax.axis_size(axis)
    held = {0: x}
    bit = n // 2
    while bit:
        for bits in sorted(held):
            held[bits | bit] = permute(held[bits], axis, bit)
        held[0] = near
        bit //= 2
    return [held[bits] for bits in range(n)]


def body(
    memory_hidden,
    kv_weight,
    kv_bias,
    memory_sections,
    group_sections,
    queries,
    new_keys,
    new_values,
    cache_keys,
    cache_values,
    cache_lengths,
    out_weight,
):
    groups, shares = lax.axis_size("dp"), lax.axis_size("tp")
    memory, depth = memory_hidden.shape
    requests, slots, cols = cache_keys.shape
    tokens = requests * NEW
    rows = (cols // HD) * PER_HEAD * tokens
    every = memory_sections.shape[0]

    gate = call(lambda *refs: None, [], jax.ShapeDtypeStruct((8, HD), f32), [], COVER, 0)()
    group, gate = lax.optimization_barrier((group_sections, gate))
    section = call(open_kernel, [SMEM, ANY], pltpu.VMEM((8, HD), f32), [], 1 << 10, 0)(group, gate)
    own, section = lax.optimization_barrier((memory_hidden, section))
    part = call(
        cache_kernel,
        [SMEM] + [VMEM] * 6,
        pltpu.VMEM((2 * up(rows, 16) + STATS, HD), bf16),
        [],
        4 * rows * slots * cols * requests,
        4 * requests * slots * cols,
    )(cache_lengths, section, queries, new_keys, new_values, cache_keys, cache_values)
    own_later, part = lax.optimization_barrier((own, part))
    hidden = passed_on(memory_hidden, own_later, "tp")
    part_far = permute(part, "dp", groups // 2)
    near, far = list(range(shares - 1)), [shares - 1]
    partial = call(
        functools.partial(project_kernel, near, True, False),
        [VMEM] * (len(near) + 1),
        [pltpu.VMEM((2 * memory, cols), f32), pltpu.VMEM((memory, HD), f32)],
        [],
        COVER,
        4 * D * cols,
    )(*[hidden[k] for k in near], kv_weight)
    kv = call(
        functools.partial(project_kernel, far, False, True),
        [VMEM] * 5,
        pltpu.VMEM((2 * memory, cols), bf16),
        [],
        4 * memory * D * cols // shares,
        4 * D * cols // shares,
    )(hidden[far[0]], kv_weight, *partial, kv_bias)
    kv_far = permute(kv, "dp", groups // 2)
    pair = call(
        pair_kernel,
        [VMEM, VMEM, ANY],
        pltpu.VMEM((2,) + part.shape, bf16),
        [],
        COVER,
        0,
    )(part, part_far, kv)
    kv_on, _ = lax.optimization_barrier((kv_far, pair))
    half = range(1, groups // 2)
    pairs = [pair, *[permute(pair, "dp", bits) for bits in half]]
    kvs = [kv, *[permute(kv, "dp", bits) for bits in half], kv_far, *[permute(kv_on, "dp", bits) for bits in half]]
    heads = cols // HD
    prepared = call(
        functools.partial(prepare_kernel, heads),
        [VMEM] * (groups // 2 + 1),
        [
            pltpu.VMEM((groups * rows, HD), bf16),
            pltpu.VMEM((groups * rows // heads, every), f32),
            pltpu.VMEM((groups * rows, HD), f32),
            pltpu.VMEM((groups * rows, HD), f32),
        ],
        [],
        PCOVER,
        0,
    )(*pairs, memory_sections.reshape(1, every))

    out_rows, out_cols = groups * tokens, out_weight.shape[1]
    share = out_rows // shares
    held = bf16 if memory % 16 == 0 else f32
    pieces = call(
        functools.partial(attend_kernel, groups, shares),
        [VMEM] * (groups + 5),
        [pltpu.VMEM((share, out_cols), f32 if k == 0 else bf16) for k in range(shares)],
        [
            pltpu.VMEM((every, cols), held),
            pltpu.VMEM((every, cols), held),
            pltpu.VMEM((out_rows, out_weight.shape[0]), f32),
            pltpu.VMEM((out_rows, out_cols), f32),
        ],
        2 * out_rows * out_weight.size,
        2 * out_weight.size,
    )(*kvs, *prepared, out_weight)
    summed = pieces[0]
    for bits in [*range(shares - 2, 0, -1), shares - 1]:
        summed = summed + permute(pieces[bits], "tp", bits).astype(f32)
    return summed.astype(bf16)


def solution(mesh):
    return jax.shard_map(
        body,
        mesh=mesh,
        in_specs=(
            P(("parts", "dp"), "tp"),
            P(None, None, "tp"),
            P(None, "tp"),
            P("parts"),
            P(("parts", "dp")),
            P(("parts", "dp"), "tp"),
            P(("parts", "dp"), "tp"),
            P(("parts", "dp"), "tp"),
            P(("parts", "dp"), None, "tp"),
            P(("parts", "dp"), None, "tp"),
            P(("parts", "dp")),
            P("tp", "dp"),
        ),
        out_specs=P(("parts", "tp"), "dp"),
        check_vma=False,
    )
```

```python
import functools

import jax
import jax.numpy as jnp
from jax import lax
from jax.experimental import pallas as pl
from jax.experimental.pallas import tpu as pltpu
from jax.sharding import PartitionSpec as P

D = 5120
HQ = 40
KVH = 8
HD = 128
NEW = 2
PER_HEAD = HQ // KVH
INV = 1.0 / HD**0.5

masked_score = -1e30
bf16 = jnp.bfloat16
COVER = 1 << 36
PCOVER = 1 << 10
f32 = jnp.float32

TOP, TOTAL, SECTION = 0, 3, 5
STATS = 16


def nt(a, b):
    return lax.dot_general(a, b, (((1,), (1,)), ((), ())), preferred_element_type=f32)


def nn(a, b):
    return jnp.dot(a, b, preferred_element_type=f32)


def spread(blocks):
    zeros = jnp.zeros_like(blocks[0])
    rows = [
        jnp.concatenate([b if i == j else zeros for i in range(len(blocks))], axis=1)
        if len(blocks) > 1
        else b
        for j, b in enumerate(blocks)
    ]
    return jnp.concatenate(rows, axis=0)


def split(x, pieces):
    out = []
    for _ in range(pieces):
        piece = x.astype(bf16).astype(f32)
        out.append(piece)
        x = x - piece
    return out


def eye(rows, cols):
    row = lax.broadcasted_iota(jnp.int32, (rows, cols), 0)
    return (row == lax.broadcasted_iota(jnp.int32, (rows, cols), 1)).astype(f32).astype(bf16)


def up(n, to):
    return -(-n // to) * to


def open_kernel(group_ref, after, out_ref):
    out_ref[...] = jnp.full(out_ref.shape, group_ref[0].astype(f32))


def cache_kernel(lens_ref, section_ref, q_ref, nk_ref, nv_ref, ck_ref, cv_ref, out_ref):
    requests, slots, cols = ck_ref.shape
    heads = cols // HD
    tokens = requests * NEW
    per = PER_HEAD * tokens
    rows = heads * per
    row = lax.broadcasted_iota(jnp.int32, (rows, 1), 0)
    request = lax.rem(lax.div(row, NEW), requests)
    token = lax.rem(row, NEW)
    q = q_ref[...].astype(f32)
    blocks = []
    for j in range(heads):
        parts = [q[:, (j * PER_HEAD + g) * HD : (j * PER_HEAD + g + 1) * HD] for g in range(PER_HEAD)]
        blocks.append(jnp.concatenate(parts, axis=0))
    out_ref[0:rows, :] = jnp.concatenate(blocks, axis=0).astype(bf16)
    qs = spread(blocks).astype(bf16)
    fresh = lax.broadcasted_iota(jnp.int32, (rows, tokens), 1)
    seen = (lax.div(fresh, NEW) == request) & (lax.rem(fresh, NEW) <= token)
    s_new = jnp.where(seen, nt(qs, nk_ref[...]) * INV, masked_score)
    limit = jnp.full((rows, 1), lens_ref[0], jnp.int32)
    for r in range(1, requests):
        limit = jnp.where(request == r, lens_ref[r], limit)
    live = lax.broadcasted_iota(jnp.int32, (rows, slots), 1) < limit
    s = nt(qs, ck_ref[0])
    for r in range(1, requests):
        s = jnp.where(request == r, nt(qs, ck_ref[r]), s)
    s = jnp.where(live, s * INV, masked_score)

    top = jnp.maximum(jnp.max(s, axis=1, keepdims=True), jnp.max(s_new, axis=1, keepdims=True))
    p = jnp.where(live, jnp.exp(s - top), 0.0)
    p_new = jnp.where(seen, jnp.exp(s_new - top), 0.0)
    total = jnp.sum(p, axis=1, keepdims=True) + jnp.sum(p_new, axis=1, keepdims=True)
    p = p.astype(bf16)
    acc = nn(p, cv_ref[0])
    for r in range(1, requests):
        acc = jnp.where(request == r, nn(p, cv_ref[r]), acc)
    acc = acc + nn(p_new.astype(bf16).astype(f32), nv_ref[...].astype(f32))
    mine = jnp.concatenate([acc[j * per : (j + 1) * per, j * HD : (j + 1) * HD] for j in range(heads)], axis=0)
    seg = up(rows, 16)
    out_ref[seg : seg + rows, :] = (mine / total).astype(bf16)

    lane = lax.broadcasted_iota(jnp.int32, (rows, HD), 1)
    stats = jnp.where(lane == SECTION, section_ref[0:1, :], 0.0)
    for i, piece in enumerate(split(top, 3)):
        stats = jnp.where(lane == TOP + i, piece, stats)
    for i, piece in enumerate(split(total, 2)):
        stats = jnp.where(lane == TOTAL + i, piece, stats)
    if rows < HD:
        stats = jnp.concatenate([stats, jnp.zeros((HD - rows, HD), f32)], axis=0)
    out_ref[2 * seg : 2 * seg + STATS, :] = nt(eye(STATS, HD), stats.astype(bf16)).astype(bf16)


def project_kernel(bits, first, last, *refs):
    count = len(bits)
    pieces, w_ref, refs = refs[:count], refs[count], refs[count + 1 :]
    rows, depth = pieces[0].shape
    me = lax.axis_index("tp")
    if first:
        acc, squares = [None, None], None
    else:
        acc = [refs[0][s * rows : (s + 1) * rows, :] for s in range(2)]
        squares = refs[1][:, 0:1]
        refs = refs[2:]
    for k, piece in zip(bits, pieces):
        h = piece[...]
        wide = h.astype(f32)
        square = jnp.sum(wide * wide, axis=1, keepdims=True)
        squares = square if squares is None else squares + square
        at = pl.multiple_of((me ^ k) * depth, depth)
        for s in range(2):
            term = nn(h, w_ref[s, pl.ds(at, depth), :])
            acc[s] = term if acc[s] is None else acc[s] + term
    if not last:
        for s in range(2):
            refs[0][s * rows : (s + 1) * rows, :] = acc[s]
        refs[1][...] = jnp.broadcast_to(squares, refs[1].shape)
        return
    b_ref, out_ref = refs
    scale = lax.rsqrt(squares / D + 1e-06)
    for s in range(2):
        bias = b_ref[s : s + 1, :].astype(f32)
        out_ref[s * rows : (s + 1) * rows, :] = (acc[s] * scale + bias).astype(bf16)


def pair_kernel(near_ref, far_ref, after, out_ref):
    out_ref[0] = near_ref[...]
    out_ref[1] = far_ref[...]


def prepare_kernel(heads, *refs):
    pairs, (section_ref, q_ref, bias_ref, old_ref, stats_ref) = refs[:-5], refs[-5:]
    parts = [pair.at[i] for i in range(2) for pair in pairs]
    groups = len(parts)
    seg = (parts[0].shape[0] - STATS) // 2
    rows = q_ref.shape[0] // groups
    per = rows // heads

    def by_head(first):
        blocks = [part[first : first + rows, :].astype(f32) for part in parts]
        return jnp.concatenate([b[j * per : (j + 1) * per, :] for j in range(heads) for b in blocks], axis=0)

    q_ref[...] = by_head(0).astype(bf16)
    stats = nt(
        eye(rows, HD), jnp.concatenate([part[2 * seg : 2 * seg + STATS, :] for part in parts], axis=0)
    )

    def column(at, pieces):
        columns = []
        for k in range(groups):
            c = k * STATS + at
            columns.append(sum([stats[:, c + i : c + i + 1] for i in range(pieces)]))
        return jnp.concatenate([c[j * per : (j + 1) * per] for j in range(heads) for c in columns], axis=0)

    top, total = column(TOP, 3), column(TOTAL, 2)
    every = section_ref.shape[1]
    memory = every // groups
    sections = jnp.broadcast_to(section_ref[...].astype(f32), (8, every))
    me = lax.axis_index("dp")
    held = []
    for k in range(groups):
        back = lax.rem(every - (me ^ k) * memory, every)
        held.append(pltpu.roll(sections, back, 1)[0:1, 0:memory])
    own_section = column(SECTION, 1)[0 : groups * per]
    bias_ref[...] = jnp.where(own_section == jnp.concatenate(held, axis=1), 0.0, masked_score)
    old_ref[...] = by_head(seg) * total
    lane = lax.broadcasted_iota(jnp.int32, stats_ref.shape, 1)
    stats_ref[...] = jnp.where(lane == 0, top, total)


def stack(blocks):
    if blocks[0].shape[0] % 16:
        return jnp.concatenate([b.astype(f32) for b in blocks], axis=0).astype(bf16)
    return jnp.concatenate(blocks, axis=0)


def attend_kernel(groups, shares, *refs):
    kvs, (q_ref, bias_ref, old_ref, stats_ref, w_ref) = refs[:groups], refs[groups : groups + 5]
    outs = refs[groups + 5 : groups + 5 + shares]
    attended_ref, sums_ref = refs[groups + 5 + shares :]
    me_dp, me_tp = lax.axis_index("dp"), lax.axis_index("tp")
    memory = kvs[0].shape[0] // 2
    heads = kvs[0].shape[1] // HD
    tokens = attended_ref.shape[0] // groups
    per = PER_HEAD * tokens
    some = groups * per
    scores = []
    for j in range(heads):
        keys = stack([kv[0:memory, j * HD : (j + 1) * HD] for kv in kvs])
        scores.append(nt(q_ref[j * some : (j + 1) * some, :], keys))
    sums = None
    for j, s in enumerate(scores):
        at_rows = slice(j * some, (j + 1) * some)
        s = s * INV + bias_ref[...]
        old_top, old_total = stats_ref[at_rows, 0:1], stats_ref[at_rows, 1:2]
        top = jnp.maximum(jnp.max(s, axis=1, keepdims=True), old_top)
        p = jnp.exp(s - top)
        shrink = jnp.exp(old_top - top)
        total = jnp.sum(p, axis=1, keepdims=True) + shrink * old_total
        values = stack([kv[memory : 2 * memory, j * HD : (j + 1) * HD] for kv in kvs])
        acc = nn(p.astype(bf16), values)
        acc = (acc + old_ref[at_rows, :] * shrink) / total
        for k in range(groups):
            at = pl.multiple_of((me_dp ^ k) * tokens, tokens)
            for g in range(PER_HEAD):
                c = (j * PER_HEAD + g) * HD
                row = k * per + g * tokens
                attended_ref[pl.ds(at, tokens), c : c + HD] = acc[row : row + tokens, :]
        width = slice(j * PER_HEAD * HD, (j + 1) * PER_HEAD * HD)
        term = nn(attended_ref[:, width].astype(bf16), w_ref[width, :])
        sums = term if sums is None else sums + term
    sums_ref[...] = sums
    share = sums_ref.shape[0] // shares
    for k, out in enumerate(outs):
        at = pl.multiple_of((me_tp ^ k) * share, share)
        out[...] = sums_ref[pl.ds(at, share), :].astype(out.dtype)


SMEM = pl.BlockSpec(memory_space=pltpu.SMEM)
VMEM = pl.BlockSpec(memory_space=pltpu.VMEM)
ANY = pl.BlockSpec(memory_space=pl.ANY)
HBM = pl.BlockSpec(memory_space=pltpu.HBM)
PARAMS = pltpu.CompilerParams(vmem_limit_bytes=24 * 1024 * 1024)


def call(kernel, in_specs, out_shape, scratch, flops, bytes_accessed):
    return pl.pallas_call(
        kernel,
        in_specs=in_specs,
        out_shape=out_shape,
        out_specs=jax.tree.map(lambda _: VMEM, out_shape),
        scratch_shapes=scratch,
        compiler_params=PARAMS,
        cost_estimate=pl.CostEstimate(flops=flops, bytes_accessed=bytes_accessed, transcendentals=0),
    )


def in_hbm(*arrays):
    return [pltpu.with_memory_space_constraint(x, pltpu.HBM) for x in arrays]


def permute(x, axis, bits):
    return lax.ppermute(x, axis, [(i, i ^ bits) for i in range(lax.axis_size(axis))])


def passed_on(x, near, axis):
    n = lax.axis_size(axis)
    held = {0: x}
    bit = n // 2
    while bit:
        for bits in sorted(held):
            held[bits | bit] = permute(held[bits], axis, bit)
        held[0] = near
        bit //= 2
    return [held[bits] for bits in range(n)]


def body(
    memory_hidden,
    kv_weight,
    kv_bias,
    memory_sections,
    group_sections,
    queries,
    new_keys,
    new_values,
    cache_keys,
    cache_values,
    cache_lengths,
    out_weight,
):
    groups, shares = lax.axis_size("dp"), lax.axis_size("tp")
    memory, depth = memory_hidden.shape
    requests, slots, cols = cache_keys.shape
    tokens = requests * NEW
    rows = (cols // HD) * PER_HEAD * tokens
    every = memory_sections.shape[0]

    gate = call(lambda *refs: None, [], jax.ShapeDtypeStruct((8, HD), f32), [], COVER, 0)()
    group, gate = lax.optimization_barrier((group_sections, gate))
    section = call(open_kernel, [SMEM, ANY], pltpu.VMEM((8, HD), f32), [], 1 << 10, 0)(group, gate)
    own, section = lax.optimization_barrier((memory_hidden, section))
    part = call(
        cache_kernel,
        [SMEM] + [VMEM] * 6,
        pltpu.VMEM((2 * up(rows, 16) + STATS, HD), bf16),
        [],
        4 * rows * slots * cols * requests,
        4 * requests * slots * cols,
    )(cache_lengths, section, queries, new_keys, new_values, cache_keys, cache_values)
    own_later, part = lax.optimization_barrier((own, part))
    hidden = passed_on(memory_hidden, own_later, "tp")
    part_far = permute(part, "dp", groups // 2)
    near, far = list(range(shares - 1)), [shares - 1]
    partial = call(
        functools.partial(project_kernel, near, True, False),
        [VMEM] * (len(near) + 1),
        [pltpu.VMEM((2 * memory, cols), f32), pltpu.VMEM((memory, HD), f32)],
        [],
        COVER,
        4 * D * cols,
    )(*[hidden[k] for k in near], kv_weight)
    kv = call(
        functools.partial(project_kernel, far, False, True),
        [VMEM] * 5,
        pltpu.VMEM((2 * memory, cols), bf16),
        [],
        4 * memory * D * cols // shares,
        4 * D * cols // shares,
    )(hidden[far[0]], kv_weight, *partial, kv_bias)
    kv_far = permute(kv, "dp", groups // 2)
    pair = call(
        pair_kernel,
        [VMEM, VMEM, ANY],
        pltpu.VMEM((2,) + part.shape, bf16),
        [],
        COVER,
        0,
    )(part, part_far, kv)
    kv_on, _ = lax.optimization_barrier((kv_far, pair))
    half = range(1, groups // 2)
    pairs = [pair, *[permute(pair, "dp", bits) for bits in half]]
    kvs = [kv, *[permute(kv, "dp", bits) for bits in half], kv_far, *[permute(kv_on, "dp", bits) for bits in half]]
    heads = cols // HD
    prepared = call(
        functools.partial(prepare_kernel, heads),
        [VMEM] * (groups // 2 + 1),
        [
            pltpu.VMEM((groups * rows, HD), bf16),
            pltpu.VMEM((groups * rows // heads, every), f32),
            pltpu.VMEM((groups * rows, HD), f32),
            pltpu.VMEM((groups * rows, HD), f32),
        ],
        [],
        PCOVER,
        0,
    )(*pairs, memory_sections.reshape(1, every))

    out_rows, out_cols = groups * tokens, out_weight.shape[1]
    share = out_rows // shares
    pieces = call(
        functools.partial(attend_kernel, groups, shares),
        [VMEM] * (groups + 5),
        [pltpu.VMEM((share, out_cols), f32 if k == 0 else bf16) for k in range(shares)],
        [
            pltpu.VMEM((out_rows, out_weight.shape[0]), f32),
            pltpu.VMEM((out_rows, out_cols), f32),
        ],
        2 * out_rows * out_weight.size,
        2 * out_weight.size,
    )(*kvs, *prepared, out_weight)
    summed = pieces[0]
    for bits in [*range(shares - 2, 0, -1), shares - 1]:
        summed = summed + permute(pieces[bits], "tp", bits).astype(f32)
    return summed.astype(bf16)


def solution(mesh):
    return jax.shard_map(
        body,
        mesh=mesh,
        in_specs=(
            P(("parts", "dp"), "tp"),
            P(None, None, "tp"),
            P(None, "tp"),
            P("parts"),
            P(("parts", "dp")),
            P(("parts", "dp"), "tp"),
            P(("parts", "dp"), "tp"),
            P(("parts", "dp"), "tp"),
            P(("parts", "dp"), None, "tp"),
            P(("parts", "dp"), None, "tp"),
            P(("parts", "dp")),
            P("tp", "dp"),
        ),
        out_specs=P(("parts", "tp"), "dp"),
        check_vma=False,
    )
```

```python
import functools

import jax
import jax.numpy as jnp
from jax import lax
from jax.experimental import pallas as pl
from jax.experimental.pallas import tpu as pltpu
from jax.sharding import PartitionSpec as P

D = 5120
HQ = 40
KVH = 8
HD = 128
NEW = 2
PER_HEAD = HQ // KVH
INV = 1.0 / HD**0.5

masked_score = -1e30
bf16 = jnp.bfloat16
COVER = 1 << 36
PCOVER = 1 << 10
f32 = jnp.float32

TOP, TOTAL, SECTION = 0, 3, 5
STATS = 16


def nt(a, b):
    return lax.dot_general(a, b, (((1,), (1,)), ((), ())), preferred_element_type=f32)


def nn(a, b):
    return jnp.dot(a, b, preferred_element_type=f32)


def spread(blocks):
    zeros = jnp.zeros_like(blocks[0])
    rows = [
        jnp.concatenate([b if i == j else zeros for i in range(len(blocks))], axis=1)
        if len(blocks) > 1
        else b
        for j, b in enumerate(blocks)
    ]
    return jnp.concatenate(rows, axis=0)


def split(x, pieces):
    out = []
    for _ in range(pieces):
        piece = x.astype(bf16).astype(f32)
        out.append(piece)
        x = x - piece
    return out


def eye(rows, cols):
    row = lax.broadcasted_iota(jnp.int32, (rows, cols), 0)
    return (row == lax.broadcasted_iota(jnp.int32, (rows, cols), 1)).astype(f32).astype(bf16)


def up(n, to):
    return -(-n // to) * to


def open_kernel(group_ref, after, out_ref):
    out_ref[...] = jnp.full(out_ref.shape, group_ref[0].astype(f32))


def cache_kernel(lens_ref, section_ref, q_ref, nk_ref, nv_ref, ck_ref, cv_ref, out_ref):
    requests, slots, cols = ck_ref.shape
    heads = cols // HD
    tokens = requests * NEW
    per = PER_HEAD * tokens
    rows = heads * per
    row = lax.broadcasted_iota(jnp.int32, (rows, 1), 0)
    request = lax.rem(lax.div(row, NEW), requests)
    token = lax.rem(row, NEW)
    q = q_ref[...].astype(f32)
    blocks = []
    for j in range(heads):
        parts = [q[:, (j * PER_HEAD + g) * HD : (j * PER_HEAD + g + 1) * HD] for g in range(PER_HEAD)]
        blocks.append(jnp.concatenate(parts, axis=0))
    out_ref[0:rows, :] = jnp.concatenate(blocks, axis=0).astype(bf16)
    qs = spread(blocks).astype(bf16)
    fresh = lax.broadcasted_iota(jnp.int32, (rows, tokens), 1)
    seen = (lax.div(fresh, NEW) == request) & (lax.rem(fresh, NEW) <= token)
    s_new = jnp.where(seen, nt(qs, nk_ref[...]) * INV, masked_score)
    limit = jnp.full((rows, 1), lens_ref[0], jnp.int32)
    for r in range(1, requests):
        limit = jnp.where(request == r, lens_ref[r], limit)
    live = lax.broadcasted_iota(jnp.int32, (rows, slots), 1) < limit
    s = nt(qs, ck_ref[0])
    for r in range(1, requests):
        s = jnp.where(request == r, nt(qs, ck_ref[r]), s)
    s = jnp.where(live, s * INV, masked_score)

    top = jnp.maximum(jnp.max(s, axis=1, keepdims=True), jnp.max(s_new, axis=1, keepdims=True))
    p = jnp.where(live, jnp.exp(s - top), 0.0)
    p_new = jnp.where(seen, jnp.exp(s_new - top), 0.0)
    total = jnp.sum(p, axis=1, keepdims=True) + jnp.sum(p_new, axis=1, keepdims=True)
    p = p.astype(bf16)
    acc = nn(p, cv_ref[0])
    for r in range(1, requests):
        acc = jnp.where(request == r, nn(p, cv_ref[r]), acc)
    acc = acc + nn(p_new.astype(bf16).astype(f32), nv_ref[...].astype(f32))
    mine = jnp.concatenate([acc[j * per : (j + 1) * per, j * HD : (j + 1) * HD] for j in range(heads)], axis=0)
    seg = up(rows, 16)
    out_ref[seg : seg + rows, :] = (mine / total).astype(bf16)

    lane = lax.broadcasted_iota(jnp.int32, (rows, HD), 1)
    stats = jnp.where(lane == SECTION, section_ref[0:1, :], 0.0)
    for i, piece in enumerate(split(top, 3)):
        stats = jnp.where(lane == TOP + i, piece, stats)
    for i, piece in enumerate(split(total, 2)):
        stats = jnp.where(lane == TOTAL + i, piece, stats)
    if rows < HD:
        stats = jnp.concatenate([stats, jnp.zeros((HD - rows, HD), f32)], axis=0)
    out_ref[2 * seg : 2 * seg + STATS, :] = nt(eye(STATS, HD), stats.astype(bf16)).astype(bf16)


def project_kernel(bits, first, last, *refs):
    count = len(bits)
    pieces, w_ref, refs = refs[:count], refs[count], refs[count + 1 :]
    rows, depth = pieces[0].shape
    me = lax.axis_index("tp")
    if first:
        acc, squares = [None, None], None
    else:
        acc = [refs[0][s * rows : (s + 1) * rows, :] for s in range(2)]
        squares = refs[1][:, 0:1]
        refs = refs[2:]
    for k, piece in zip(bits, pieces):
        h = piece[...]
        wide = h.astype(f32)
        square = jnp.sum(wide * wide, axis=1, keepdims=True)
        squares = square if squares is None else squares + square
        at = pl.multiple_of((me ^ k) * depth, depth)
        for s in range(2):
            term = nn(h, w_ref[s, pl.ds(at, depth), :])
            acc[s] = term if acc[s] is None else acc[s] + term
    if not last:
        for s in range(2):
            refs[0][s * rows : (s + 1) * rows, :] = acc[s]
        refs[1][...] = jnp.broadcast_to(squares, refs[1].shape)
        return
    b_ref, out_ref = refs
    scale = lax.rsqrt(squares / D + 1e-06)
    for s in range(2):
        bias = b_ref[s : s + 1, :].astype(f32)
        out_ref[s * rows : (s + 1) * rows, :] = (acc[s] * scale + bias).astype(bf16)


def pair_kernel(near_ref, far_ref, after, out_ref):
    out_ref[0] = near_ref[...]
    out_ref[1] = far_ref[...]


def prepare_kernel(heads, *refs):
    pairs, (section_ref, q_ref, bias_ref, old_ref, stats_ref) = refs[:-5], refs[-5:]
    parts = [pair.at[i] for i in range(2) for pair in pairs]
    groups = len(parts)
    seg = (parts[0].shape[0] - STATS) // 2
    rows = q_ref.shape[0] // groups
    per = rows // heads

    def by_head(first):
        blocks = [part[first : first + rows, :].astype(f32) for part in parts]
        return jnp.concatenate([b[j * per : (j + 1) * per, :] for j in range(heads) for b in blocks], axis=0)

    q_ref[...] = by_head(0).astype(bf16)
    stats = nt(
        eye(rows, HD), jnp.concatenate([part[2 * seg : 2 * seg + STATS, :] for part in parts], axis=0)
    )

    def column(at, pieces):
        columns = []
        for k in range(groups):
            c = k * STATS + at
            columns.append(sum([stats[:, c + i : c + i + 1] for i in range(pieces)]))
        return jnp.concatenate([c[j * per : (j + 1) * per] for j in range(heads) for c in columns], axis=0)

    top, total = column(TOP, 3), column(TOTAL, 2)
    own_section = column(SECTION, 1)[0 : groups * per]
    bias_ref[...] = jnp.where(own_section == section_ref[...].astype(f32), 0.0, masked_score)
    old_ref[...] = by_head(seg) * total
    lane = lax.broadcasted_iota(jnp.int32, stats_ref.shape, 1)
    stats_ref[...] = jnp.where(lane == 0, top, total)


def attend_kernel(groups, shares, *refs):
    kvs, (q_ref, bias_ref, old_ref, stats_ref, w_ref) = refs[:groups], refs[groups : groups + 5]
    outs = refs[groups + 5 : groups + 5 + shares]
    k_ref, v_ref, attended_ref, sums_ref = refs[groups + 5 + shares :]
    me_dp, me_tp = lax.axis_index("dp"), lax.axis_index("tp")
    memory = kvs[0].shape[0] // 2
    heads = kvs[0].shape[1] // HD
    tokens = attended_ref.shape[0] // groups
    per = PER_HEAD * tokens
    for bits, kv in enumerate(kvs):
        first = pl.multiple_of((me_dp ^ bits) * memory, memory)
        k_ref[pl.ds(first, memory), :] = kv[0:memory, :].astype(k_ref.dtype)
        v_ref[pl.ds(first, memory), :] = kv[memory : 2 * memory, :].astype(v_ref.dtype)
    some = groups * per
    sums = None
    for j in range(heads):
        at_rows, lanes = slice(j * some, (j + 1) * some), slice(j * HD, (j + 1) * HD)
        s = nt(q_ref[at_rows, :], k_ref[:, lanes].astype(bf16)) * INV + bias_ref[...]
        old_top, old_total = stats_ref[at_rows, 0:1], stats_ref[at_rows, 1:2]
        top = jnp.maximum(jnp.max(s, axis=1, keepdims=True), old_top)
        p = jnp.exp(s - top)
        shrink = jnp.exp(old_top - top)
        total = jnp.sum(p, axis=1, keepdims=True) + shrink * old_total
        acc = nn(p.astype(bf16), v_ref[:, lanes].astype(bf16))
        acc = (acc + old_ref[at_rows, :] * shrink) / total
        for k in range(groups):
            at = pl.multiple_of((me_dp ^ k) * tokens, tokens)
            for g in range(PER_HEAD):
                c = (j * PER_HEAD + g) * HD
                row = k * per + g * tokens
                attended_ref[pl.ds(at, tokens), c : c + HD] = acc[row : row + tokens, :]
        width = slice(j * PER_HEAD * HD, (j + 1) * PER_HEAD * HD)
        term = nn(attended_ref[:, width].astype(bf16), w_ref[width, :])
        sums = term if sums is None else sums + term
    sums_ref[...] = sums
    share = sums_ref.shape[0] // shares
    for k, out in enumerate(outs):
        at = pl.multiple_of((me_tp ^ k) * share, share)
        out[...] = sums_ref[pl.ds(at, share), :].astype(out.dtype)


SMEM = pl.BlockSpec(memory_space=pltpu.SMEM)
VMEM = pl.BlockSpec(memory_space=pltpu.VMEM)
ANY = pl.BlockSpec(memory_space=pl.ANY)
HBM = pl.BlockSpec(memory_space=pltpu.HBM)
PARAMS = pltpu.CompilerParams(vmem_limit_bytes=24 * 1024 * 1024)


def call(kernel, in_specs, out_shape, scratch, flops, bytes_accessed):
    return pl.pallas_call(
        kernel,
        in_specs=in_specs,
        out_shape=out_shape,
        out_specs=jax.tree.map(lambda _: VMEM, out_shape),
        scratch_shapes=scratch,
        compiler_params=PARAMS,
        cost_estimate=pl.CostEstimate(flops=flops, bytes_accessed=bytes_accessed, transcendentals=0),
    )


def in_hbm(*arrays):
    return [pltpu.with_memory_space_constraint(x, pltpu.HBM) for x in arrays]


def permute(x, axis, bits):
    return lax.ppermute(x, axis, [(i, i ^ bits) for i in range(lax.axis_size(axis))])


def passed_on(x, near, axis):
    n = lax.axis_size(axis)
    held = {0: x}
    bit = n // 2
    while bit:
        for bits in sorted(held):
            held[bits | bit] = permute(held[bits], axis, bit)
        held[0] = near
        bit //= 2
    return [held[bits] for bits in range(n)]


def body(
    memory_hidden,
    kv_weight,
    kv_bias,
    memory_sections,
    group_sections,
    queries,
    new_keys,
    new_values,
    cache_keys,
    cache_values,
    cache_lengths,
    out_weight,
):
    groups, shares = lax.axis_size("dp"), lax.axis_size("tp")
    memory, depth = memory_hidden.shape
    requests, slots, cols = cache_keys.shape
    tokens = requests * NEW
    rows = (cols // HD) * PER_HEAD * tokens
    every = memory_sections.shape[0]

    gate = call(lambda *refs: None, [], jax.ShapeDtypeStruct((8, HD), f32), [], COVER, 0)()
    group, gate = lax.optimization_barrier((group_sections, gate))
    section = call(open_kernel, [SMEM, ANY], pltpu.VMEM((8, HD), f32), [], 1 << 10, 0)(group, gate)
    own, section = lax.optimization_barrier((memory_hidden, section))
    weight, section = lax.optimization_barrier((kv_weight, section))
    part = call(
        cache_kernel,
        [SMEM] + [VMEM] * 6,
        pltpu.VMEM((2 * up(rows, 16) + STATS, HD), bf16),
        [],
        COVER,
        4 * requests * slots * cols,
    )(cache_lengths, section, queries, new_keys, new_values, cache_keys, cache_values)
    own_later, part = lax.optimization_barrier((own, part))
    hidden = passed_on(memory_hidden, own_later, "tp")
    part_far = permute(part, "dp", groups // 2)
    near, far = list(range(shares - 1)), [shares - 1]
    partial = call(
        functools.partial(project_kernel, near, True, False),
        [VMEM] * (len(near) + 1),
        [pltpu.VMEM((2 * memory, cols), f32), pltpu.VMEM((memory, HD), f32)],
        [],
        COVER,
        4 * D * cols,
    )(*[hidden[k] for k in near], weight)
    kv = call(
        functools.partial(project_kernel, far, False, True),
        [VMEM] * 5,
        pltpu.VMEM((2 * memory, cols), bf16),
        [],
        4 * memory * D * cols // shares,
        4 * D * cols // shares,
    )(hidden[far[0]], weight, *partial, kv_bias)
    kv_far = permute(kv, "dp", groups // 2)
    pair = call(
        pair_kernel,
        [VMEM, VMEM, ANY],
        pltpu.VMEM((2,) + part.shape, bf16),
        [],
        COVER,
        0,
    )(part, part_far, kv)
    kv_on, _ = lax.optimization_barrier((kv_far, pair))
    half = range(1, groups // 2)
    pairs = [pair, *[permute(pair, "dp", bits) for bits in half]]
    kvs = [kv, *[permute(kv, "dp", bits) for bits in half], kv_far, *[permute(kv_on, "dp", bits) for bits in half]]
    heads = cols // HD
    prepared = call(
        functools.partial(prepare_kernel, heads),
        [VMEM] * (groups // 2 + 1),
        [
            pltpu.VMEM((groups * rows, HD), bf16),
            pltpu.VMEM((groups * rows // heads, every), f32),
            pltpu.VMEM((groups * rows, HD), f32),
            pltpu.VMEM((groups * rows, HD), f32),
        ],
        [],
        PCOVER,
        0,
    )(*pairs, memory_sections.reshape(1, every))

    out_rows, out_cols = groups * tokens, out_weight.shape[1]
    share = out_rows // shares
    held = bf16 if memory % 16 == 0 else f32
    pieces = call(
        functools.partial(attend_kernel, groups, shares),
        [VMEM] * (groups + 5),
        [pltpu.VMEM((share, out_cols), f32 if k == 0 else bf16) for k in range(shares)],
        [
            pltpu.VMEM((every, cols), held),
            pltpu.VMEM((every, cols), held),
            pltpu.VMEM((out_rows, out_weight.shape[0]), f32),
            pltpu.VMEM((out_rows, out_cols), f32),
        ],
        2 * out_rows * out_weight.size,
        2 * out_weight.size,
    )(*kvs, *prepared, out_weight)
    summed = pieces[0]
    for bits in [*range(shares - 2, 0, -1), shares - 1]:
        summed = summed + permute(pieces[bits], "tp", bits).astype(f32)
    return summed.astype(bf16)


def solution(mesh):
    return jax.shard_map(
        body,
        mesh=mesh,
        in_specs=(
            P(("parts", "dp"), "tp"),
            P(None, None, "tp"),
            P(None, "tp"),
            P("parts"),
            P(("parts", "dp")),
            P(("parts", "dp"), "tp"),
            P(("parts", "dp"), "tp"),
            P(("parts", "dp"), "tp"),
            P(("parts", "dp"), None, "tp"),
            P(("parts", "dp"), None, "tp"),
            P(("parts", "dp")),
            P("tp", "dp"),
        ),
        out_specs=P(("parts", "tp"), "dp"),
        check_vma=False,
    )
```

```python
import functools

import jax
import jax.numpy as jnp
from jax import lax
from jax.experimental import pallas as pl
from jax.experimental.pallas import tpu as pltpu
from jax.sharding import PartitionSpec as P

D = 5120
HQ = 40
KVH = 8
HD = 128
NEW = 2
PER_HEAD = HQ // KVH
INV = 1.0 / HD**0.5

masked_score = -1e30
bf16 = jnp.bfloat16
COVER = 1 << 36
PCOVER = 1 << 10
f32 = jnp.float32

TOP, TOTAL, SECTION = 0, 3, 5
STATS = 16


def nt(a, b):
    return lax.dot_general(a, b, (((1,), (1,)), ((), ())), preferred_element_type=f32)


def nn(a, b):
    return jnp.dot(a, b, preferred_element_type=f32)


def spread(blocks):
    zeros = jnp.zeros_like(blocks[0])
    rows = [
        jnp.concatenate([b if i == j else zeros for i in range(len(blocks))], axis=1)
        if len(blocks) > 1
        else b
        for j, b in enumerate(blocks)
    ]
    return jnp.concatenate(rows, axis=0)


def split(x, pieces):
    out = []
    for _ in range(pieces):
        piece = x.astype(bf16).astype(f32)
        out.append(piece)
        x = x - piece
    return out


def eye(rows, cols):
    row = lax.broadcasted_iota(jnp.int32, (rows, cols), 0)
    return (row == lax.broadcasted_iota(jnp.int32, (rows, cols), 1)).astype(f32).astype(bf16)


def up(n, to):
    return -(-n // to) * to


def open_kernel(group_ref, after, out_ref):
    out_ref[...] = jnp.full(out_ref.shape, group_ref[0].astype(f32))


def cache_kernel(lens_ref, section_ref, q_ref, nk_ref, nv_ref, ck_ref, cv_ref, out_ref):
    requests, slots, cols = ck_ref.shape
    heads = cols // HD
    tokens = requests * NEW
    per = PER_HEAD * tokens
    rows = heads * per
    row = lax.broadcasted_iota(jnp.int32, (rows, 1), 0)
    request = lax.rem(lax.div(row, NEW), requests)
    token = lax.rem(row, NEW)
    q = q_ref[...].astype(f32)
    blocks = []
    for j in range(heads):
        parts = [q[:, (j * PER_HEAD + g) * HD : (j * PER_HEAD + g + 1) * HD] for g in range(PER_HEAD)]
        blocks.append(jnp.concatenate(parts, axis=0))
    out_ref[0:rows, :] = jnp.concatenate(blocks, axis=0).astype(bf16)
    qs = spread(blocks).astype(bf16)
    fresh = lax.broadcasted_iota(jnp.int32, (rows, tokens), 1)
    seen = (lax.div(fresh, NEW) == request) & (lax.rem(fresh, NEW) <= token)
    s_new = jnp.where(seen, nt(qs, nk_ref[...]) * INV, masked_score)
    limit = jnp.full((rows, 1), lens_ref[0], jnp.int32)
    for r in range(1, requests):
        limit = jnp.where(request == r, lens_ref[r], limit)
    live = lax.broadcasted_iota(jnp.int32, (rows, slots), 1) < limit
    s = nt(qs, ck_ref[0])
    for r in range(1, requests):
        s = jnp.where(request == r, nt(qs, ck_ref[r]), s)
    s = jnp.where(live, s * INV, masked_score)

    top = jnp.maximum(jnp.max(s, axis=1, keepdims=True), jnp.max(s_new, axis=1, keepdims=True))
    p = jnp.where(live, jnp.exp(s - top), 0.0)
    p_new = jnp.where(seen, jnp.exp(s_new - top), 0.0)
    total = jnp.sum(p, axis=1, keepdims=True) + jnp.sum(p_new, axis=1, keepdims=True)
    p = p.astype(bf16)
    acc = nn(p, cv_ref[0])
    for r in range(1, requests):
        acc = jnp.where(request == r, nn(p, cv_ref[r]), acc)
    acc = acc + nn(p_new.astype(bf16).astype(f32), nv_ref[...].astype(f32))
    mine = jnp.concatenate([acc[j * per : (j + 1) * per, j * HD : (j + 1) * HD] for j in range(heads)], axis=0)
    seg = up(rows, 16)
    out_ref[seg : seg + rows, :] = (mine / total).astype(bf16)

    lane = lax.broadcasted_iota(jnp.int32, (rows, HD), 1)
    stats = jnp.where(lane == SECTION, section_ref[0:1, :], 0.0)
    for i, piece in enumerate(split(top, 3)):
        stats = jnp.where(lane == TOP + i, piece, stats)
    for i, piece in enumerate(split(total, 2)):
        stats = jnp.where(lane == TOTAL + i, piece, stats)
    if rows < HD:
        stats = jnp.concatenate([stats, jnp.zeros((HD - rows, HD), f32)], axis=0)
    out_ref[2 * seg : 2 * seg + STATS, :] = nt(eye(STATS, HD), stats.astype(bf16)).astype(bf16)


def project_kernel(bits, first, last, *refs):
    count = len(bits)
    pieces, w_ref, refs = refs[:count], refs[count], refs[count + 1 :]
    rows, depth = pieces[0].shape
    me = lax.axis_index("tp")
    if first:
        acc, squares = [None, None], None
    else:
        acc = [refs[0][s * rows : (s + 1) * rows, :] for s in range(2)]
        squares = refs[1][:, 0:1]
        refs = refs[2:]
    for k, piece in zip(bits, pieces):
        h = piece[...]
        wide = h.astype(f32)
        square = jnp.sum(wide * wide, axis=1, keepdims=True)
        squares = square if squares is None else squares + square
        at = pl.multiple_of((me ^ k) * depth, depth)
        for s in range(2):
            term = nn(h, w_ref[s, pl.ds(at, depth), :])
            acc[s] = term if acc[s] is None else acc[s] + term
    if not last:
        for s in range(2):
            refs[0][s * rows : (s + 1) * rows, :] = acc[s]
        refs[1][...] = jnp.broadcast_to(squares, refs[1].shape)
        return
    b_ref, out_ref = refs
    scale = lax.rsqrt(squares / D + 1e-06)
    for s in range(2):
        bias = b_ref[s : s + 1, :].astype(f32)
        out_ref[s * rows : (s + 1) * rows, :] = (acc[s] * scale + bias).astype(bf16)


def pair_kernel(near_ref, far_ref, after, out_ref):
    out_ref[0] = near_ref[...]
    out_ref[1] = far_ref[...]


def prepare_kernel(heads, *refs):
    pairs, (section_ref, q_ref, bias_ref, old_ref, stats_ref) = refs[:-5], refs[-5:]
    parts = [pair.at[i] for i in range(2) for pair in pairs]
    groups = len(parts)
    seg = (parts[0].shape[0] - STATS) // 2
    rows = q_ref.shape[0] // groups
    per = rows // heads

    def by_head(first):
        blocks = [part[first : first + rows, :].astype(f32) for part in parts]
        return jnp.concatenate([b[j * per : (j + 1) * per, :] for j in range(heads) for b in blocks], axis=0)

    q_ref[...] = by_head(0).astype(bf16)
    stats = nt(
        eye(rows, HD), jnp.concatenate([part[2 * seg : 2 * seg + STATS, :] for part in parts], axis=0)
    )

    def column(at, pieces):
        columns = []
        for k in range(groups):
            c = k * STATS + at
            columns.append(sum([stats[:, c + i : c + i + 1] for i in range(pieces)]))
        return jnp.concatenate([c[j * per : (j + 1) * per] for j in range(heads) for c in columns], axis=0)

    top, total = column(TOP, 3), column(TOTAL, 2)
    every = section_ref.shape[1]
    memory = every // groups
    sections = jnp.broadcast_to(section_ref[...].astype(f32), (8, every))
    me = lax.axis_index("dp")
    held = []
    for k in range(groups):
        back = lax.rem(every - (me ^ k) * memory, every)
        held.append(pltpu.roll(sections, back, 1)[0:1, 0:memory])
    own_section = column(SECTION, 1)[0 : groups * per]
    bias_ref[...] = jnp.where(own_section == jnp.concatenate(held, axis=1), 0.0, masked_score)
    old_ref[...] = by_head(seg) * total
    lane = lax.broadcasted_iota(jnp.int32, stats_ref.shape, 1)
    stats_ref[...] = jnp.where(lane == 0, top, total)


def stack(blocks):
    if blocks[0].shape[0] % 16:
        return jnp.concatenate([b.astype(f32) for b in blocks], axis=0).astype(bf16)
    return jnp.concatenate(blocks, axis=0)


def attend_kernel(groups, shares, *refs):
    kvs, (q_ref, bias_ref, old_ref, stats_ref, w_ref) = refs[:groups], refs[groups : groups + 5]
    outs = refs[groups + 5 : groups + 5 + shares]
    attended_ref, sums_ref = refs[groups + 5 + shares :]
    me_dp, me_tp = lax.axis_index("dp"), lax.axis_index("tp")
    memory = kvs[0].shape[0] // 2
    heads = kvs[0].shape[1] // HD
    tokens = attended_ref.shape[0] // groups
    per = PER_HEAD * tokens
    some = groups * per
    scores = []
    for j in range(heads):
        keys = stack([kv[0:memory, j * HD : (j + 1) * HD] for kv in kvs])
        scores.append(nt(q_ref[j * some : (j + 1) * some, :], keys))
    sums = None
    for j, s in enumerate(scores):
        at_rows = slice(j * some, (j + 1) * some)
        s = s * INV + bias_ref[...]
        old_top, old_total = stats_ref[at_rows, 0:1], stats_ref[at_rows, 1:2]
        top = jnp.maximum(jnp.max(s, axis=1, keepdims=True), old_top)
        p = jnp.exp(s - top)
        shrink = jnp.exp(old_top - top)
        total = jnp.sum(p, axis=1, keepdims=True) + shrink * old_total
        values = stack([kv[memory : 2 * memory, j * HD : (j + 1) * HD] for kv in kvs])
        acc = nn(p.astype(bf16), values)
        acc = (acc + old_ref[at_rows, :] * shrink) / total
        for k in range(groups):
            at = pl.multiple_of((me_dp ^ k) * tokens, tokens)
            for g in range(PER_HEAD):
                c = (j * PER_HEAD + g) * HD
                row = k * per + g * tokens
                attended_ref[pl.ds(at, tokens), c : c + HD] = acc[row : row + tokens, :]
        width = slice(j * PER_HEAD * HD, (j + 1) * PER_HEAD * HD)
        term = nn(attended_ref[:, width].astype(bf16), w_ref[width, :])
        sums = term if sums is None else sums + term
    sums_ref[...] = sums
    share = sums_ref.shape[0] // shares
    for k, out in enumerate(outs):
        at = pl.multiple_of((me_tp ^ k) * share, share)
        out[...] = sums_ref[pl.ds(at, share), :].astype(out.dtype)


SMEM = pl.BlockSpec(memory_space=pltpu.SMEM)
VMEM = pl.BlockSpec(memory_space=pltpu.VMEM)
ANY = pl.BlockSpec(memory_space=pl.ANY)
HBM = pl.BlockSpec(memory_space=pltpu.HBM)
PARAMS = pltpu.CompilerParams(vmem_limit_bytes=24 * 1024 * 1024)


def call(kernel, in_specs, out_shape, scratch, flops, bytes_accessed):
    return pl.pallas_call(
        kernel,
        in_specs=in_specs,
        out_shape=out_shape,
        out_specs=jax.tree.map(lambda _: VMEM, out_shape),
        scratch_shapes=scratch,
        compiler_params=PARAMS,
        cost_estimate=pl.CostEstimate(flops=flops, bytes_accessed=bytes_accessed, transcendentals=0),
    )


def in_hbm(*arrays):
    return [pltpu.with_memory_space_constraint(x, pltpu.HBM) for x in arrays]


def permute(x, axis, bits):
    return lax.ppermute(x, axis, [(i, i ^ bits) for i in range(lax.axis_size(axis))])


def passed_on(x, near, axis):
    n = lax.axis_size(axis)
    held = {0: x}
    bit = n // 2
    while bit:
        for bits in sorted(held):
            held[bits | bit] = permute(held[bits], axis, bit)
        held[0] = near
        bit //= 2
    return [held[bits] for bits in range(n)]


def body(
    memory_hidden,
    kv_weight,
    kv_bias,
    memory_sections,
    group_sections,
    queries,
    new_keys,
    new_values,
    cache_keys,
    cache_values,
    cache_lengths,
    out_weight,
):
    groups, shares = lax.axis_size("dp"), lax.axis_size("tp")
    memory, depth = memory_hidden.shape
    requests, slots, cols = cache_keys.shape
    tokens = requests * NEW
    rows = (cols // HD) * PER_HEAD * tokens
    every = memory_sections.shape[0]

    gate = call(lambda *refs: None, [], jax.ShapeDtypeStruct((8, HD), f32), [], COVER, 0)()
    group, gate = lax.optimization_barrier((group_sections, gate))
    section = call(open_kernel, [SMEM, ANY], pltpu.VMEM((8, HD), f32), [], 1 << 10, 0)(group, gate)
    own, section = lax.optimization_barrier((memory_hidden, section))
    weight, section = lax.optimization_barrier((kv_weight, section))
    part = call(
        cache_kernel,
        [SMEM] + [VMEM] * 6,
        pltpu.VMEM((2 * up(rows, 16) + STATS, HD), bf16),
        [],
        COVER,
        4 * requests * slots * cols,
    )(cache_lengths, section, queries, new_keys, new_values, cache_keys, cache_values)
    own_later, part = lax.optimization_barrier((own, part))
    hidden = passed_on(memory_hidden, own_later, "tp")
    part_far = permute(part, "dp", groups // 2)
    near, far = list(range(shares - 1)), [shares - 1]
    partial = call(
        functools.partial(project_kernel, near, True, False),
        [VMEM] * (len(near) + 1),
        [pltpu.VMEM((2 * memory, cols), f32), pltpu.VMEM((memory, HD), f32)],
        [],
        COVER,
        4 * D * cols,
    )(*[hidden[k] for k in near], weight)
    kv = call(
        functools.partial(project_kernel, far, False, True),
        [VMEM] * 5,
        pltpu.VMEM((2 * memory, cols), bf16),
        [],
        4 * memory * D * cols // shares,
        4 * D * cols // shares,
    )(hidden[far[0]], weight, *partial, kv_bias)
    kv_far = permute(kv, "dp", groups // 2)
    pair = call(
        pair_kernel,
        [VMEM, VMEM, ANY],
        pltpu.VMEM((2,) + part.shape, bf16),
        [],
        COVER,
        0,
    )(part, part_far, kv)
    kv_on, _ = lax.optimization_barrier((kv_far, pair))
    half = range(1, groups // 2)
    pairs = [pair, *[permute(pair, "dp", bits) for bits in half]]
    kvs = [kv, *[permute(kv, "dp", bits) for bits in half], kv_far, *[permute(kv_on, "dp", bits) for bits in half]]
    heads = cols // HD
    prepared = call(
        functools.partial(prepare_kernel, heads),
        [VMEM] * (groups // 2 + 1),
        [
            pltpu.VMEM((groups * rows, HD), bf16),
            pltpu.VMEM((groups * rows // heads, every), f32),
            pltpu.VMEM((groups * rows, HD), f32),
            pltpu.VMEM((groups * rows, HD), f32),
        ],
        [],
        PCOVER,
        0,
    )(*pairs, memory_sections.reshape(1, every))

    out_rows, out_cols = groups * tokens, out_weight.shape[1]
    share = out_rows // shares
    pieces = call(
        functools.partial(attend_kernel, groups, shares),
        [VMEM] * (groups + 5),
        [pltpu.VMEM((share, out_cols), f32 if k == 0 else bf16) for k in range(shares)],
        [
            pltpu.VMEM((out_rows, out_weight.shape[0]), f32),
            pltpu.VMEM((out_rows, out_cols), f32),
        ],
        2 * out_rows * out_weight.size,
        2 * out_weight.size,
    )(*kvs, *prepared, out_weight)
    summed = pieces[0]
    for bits in [*range(shares - 2, 0, -1), shares - 1]:
        summed = summed + permute(pieces[bits], "tp", bits).astype(f32)
    return summed.astype(bf16)


def solution(mesh):
    return jax.shard_map(
        body,
        mesh=mesh,
        in_specs=(
            P(("parts", "dp"), "tp"),
            P(None, None, "tp"),
            P(None, "tp"),
            P("parts"),
            P(("parts", "dp")),
            P(("parts", "dp"), "tp"),
            P(("parts", "dp"), "tp"),
            P(("parts", "dp"), "tp"),
            P(("parts", "dp"), None, "tp"),
            P(("parts", "dp"), None, "tp"),
            P(("parts", "dp")),
            P("tp", "dp"),
        ),
        out_specs=P(("parts", "tp"), "dp"),
        check_vma=False,
    )
```

```python
import functools

import jax
import jax.numpy as jnp
from jax import lax
from jax.experimental import pallas as pl
from jax.experimental.pallas import tpu as pltpu
from jax.sharding import PartitionSpec as P

D = 5120
HQ = 40
KVH = 8
HD = 128
NEW = 2
PER_HEAD = HQ // KVH
INV = 1.0 / HD**0.5

masked_score = -1e30
bf16 = jnp.bfloat16
COVER = 1 << 36
PCOVER = 1 << 10
f32 = jnp.float32

TOP, TOTAL, SECTION = 0, 3, 5
STATS = 16


def nt(a, b):
    return lax.dot_general(a, b, (((1,), (1,)), ((), ())), preferred_element_type=f32)


def nn(a, b):
    return jnp.dot(a, b, preferred_element_type=f32)


def spread(blocks):
    zeros = jnp.zeros_like(blocks[0])
    rows = [
        jnp.concatenate([b if i == j else zeros for i in range(len(blocks))], axis=1)
        if len(blocks) > 1
        else b
        for j, b in enumerate(blocks)
    ]
    return jnp.concatenate(rows, axis=0)


def split(x, pieces):
    out = []
    for _ in range(pieces):
        piece = x.astype(bf16).astype(f32)
        out.append(piece)
        x = x - piece
    return out


def eye(rows, cols):
    row = lax.broadcasted_iota(jnp.int32, (rows, cols), 0)
    return (row == lax.broadcasted_iota(jnp.int32, (rows, cols), 1)).astype(f32).astype(bf16)


def up(n, to):
    return -(-n // to) * to


def open_kernel(group_ref, after, out_ref):
    out_ref[...] = jnp.full(out_ref.shape, group_ref[0].astype(f32))


def cache_kernel(lens_ref, section_ref, q_ref, nk_ref, nv_ref, ck_ref, cv_ref, out_ref):
    requests, slots, cols = ck_ref.shape
    heads = cols // HD
    tokens = requests * NEW
    per = PER_HEAD * tokens
    rows = heads * per
    row = lax.broadcasted_iota(jnp.int32, (rows, 1), 0)
    request = lax.rem(lax.div(row, NEW), requests)
    token = lax.rem(row, NEW)
    q = q_ref[...].astype(f32)
    blocks = []
    for j in range(heads):
        parts = [q[:, (j * PER_HEAD + g) * HD : (j * PER_HEAD + g + 1) * HD] for g in range(PER_HEAD)]
        blocks.append(jnp.concatenate(parts, axis=0))
    out_ref[0:rows, :] = jnp.concatenate(blocks, axis=0).astype(bf16)
    qs = spread(blocks).astype(bf16)
    fresh = lax.broadcasted_iota(jnp.int32, (rows, tokens), 1)
    seen = (lax.div(fresh, NEW) == request) & (lax.rem(fresh, NEW) <= token)
    s_new = jnp.where(seen, nt(qs, nk_ref[...]) * INV, masked_score)
    limit = jnp.full((rows, 1), lens_ref[0], jnp.int32)
    for r in range(1, requests):
        limit = jnp.where(request == r, lens_ref[r], limit)
    live = lax.broadcasted_iota(jnp.int32, (rows, slots), 1) < limit
    s = nt(qs, ck_ref[0])
    for r in range(1, requests):
        s = jnp.where(request == r, nt(qs, ck_ref[r]), s)
    s = jnp.where(live, s * INV, masked_score)

    top = jnp.maximum(jnp.max(s, axis=1, keepdims=True), jnp.max(s_new, axis=1, keepdims=True))
    p = jnp.where(live, jnp.exp(s - top), 0.0)
    p_new = jnp.where(seen, jnp.exp(s_new - top), 0.0)
    total = jnp.sum(p, axis=1, keepdims=True) + jnp.sum(p_new, axis=1, keepdims=True)
    p = p.astype(bf16)
    acc = nn(p, cv_ref[0])
    for r in range(1, requests):
        acc = jnp.where(request == r, nn(p, cv_ref[r]), acc)
    acc = acc + nn(p_new.astype(bf16).astype(f32), nv_ref[...].astype(f32))
    mine = jnp.concatenate([acc[j * per : (j + 1) * per, j * HD : (j + 1) * HD] for j in range(heads)], axis=0)
    seg = up(rows, 16)
    out_ref[seg : seg + rows, :] = (mine / total).astype(bf16)

    lane = lax.broadcasted_iota(jnp.int32, (rows, HD), 1)
    stats = jnp.where(lane == SECTION, section_ref[0:1, :], 0.0)
    for i, piece in enumerate(split(top, 3)):
        stats = jnp.where(lane == TOP + i, piece, stats)
    for i, piece in enumerate(split(total, 2)):
        stats = jnp.where(lane == TOTAL + i, piece, stats)
    if rows < HD:
        stats = jnp.concatenate([stats, jnp.zeros((HD - rows, HD), f32)], axis=0)
    out_ref[2 * seg : 2 * seg + STATS, :] = nt(eye(STATS, HD), stats.astype(bf16)).astype(bf16)


def project_kernel(bits, first, last, *refs):
    count = len(bits)
    pieces, w_ref, refs = refs[:count], refs[count], refs[count + 1 :]
    rows, depth = pieces[0].shape
    me = lax.axis_index("tp")
    if first:
        acc, squares = [None, None], None
    else:
        acc = [refs[0][s * rows : (s + 1) * rows, :] for s in range(2)]
        squares = refs[1][:, 0:1]
        refs = refs[2:]
    for k, piece in zip(bits, pieces):
        h = piece[...]
        wide = h.astype(f32)
        square = jnp.sum(wide * wide, axis=1, keepdims=True)
        squares = square if squares is None else squares + square
        at = pl.multiple_of((me ^ k) * depth, depth)
        for s in range(2):
            term = nn(h, w_ref[s, pl.ds(at, depth), :])
            acc[s] = term if acc[s] is None else acc[s] + term
    if not last:
        for s in range(2):
            refs[0][s * rows : (s + 1) * rows, :] = acc[s]
        refs[1][...] = jnp.broadcast_to(squares, refs[1].shape)
        return
    b_ref, out_ref = refs
    scale = lax.rsqrt(squares / D + 1e-06)
    for s in range(2):
        bias = b_ref[s : s + 1, :].astype(f32)
        out_ref[s * rows : (s + 1) * rows, :] = (acc[s] * scale + bias).astype(bf16)


def pair_kernel(near_ref, far_ref, after, out_ref):
    out_ref[0] = near_ref[...]
    out_ref[1] = far_ref[...]


def prepare_kernel(heads, *refs):
    pairs, (section_ref, q_ref, bias_ref, old_ref, stats_ref) = refs[:-5], refs[-5:]
    parts = [pair.at[i] for i in range(2) for pair in pairs]
    groups = len(parts)
    seg = (parts[0].shape[0] - STATS) // 2
    rows = q_ref.shape[0] // groups
    per = rows // heads

    def by_head(first):
        blocks = [part[first : first + rows, :].astype(f32) for part in parts]
        return jnp.concatenate([b[j * per : (j + 1) * per, :] for j in range(heads) for b in blocks], axis=0)

    q_ref[...] = by_head(0).astype(bf16)
    stats = nt(
        eye(rows, HD), jnp.concatenate([part[2 * seg : 2 * seg + STATS, :] for part in parts], axis=0)
    )

    def column(at, pieces):
        columns = []
        for k in range(groups):
            c = k * STATS + at
            columns.append(sum([stats[:, c + i : c + i + 1] for i in range(pieces)]))
        return jnp.concatenate([c[j * per : (j + 1) * per] for j in range(heads) for c in columns], axis=0)

    top, total = column(TOP, 3), column(TOTAL, 2)
    every = section_ref.shape[1]
    memory = every // groups
    sections = jnp.broadcast_to(section_ref[...].astype(f32), (8, every))
    me = lax.axis_index("dp")
    held = []
    for k in range(groups):
        back = lax.rem(every - (me ^ k) * memory, every)
        held.append(pltpu.roll(sections, back, 1)[0:1, 0:memory])
    own_section = column(SECTION, 1)[0 : groups * per]
    bias_ref[...] = jnp.where(own_section == jnp.concatenate(held, axis=1), 0.0, masked_score)
    old_ref[...] = by_head(seg) * total
    lane = lax.broadcasted_iota(jnp.int32, stats_ref.shape, 1)
    stats_ref[...] = jnp.where(lane == 0, top, total)


def stack(blocks):
    if blocks[0].shape[0] % 16:
        return jnp.concatenate([b.astype(f32) for b in blocks], axis=0).astype(bf16)
    return jnp.concatenate(blocks, axis=0)


def attend_kernel(groups, shares, *refs):
    kvs, (q_ref, bias_ref, old_ref, stats_ref, w_ref) = refs[:groups], refs[groups : groups + 5]
    outs = refs[groups + 5 : groups + 5 + shares]
    attended_ref, sums_ref = refs[groups + 5 + shares :]
    me_dp, me_tp = lax.axis_index("dp"), lax.axis_index("tp")
    memory = kvs[0].shape[0] // 2
    heads = kvs[0].shape[1] // HD
    tokens = attended_ref.shape[0] // groups
    per = PER_HEAD * tokens
    some = groups * per
    scores = []
    for j in range(heads):
        keys = stack([kv[0:memory, j * HD : (j + 1) * HD] for kv in kvs])
        scores.append(nt(q_ref[j * some : (j + 1) * some, :], keys))
    sums = None
    for j, s in enumerate(scores):
        at_rows = slice(j * some, (j + 1) * some)
        s = s * INV + bias_ref[...]
        old_top, old_total = stats_ref[at_rows, 0:1], stats_ref[at_rows, 1:2]
        top = jnp.maximum(jnp.max(s, axis=1, keepdims=True), old_top)
        p = jnp.exp(s - top)
        shrink = jnp.exp(old_top - top)
        total = jnp.sum(p, axis=1, keepdims=True) + shrink * old_total
        values = stack([kv[memory : 2 * memory, j * HD : (j + 1) * HD] for kv in kvs])
        acc = nn(p.astype(bf16), values)
        acc = (acc + old_ref[at_rows, :] * shrink) / total
        for k in range(groups):
            at = pl.multiple_of((me_dp ^ k) * tokens, tokens)
            for g in range(PER_HEAD):
                c = (j * PER_HEAD + g) * HD
                row = k * per + g * tokens
                attended_ref[pl.ds(at, tokens), c : c + HD] = acc[row : row + tokens, :]
        width = slice(j * PER_HEAD * HD, (j + 1) * PER_HEAD * HD)
        term = nn(attended_ref[:, width].astype(bf16), w_ref[width, :])
        sums = term if sums is None else sums + term
    sums_ref[...] = sums
    share = sums_ref.shape[0] // shares
    for k, out in enumerate(outs):
        at = pl.multiple_of((me_tp ^ k) * share, share)
        out[...] = sums_ref[pl.ds(at, share), :].astype(out.dtype)


def sum_kernel(own_ref, *refs):
    total = own_ref[...]
    for ref in refs[:-1]:
        total = total + ref[...].astype(f32)
    refs[-1][...] = total.astype(bf16)


SMEM = pl.BlockSpec(memory_space=pltpu.SMEM)
VMEM = pl.BlockSpec(memory_space=pltpu.VMEM)
ANY = pl.BlockSpec(memory_space=pl.ANY)
HBM = pl.BlockSpec(memory_space=pltpu.HBM)
PARAMS = pltpu.CompilerParams(vmem_limit_bytes=24 * 1024 * 1024)


def call(kernel, in_specs, out_shape, scratch, flops, bytes_accessed):
    return pl.pallas_call(
        kernel,
        in_specs=in_specs,
        out_shape=out_shape,
        out_specs=jax.tree.map(lambda _: VMEM, out_shape),
        scratch_shapes=scratch,
        compiler_params=PARAMS,
        cost_estimate=pl.CostEstimate(flops=flops, bytes_accessed=bytes_accessed, transcendentals=0),
    )


def in_hbm(*arrays):
    return [pltpu.with_memory_space_constraint(x, pltpu.HBM) for x in arrays]


def permute(x, axis, bits):
    return lax.ppermute(x, axis, [(i, i ^ bits) for i in range(lax.axis_size(axis))])


def passed_on(x, near, axis):
    n = lax.axis_size(axis)
    held = {0: x}
    bit = n // 2
    while bit:
        for bits in sorted(held):
            held[bits | bit] = permute(held[bits], axis, bit)
        held[0] = near
        bit //= 2
    return [held[bits] for bits in range(n)]


def body(
    memory_hidden,
    kv_weight,
    kv_bias,
    memory_sections,
    group_sections,
    queries,
    new_keys,
    new_values,
    cache_keys,
    cache_values,
    cache_lengths,
    out_weight,
):
    groups, shares = lax.axis_size("dp"), lax.axis_size("tp")
    memory, depth = memory_hidden.shape
    requests, slots, cols = cache_keys.shape
    tokens = requests * NEW
    rows = (cols // HD) * PER_HEAD * tokens
    every = memory_sections.shape[0]

    gate = call(lambda *refs: None, [], jax.ShapeDtypeStruct((8, HD), f32), [], COVER, 0)()
    group, gate = lax.optimization_barrier((group_sections, gate))
    section = call(open_kernel, [SMEM, ANY], pltpu.VMEM((8, HD), f32), [], 1 << 10, 0)(group, gate)
    own, section = lax.optimization_barrier((memory_hidden, section))
    weight, section = lax.optimization_barrier((kv_weight, section))
    part = call(
        cache_kernel,
        [SMEM] + [VMEM] * 6,
        pltpu.VMEM((2 * up(rows, 16) + STATS, HD), bf16),
        [],
        COVER,
        4 * requests * slots * cols,
    )(cache_lengths, section, queries, new_keys, new_values, cache_keys, cache_values)
    own_later, part = lax.optimization_barrier((own, part))
    hidden = passed_on(memory_hidden, own_later, "tp")
    part_far = permute(part, "dp", groups // 2)
    near, far = list(range(shares - 1)), [shares - 1]
    partial = call(
        functools.partial(project_kernel, near, True, False),
        [VMEM] * (len(near) + 1),
        [pltpu.VMEM((2 * memory, cols), f32), pltpu.VMEM((memory, HD), f32)],
        [],
        COVER,
        4 * D * cols,
    )(*[hidden[k] for k in near], weight)
    kv = call(
        functools.partial(project_kernel, far, False, True),
        [VMEM] * 5,
        pltpu.VMEM((2 * memory, cols), bf16),
        [],
        4 * memory * D * cols // shares,
        4 * D * cols // shares,
    )(hidden[far[0]], weight, *partial, kv_bias)
    kv_far = permute(kv, "dp", groups // 2)
    pair = call(
        pair_kernel,
        [VMEM, VMEM, ANY],
        pltpu.VMEM((2,) + part.shape, bf16),
        [],
        COVER,
        0,
    )(part, part_far, kv)
    kv_on, _ = lax.optimization_barrier((kv_far, pair))
    half = range(1, groups // 2)
    pairs = [pair, *[permute(pair, "dp", bits) for bits in half]]
    kvs = [kv, *[permute(kv, "dp", bits) for bits in half], kv_far, *[permute(kv_on, "dp", bits) for bits in half]]
    heads = cols // HD
    prepared = call(
        functools.partial(prepare_kernel, heads),
        [VMEM] * (groups // 2 + 1),
        [
            pltpu.VMEM((groups * rows, HD), bf16),
            pltpu.VMEM((groups * rows // heads, every), f32),
            pltpu.VMEM((groups * rows, HD), f32),
            pltpu.VMEM((groups * rows, HD), f32),
        ],
        [],
        PCOVER,
        0,
    )(*pairs, memory_sections.reshape(1, every))

    out_rows, out_cols = groups * tokens, out_weight.shape[1]
    share = out_rows // shares
    pieces = call(
        functools.partial(attend_kernel, groups, shares),
        [VMEM] * (groups + 5),
        [pltpu.VMEM((share, out_cols), f32 if k == 0 else bf16) for k in range(shares)],
        [
            pltpu.VMEM((out_rows, out_weight.shape[0]), f32),
            pltpu.VMEM((out_rows, out_cols), f32),
        ],
        2 * out_rows * out_weight.size,
        2 * out_weight.size,
    )(*kvs, *prepared, out_weight)
    order = [*range(shares - 2, 0, -1), shares - 1]
    arrived = [permute(pieces[bits], "tp", bits) for bits in order]
    return call(
        sum_kernel,
        [VMEM] * shares,
        jax.ShapeDtypeStruct((share, out_cols), bf16),
        [],
        shares * share * out_cols,
        2 * shares * share * out_cols,
    )(pieces[0], *arrived)


def solution(mesh):
    return jax.shard_map(
        body,
        mesh=mesh,
        in_specs=(
            P(("parts", "dp"), "tp"),
            P(None, None, "tp"),
            P(None, "tp"),
            P("parts"),
            P(("parts", "dp")),
            P(("parts", "dp"), "tp"),
            P(("parts", "dp"), "tp"),
            P(("parts", "dp"), "tp"),
            P(("parts", "dp"), None, "tp"),
            P(("parts", "dp"), None, "tp"),
            P(("parts", "dp")),
            P("tp", "dp"),
        ),
        out_specs=P(("parts", "tp"), "dp"),
        check_vma=False,
    )
```
